256 devices in a mesh: row: 32 (over x, z), col: 8 (over y, core).
Axes of the slice: x: 4, y: 4, z: 8, core: 2. Of those that a mesh axis runs over, the one named last changes fastest.
Arguments:
- weight: float32 [9, 7168, 2048], P(None, 'row', 'col'), may hold values from -6 to 6
- grad: bfloat16 [9, 7168, 2048], P(None, 'row', 'col'), may hold values from -162 to 162
- momentum: float32 [9, 7168, 2048], P(None, 'row', 'col'), may hold values from -6 to 6
- right: float32 [2048, 9, 64], P('col'), may hold values from -6 to 6
Outputs:
- new_weight: float32 [9, 7168, 2048], P(None, 'row', 'col')
- new_momentum: float32 [9, 7168, 2048], P(None, 'row', 'col')
- new_right: float32 [2048, 9, 64], P('col')
The draws below stay inside these ranges and needn't reach their ends.
All inputs are finite; a program needn't handle non-finite values.
Results may differ from the reference program's by a relative error of at most 0.0003.
Values sent between devices are 32-bit elements; how exact they have to be, the bound alone decides.
A program may use at most 64 MiB of HBM per device.

```python
import math
import jax
import jax.numpy as jnp
from jax import lax

D = 7168
FF = 2048
RANK = 64
MATS = 9


def draw_grad(key, part):
    key = jax.random.fold_in(key, 11)
    first, second, third = jax.random.split(key, 3)
    shape = (MATS, D, FF)
    row_ramp = jnp.exp(math.log(3.0) * jnp.arange(D, dtype=jnp.float32) / D)
    col_ramp = jnp.exp(math.log(3.0) * jnp.arange(FF, dtype=jnp.float32) / FF)
    row_scale = jnp.exp(jax.random.uniform(second, (MATS, D, 1), jnp.float32, 0.0, math.log(3.0))) * row_ramp[None, :, None]
    col_scale = jnp.exp(jax.random.uniform(third, (MATS, 1, FF), jnp.float32, 0.0, math.log(10.0))) * col_ramp[None, None, :]
    base = jnp.clip(jax.random.normal(first, shape, jnp.float32), -6.0, 6.0)
    factor_value = 0.1
    return (factor_value * base * row_scale * col_scale).astype(jnp.bfloat16)


def draw_right(key, part):
    key = jax.random.fold_in(key, 23)
    first, second, third = jax.random.split(key, 3)
    segment = FF // 8
    shared = jnp.clip(jax.random.normal(first, (FF, MATS, 1), jnp.float32), -2.4, 2.4)
    directions = jnp.clip(jax.random.normal(third, (8, MATS, RANK), jnp.float32), -2.4, 2.4)
    spread = jnp.clip(jax.random.normal(second, (FF, MATS, RANK), jnp.float32), -5.0, 5.0)
    expanded = jnp.repeat(directions, segment, axis=0)
    return shared * expanded + 0.006 * spread


def level_of(key, shape, pieces, least, largest):
    def one(dim, shards_of):
        heights = jax.random.uniform(jax.random.fold_in(jax.random.fold_in(key, 6), dim), (shards_of,), jnp.float32, least / len(pieces), largest / len(pieces))
        return jnp.repeat(jnp.exp(heights), shape[dim] // shards_of).reshape((-1,) + (1,) * (len(shape) - dim - 1))

    level = one(*pieces[0])
    for cut in pieces[1:]:
        level = level * one(*cut)
    return level


def normal_values(stream_key, extent, scale, limit, pieces=(), held_as=jnp.bfloat16):
    level = level_of(stream_key, extent, pieces, -0.22, 0.18) if pieces else 1.0
    values = jax.random.normal(stream_key, extent, jnp.float32) * scale * level
    return jnp.minimum(jnp.maximum(values, -limit), limit).astype(held_as)


def setup_inputs(seed: int = 0) -> dict:
    seeds = jax.random.split(jax.random.key(seed), 5)
    return {
        "weight": normal_values(seeds[0], (MATS, D, FF), 1.0, 6.0, ((1, 32), (2, 8)), jnp.float32),
        "grad": draw_grad(jax.random.fold_in(seeds[4], 71), 0),
        "momentum": normal_values(seeds[2], (MATS, D, FF), 1.0, 6.0, ((1, 32), (2, 8)), jnp.float32),
        "right": draw_right(jax.random.fold_in(seeds[4], 71), 0),
    }


epsilon = 1e-06
momentum_decay = 0.95

def one_matrix(operands):
    weight, grad, momentum, right = operands
    highest = lax.Precision.HIGHEST
    stacked = momentum + grad.astype(jnp.float32)
    power = jnp.dot(stacked.astype(jnp.float32), right.astype(jnp.float32), preferred_element_type=jnp.float32, precision=highest)
    factor, upper = jnp.linalg.qr(power)
    signs = jnp.sign(jnp.diagonal(upper))
    factor = factor * signs[None, :]
    product = jnp.dot(stacked.T.astype(jnp.float32), factor.astype(jnp.float32), preferred_element_type=jnp.float32, precision=highest)
    scale_cols = jnp.sqrt(lax.optimization_barrier(jnp.mean(product * product, axis=0)) + epsilon)
    new_right = product / scale_cols[None, :]
    feedback = jnp.dot(factor.astype(jnp.float32), product.T.astype(jnp.float32), preferred_element_type=jnp.float32, precision=highest)
    new_momentum = stacked - (1.0 - momentum_decay) * feedback
    update = jnp.dot(factor.astype(jnp.float32), new_right.T.astype(jnp.float32), preferred_element_type=jnp.float32, precision=highest)
    new_weight = weight - jnp.sqrt(D / FF) * update
    return (new_weight, new_momentum, new_right)

def reference(weight, grad, momentum, right):
    outputs = lax.map(one_matrix, (weight, grad, momentum, jnp.transpose(right, (1, 0, 2))))
    return (outputs[0], outputs[1], jnp.transpose(outputs[2], (1, 0, 2)))
```

```python
import functools
import math

import jax
import jax.numpy as jnp
from jax import lax
from jax.experimental import pallas as pl
from jax.experimental.pallas import tpu as pltpu
from jax.sharding import PartitionSpec as P

MESH = pl.DeviceIdType.MESH
HIGHEST = lax.Precision.HIGHEST
F32 = jnp.float32
BF16 = jnp.bfloat16

EPSILON = 1e-06
DECAY = 0.95
RANK = 64


def two_sum(a, b):
    s = a + b
    back = s - a
    return s, (a - (s - back)) + (b - back)


def split(a):
    t = a * 4097.0
    high = t - (t - a)
    return high, a - high


def two_prod(a, b):
    p = a * b
    ah, al = split(a)
    bh, bl = split(b)
    return p, ((ah * bh - p) + ah * bl + al * bh) + al * bl


def add_pair(ah, al, bh, bl):
    s, t = two_sum(ah, bh)
    t = t + (al + bl)
    h = s + t
    return h, t - (h - s)


def nt(a, b, precision=None):
    return lax.dot_general(a, b, (((1,), (1,)), ((), ())), precision=precision, preferred_element_type=F32)


def nn(a, b, precision=None):
    return lax.dot_general(a, b, (((1,), (0,)), ((), ())), precision=precision, preferred_element_type=F32)


def tn(a, b, precision=None):
    return lax.dot_general(a, b, (((0,), (0,)), ((), ())), precision=precision, preferred_element_type=F32)


def round_int(v):
    magic = 1.5 * 2.0**23
    return (v + magic) - magic


def exact_gram(x):
    top = jnp.maximum(jnp.max(jnp.abs(x), axis=1, keepdims=True), 1e-18)
    top = jnp.broadcast_to(top, (RANK, 128))
    power = jnp.floor(jnp.log(top) * (1.0 / math.log(2.0))) + 1.0
    unit = jnp.exp2(power - 7.0).astype(BF16).astype(F32)
    inverse = jnp.exp2(7.0 - power).astype(BF16).astype(F32)
    y = x * inverse[:, 0:1]
    slices = []
    for i in range(4):
        q = round_int(y)
        slices.append(q.astype(BF16))
        y = (y - q) * 256.0
    q = jnp.concatenate(slices, axis=0)
    e = nt(q, q)
    low = [e[RANK * a : RANK * (a + 1), 0:128] for a in range(4)]
    high = [e[RANK * a : RANK * (a + 1), 128:256] for a in range(4)]
    levels = [low[0], low[1], low[2] + high[0], low[3] + high[1], high[2], high[3]]
    s, t = levels[0], jnp.zeros_like(levels[0])
    for i in range(1, 6):
        s, err = two_sum(s, levels[i] * (2.0 ** (-8 * i)))
        t = t + err
    s2 = pltpu.roll(s, 64, 1) * (1.0 / 256.0)
    t2 = pltpu.roll(t, 64, 1) * (1.0 / 256.0)
    gh, gl = add_pair(s, t, s2, t2)
    rows = lax.broadcasted_iota(jnp.int32, (RANK, 128), 0)
    lanes = lax.broadcasted_iota(jnp.int32, (RANK, 128), 1)
    across = jnp.sum(jnp.where(rows == lanes, unit, 0.0), axis=0, keepdims=True)
    return gh * unit * across, gl * unit * across


def factor_block(mh, ml, first, count, begin, end):
    rows = lax.broadcasted_iota(jnp.int32, (count, 128), 0) + first
    lanes = lax.broadcasted_iota(jnp.int32, (count, 128), 1)
    half = jnp.where(lanes >= 64, 64, 0)
    column = lanes - half

    def step(k, carry):
        ah, al = mh[first:, :], ml[first:, :]
        rh, rl = mh[pl.ds(k, 1), :], ml[pl.ds(k, 1), :]
        index = half + k
        ch = jnp.take_along_axis(ah, index, axis=1)
        cl = jnp.take_along_axis(al, index, axis=1)
        dh = jnp.take_along_axis(jnp.broadcast_to(rh, (8, 128)), index[0:8], axis=1)[0:1]
        dl = jnp.take_along_axis(jnp.broadcast_to(rl, (8, 128)), index[0:8], axis=1)[0:1]
        inv = 1.0 / dh
        p, e = two_prod(dh, inv)
        inv_low = inv * (((1.0 - p) - e) - dl * inv)
        p, e = two_prod(ch, inv)
        t = e + (ch * inv_low + cl * inv)
        nh = p + t
        nl = t - (nh - p)
        later = rows > k
        nh = jnp.where(later, nh, 0.0)
        nl = jnp.where(later, nl, 0.0)
        here = column == k
        rh = jnp.where(here[0:1], 1.0, rh)
        rl = jnp.where(here[0:1], 0.0, rl)
        clear = here & later
        ah = jnp.where(clear, 0.0, ah)
        al = jnp.where(clear, 0.0, al)
        p, e = two_prod(nh, rh)
        q = e + (nh * rl + nl * rh)
        s, t = two_sum(ah, -p)
        t = t + (al - q)
        h = s + t
        mh[first:, :] = h
        ml[first:, :] = t - (h - s)
        return carry

    lax.fori_loop(begin, end, step, 0)


def factor_pair(mh, ml, begin, end):
    for first in range(begin, end, 8):
        factor_block(mh, ml, first, RANK - first, first, first + 8)


def inverse_of(mh):
    m = mh[...]
    rows = lax.broadcasted_iota(jnp.int32, (RANK, 128), 0)
    lanes = lax.broadcasted_iota(jnp.int32, (RANK, 128), 1)
    left = lanes < 64
    column = jnp.where(left, lanes, lanes - 64)
    diagonal = jnp.where(column == rows, m, 0.0)
    da = jnp.sum(jnp.where(left, diagonal, 0.0), axis=1, keepdims=True)
    db = jnp.sum(jnp.where(left, 0.0, diagonal), axis=1, keepdims=True)
    root = 1.0 / jnp.sqrt(jnp.where(left, da, db))
    return jnp.where(column < rows, m * root, jnp.where(column == rows, root, 0.0))


def exchange_kernel(nx, nz, ny, grad, mom, right, qt_out, prod_out, scale_out, s_v, g_v, r_v, part, mate, ysend, yrecv,
                    pt, gx, gz, mh, ml, linv, tp, trecv, tfull, sq, load_sem, mate_send, mate_recv, y_send, y_recv,
                    ag_send, ag_recv, fw_send, fw_recv, h_send, h_recv, gx_send, gx_recv, gz_send, gz_recv, t_send,
                    t_recv, ta_send, ta_recv, l_send, l_recv, sq_send, sq_recv):
    nr, nc = nx * nz, ny * 2
    mats = nc + 1
    last = mats - 1
    ff = 256 * nc
    row, col = lax.axis_index("row"), lax.axis_index("col")
    x, z = row // nz, row % nz
    y, k = col // 2, col % 2
    mate_id = (row, y * 2 + (1 - k))
    half = RANK // 2

    def remote(src, dst, send, recv, target):
        return pltpu.make_async_remote_copy(src_ref=src, dst_ref=dst, send_sem=send, recv_sem=recv, device_id=target,
                                            device_id_type=MESH)

    load_right = pltpu.make_async_copy(right, r_v, load_sem.at[2 * mats])
    load_right.start()

    def loads(m):
        return (pltpu.make_async_copy(mom.at[m], s_v.at[m], load_sem.at[m]),
                pltpu.make_async_copy(grad.at[m], g_v.at[m], load_sem.at[mats + m]))

    order = [2 * i + (1 - k) for i in range(ny)] + [last] + [2 * i + k for i in range(ny)]
    for m in order:
        for c in loads(m):
            c.start()

    barrier = pltpu.get_barrier_semaphore()

    def greet(i, c):
        pl.semaphore_signal(barrier, inc=1, device_id=(lax.rem(row + i, nr), col), device_id_type=MESH)
        return c

    def greet_col(i, c):
        pl.semaphore_signal(barrier, inc=1, device_id=(row, lax.rem(col + i, nc)), device_id_type=MESH)
        return c

    lax.fori_loop(1, nr, greet, 0)
    lax.fori_loop(1, nc, greet_col, 0)
    load_right.wait()

    def power(m):
        for c in loads(m):
            c.wait()
        s = s_v[m] + g_v[m].astype(F32)
        s_v[m] = s
        part[m] = nt(r_v[m], s, HIGHEST)

    to_mate = []
    for i in range(ny):
        m = 2 * i + (1 - k)
        power(m)
        if i == 0:
            pl.semaphore_wait(barrier, nr + nc - 2)
        c = remote(part.at[m], mate.at[i], mate_send.at[i], mate_recv.at[i], mate_id)
        c.start()
        to_mate.append(c)
    power(last)
    other_rows = pl.ds(pl.multiple_of((1 - k) * half, half), half)
    my_rows = pl.ds(pl.multiple_of(k * half, half), half)
    c = remote(part.at[last, other_rows], mate.at[ny, pl.ds(0, half)], mate_send.at[ny], mate_recv.at[ny], mate_id)
    c.start()
    to_mate.append(c)
    for i in range(ny):
        power(2 * i + k)

    to_mate[ny].wait_recv()
    shared = part[last, my_rows, :] + mate[ny, 0:half, :]
    for i in range(ny):
        to_mate[i].wait_recv()
    to_y = []
    for i in range(1, ny):
        yd = lax.rem(y + i, ny)
        ysend[yd, 0:RANK, :] = part[2 * yd + k] + mate[yd]
        ysend[yd, RANK:, :] = shared
        c = remote(ysend.at[yd], yrecv.at[y], y_send.at[i], y_recv.at[i], (row, 2 * yd + k))
        c.start()
        to_y.append(c)
    own = 2 * y + k
    yrecv[y, 0:RANK, :] = part[own] + mate[y]
    yrecv[y, RANK:, :] = shared
    for c in to_y:
        c.wait_recv()
    total = yrecv[0]
    for i in range(1, ny):
        total = total + yrecv[i]
    pt[own] = total[0:RANK]
    pt[last, my_rows, :] = total[RANK:]
    swap = remote(pt.at[last, my_rows], pt.at[last, my_rows], h_send, h_recv, mate_id)
    swap.start()
    gather = []
    for i in range(1, ny):
        yd = lax.rem(y + i, ny)
        c = remote(pt.at[own], pt.at[own], ag_send.at[i], ag_recv.at[i], (row, 2 * yd + k))
        c.start()
        gather.append(c)
    forward = [remote(pt.at[own], pt.at[own], fw_send.at[0], fw_recv.at[0], mate_id)]
    forward[0].start()
    swap.wait_recv()

    ah, al = exact_gram(pt[own])
    bh, bl = exact_gram(pt[last])
    lanes = lax.broadcasted_iota(jnp.int32, (RANK, 128), 1)
    gx[x, 0] = jnp.where(lanes < 64, ah, pltpu.roll(bh, 64, 1))
    gx[x, 1] = jnp.where(lanes < 64, al, pltpu.roll(bl, 64, 1))
    to_x = []
    for i in range(1, nx):
        xd = lax.rem(x + i, nx)
        c = remote(gx.at[x], gx.at[x], gx_send.at[i], gx_recv.at[i], (xd * nz + z, col))
        c.start()
        to_x.append(c)

    for i in range(1, ny):
        gather[i - 1].wait_recv()
        m = 2 * lax.rem(y - i + ny, ny) + k
        c = remote(pt.at[m], pt.at[m], fw_send.at[i], fw_recv.at[i], mate_id)
        c.start()
        forward.append(c)
    for c in forward:
        c.wait_recv()

    rows_t = tp.shape[1]

    def times(m, c):
        t = nn(pt[m], s_v[m], HIGHEST)
        at = pl.ds(pl.multiple_of(m * RANK, RANK), RANK)
        tp[0, at, :] = t[:, 0:128]
        tp[1, at, :] = t[:, 128:256]
        return c

    lax.fori_loop(0, mats, times, 0)
    if rows_t > mats * RANK:
        tp[:, mats * RANK :, :] = jnp.zeros((2, rows_t - mats * RANK, 128), F32)

    for c in to_x:
        c.wait_recv()
    gh, gl = gx[0, 0], gx[0, 1]
    for i in range(1, nx):
        gh, gl = add_pair(gh, gl, gx[i, 0], gx[i, 1])
    gz[z, 0] = gh
    gz[z, 1] = gl
    to_z = []
    for i in range(1, nz):
        zd = lax.rem(z + i, nz)
        c = remote(gz.at[z], gz.at[z], gz_send.at[i], gz_recv.at[i], (x * nz + zd, col))
        c.start()
        to_z.append(c)

    piece = 2 * rows_t // nr
    per_half = nr // 2

    def piece_of(ref, d):
        return ref.at[d // per_half, pl.ds(pl.multiple_of((d % per_half) * piece, piece), piece)]

    def t_copy(i):
        d = lax.rem(row + i, nr)
        return remote(piece_of(tp, d), trecv.at[row], t_send.at[i], t_recv.at[i], (d, col))

    def ta_copy(i):
        d = lax.rem(row + i, nr)
        return remote(piece_of(tfull, row), piece_of(tfull, row), ta_send.at[i], ta_recv.at[i], (d, col))

    def start(copy):
        def go(i, c):
            copy(i).start()
            return c
        return go

    def wait_recv(copy):
        def go(i, c):
            copy(i).wait_recv()
            return c
        return go

    def wait_send(copy):
        def go(i, c):
            copy(i).wait_send()
            return c
        return go

    lax.fori_loop(1, nr, start(t_copy), 0)
    my_at = pl.ds(pl.multiple_of((row % per_half) * piece, piece), piece)
    trecv[row] = tp[row // per_half, my_at, :]

    for c in to_z:
        c.wait_recv()
    gh, gl = gz[0, 0], gz[0, 1]
    for i in range(1, nz):
        gh, gl = add_pair(gh, gl, gz[i, 0], gz[i, 1])
    mh[...] = gh
    ml[...] = gl
    factor_pair(mh, ml, 0, 32)

    lax.fori_loop(1, nr, wait_recv(t_copy), 0)
    tfull[row // per_half, my_at, :] = lax.fori_loop(1, nr, lambda i, acc: acc + trecv[i], trecv[0])
    lax.fori_loop(1, nr, start(ta_copy), 0)

    factor_pair(mh, ml, 32, RANK)
    linv[own] = inverse_of(mh)
    spread = []
    for i in range(1, nc):
        cd = lax.rem(col + i, nc)
        c = remote(linv.at[own], linv.at[own], l_send.at[i], l_recv.at[i], (row, cd))
        c.start()
        spread.append(c)
    last_inverse = pltpu.roll(linv[own], 64, 1)
    for c in spread:
        c.wait_recv()
    linv[last] = last_inverse

    def orthonormal(m, c):
        qt_out[m] = nn(linv[m][:, 0:RANK], pt[m], HIGHEST)
        return c

    lax.fori_loop(0, mats, orthonormal, 0)
    lax.fori_loop(1, nr, wait_recv(ta_copy), 0)

    def apply(m, acc):
        at = pl.ds(pl.multiple_of(m * RANK, RANK), RANK)
        t = jnp.concatenate([tfull[0, at, :], tfull[1, at, :]], axis=1)
        p = nn(linv[m][:, 0:RANK], t, HIGHEST)
        prod_out[m] = p
        ones = jnp.where(lax.broadcasted_iota(jnp.int32, (16, 256), 0) == m, 1.0, 0.0)
        return acc + nt(ones, p * p, HIGHEST)

    squares = lax.fori_loop(0, mats, apply, jnp.zeros((16, RANK), F32))
    sq[col] = jnp.concatenate([squares, jnp.zeros((16, 128 - RANK), F32)], axis=1)
    to_all = []
    for i in range(1, nc):
        cd = lax.rem(col + i, nc)
        c = remote(sq.at[col], sq.at[col], sq_send.at[i], sq_recv.at[i], (row, cd))
        c.start()
        to_all.append(c)
    for c in to_all:
        c.wait_recv()
    squares = sq[0]
    for i in range(1, nc):
        squares = squares + sq[i]
    scale = 1.0 / jnp.sqrt(squares * (1.0 / ff) + EPSILON)
    scale_out[...] = jnp.transpose(scale)

    for c in to_mate + to_y + gather + forward + [swap] + to_x + to_z + spread + to_all:
        c.wait_send()
    lax.fori_loop(1, nr, wait_send(t_copy), 0)
    lax.fori_loop(1, nr, wait_send(ta_copy), 0)


def update_kernel(gain, weight, grad, mom, qt, prod, scale, new_weight, new_mom, new_right):
    m = pl.program_id(0)
    table = scale[...]
    lanes = lax.broadcasted_iota(jnp.int32, table.shape, 1)
    column = jnp.sum(jnp.where(lanes == m, table, 0.0), axis=1, keepdims=True)[0:RANK]
    q, p = qt[0], prod[0]
    normed = p * column
    new_right[0] = normed
    stacked = mom[0] + grad[0].astype(F32)
    new_mom[0] = stacked - tn(q * (1.0 - DECAY), p, HIGHEST)
    new_weight[0] = weight[0] - tn(q * gain, normed, HIGHEST)


def body(nx, nz, ny, depth, weight, grad, momentum, right):
    nr, nc = nx * nz, ny * 2
    mats, rows, cols = weight.shape
    ff = cols * nc
    rt = jnp.transpose(right, (1, 2, 0))
    piece = -(-2 * mats * RANK // nr)
    piece = -(-piece // 8) * 8
    rows_t = piece * nr // 2
    vmem = pl.BlockSpec(memory_space=pltpu.VMEM)
    hbm = pl.BlockSpec(memory_space=pl.ANY)
    dma = pltpu.SemaphoreType.DMA
    half = RANK // 2
    qt, prod, scale = pl.pallas_call(
        functools.partial(exchange_kernel, nx, nz, ny),
        out_shape=(
            jax.ShapeDtypeStruct((mats, RANK, rows), F32),
            jax.ShapeDtypeStruct((mats, RANK, cols), F32),
            jax.ShapeDtypeStruct((128, 16), F32),
        ),
        in_specs=[hbm, hbm, hbm],
        out_specs=(vmem, vmem, vmem),
        scratch_shapes=[
            pltpu.VMEM((mats, rows, cols), F32),
            pltpu.VMEM((mats, rows, cols), BF16),
            pltpu.VMEM((mats, RANK, cols), F32),
            pltpu.VMEM((mats, RANK, rows), F32),
            pltpu.VMEM((ny + 1, RANK, rows), F32),
            pltpu.VMEM((ny, RANK + half, rows), F32),
            pltpu.VMEM((ny, RANK + half, rows), F32),
            pltpu.VMEM((mats, RANK, rows), F32),
            pltpu.VMEM((nx, 2, RANK, 128), F32),
            pltpu.VMEM((nz, 2, RANK, 128), F32),
            pltpu.VMEM((RANK, 128), F32),
            pltpu.VMEM((RANK, 128), F32),
            pltpu.VMEM((mats, RANK, 128), F32),
            pltpu.VMEM((2, rows_t, 128), F32),
            pltpu.VMEM((nr, piece, 128), F32),
            pltpu.VMEM((2, rows_t, 128), F32),
            pltpu.VMEM((nc, 16, 128), F32),
            dma((2 * mats + 1,)),
            dma((ny + 1,)), dma((ny + 1,)),
            dma((ny,)), dma((ny,)),
            dma((ny,)), dma((ny,)),
            dma((ny,)), dma((ny,)),
            dma, dma,
            dma((nx,)), dma((nx,)),
            dma((nz,)), dma((nz,)),
            dma((nr,)), dma((nr,)),
            dma((nr,)), dma((nr,)),
            dma((nc,)), dma((nc,)),
            dma((nc,)), dma((nc,)),
        ],
        compiler_params=pltpu.CompilerParams(
            collective_id=0, has_side_effects=True, vmem_limit_bytes=40 * 1024 * 1024
        ),
        name="exchange",
    )(grad, momentum, rt)

    def block(*shape):
        return pl.BlockSpec((1,) + shape, lambda m: (m, 0, 0))

    big = block(rows, cols)
    gain = math.sqrt(depth / ff)
    new_weight, new_momentum, new_right = pl.pallas_call(
        functools.partial(update_kernel, gain),
        grid=(mats,),
        out_shape=(
            jax.ShapeDtypeStruct(weight.shape, F32),
            jax.ShapeDtypeStruct(weight.shape, F32),
            jax.ShapeDtypeStruct((mats, RANK, cols), F32),
        ),
        in_specs=[big, big, big, block(RANK, rows), block(RANK, cols), pl.BlockSpec((128, 16), lambda m: (0, 0))],
        out_specs=(big, big, block(RANK, cols)),
        name="update",
    )(weight, grad, momentum, qt, prod, scale)
    return new_weight, new_momentum, jnp.transpose(new_right, (2, 0, 1))


def solution(mesh):
    nr, nc = mesh.shape["row"], mesh.shape["col"]
    nz = min(nr, 8)
    nx = nr // nz

    def run(weight, grad, momentum, right):
        return body(nx, nz, nc // 2, weight.shape[1] * nr, weight, grad, momentum, right)

    placed = P(None, "row", "col")
    return jax.shard_map(
        run,
        mesh=mesh,
        in_specs=(placed, placed, placed, P("col", None, None)),
        out_specs=(placed, placed, P("col", None, None)),
        check_vma=False,
    )
```

```python
import functools
import math

import jax
import jax.numpy as jnp
from jax import lax
from jax.experimental import pallas as pl
from jax.experimental.pallas import tpu as pltpu
from jax.sharding import PartitionSpec as P

MESH = pl.DeviceIdType.MESH
HIGHEST = lax.Precision.HIGHEST
F32 = jnp.float32
BF16 = jnp.bfloat16

EPSILON = 1e-06
DECAY = 0.95
RANK = 64


def two_sum(a, b):
    s = a + b
    back = s - a
    return s, (a - (s - back)) + (b - back)


def split(a):
    t = a * 4097.0
    high = t - (t - a)
    return high, a - high


def two_prod(a, b):
    p = a * b
    ah, al = split(a)
    bh, bl = split(b)
    return p, ((ah * bh - p) + ah * bl + al * bh) + al * bl


def add_pair(ah, al, bh, bl):
    s, t = two_sum(ah, bh)
    t = t + (al + bl)
    h = s + t
    return h, t - (h - s)


def nt(a, b, precision=None):
    return lax.dot_general(a, b, (((1,), (1,)), ((), ())), precision=precision, preferred_element_type=F32)


def nn(a, b, precision=None):
    return lax.dot_general(a, b, (((1,), (0,)), ((), ())), precision=precision, preferred_element_type=F32)


def tn(a, b, precision=None):
    return lax.dot_general(a, b, (((0,), (0,)), ((), ())), precision=precision, preferred_element_type=F32)


def cut(a):
    a1 = a.astype(BF16)
    rest = a - a1.astype(F32)
    a2 = rest.astype(BF16)
    return a1, a2, (rest - a2.astype(F32)).astype(BF16)


def cut_product(dot, a, b):
    a1, a2, a3 = cut(a)
    b1, b2, b3 = cut(b)
    p = dot(jnp.concatenate([a1, a2, a3], axis=0), b1)
    q = dot(jnp.concatenate([a1, a2], axis=0), b2)
    r = dot(a1, b3)
    return p[0:RANK] + ((p[RANK : 2 * RANK] + q[0:RANK]) + (p[2 * RANK :] + q[RANK:] + r))


def round_int(v):
    magic = 1.5 * 2.0**23
    return (v + magic) - magic


def exact_gram(x):
    top = jnp.maximum(jnp.max(jnp.abs(x), axis=1, keepdims=True), 1e-18)
    top = jnp.broadcast_to(top, (RANK, 128))
    power = jnp.floor(jnp.log(top) * (1.0 / math.log(2.0))) + 1.0
    unit = jnp.exp2(power - 7.0).astype(BF16).astype(F32)
    inverse = jnp.exp2(7.0 - power).astype(BF16).astype(F32)
    y = x * inverse[:, 0:1]
    slices = []
    for i in range(4):
        q = round_int(y)
        slices.append(q.astype(BF16))
        y = (y - q) * 256.0
    q = jnp.concatenate(slices, axis=0)
    e = nt(q, q)
    low = [e[RANK * a : RANK * (a + 1), 0:128] for a in range(4)]
    high = [e[RANK * a : RANK * (a + 1), 128:256] for a in range(4)]
    levels = [low[0], low[1], low[2] + high[0], low[3] + high[1], high[2], high[3]]
    s, t = levels[0], jnp.zeros_like(levels[0])
    for i in range(1, 6):
        s, err = two_sum(s, levels[i] * (2.0 ** (-8 * i)))
        t = t + err
    s2 = pltpu.roll(s, 64, 1) * (1.0 / 256.0)
    t2 = pltpu.roll(t, 64, 1) * (1.0 / 256.0)
    gh, gl = add_pair(s, t, s2, t2)
    rows = lax.broadcasted_iota(jnp.int32, (RANK, 128), 0)
    lanes = lax.broadcasted_iota(jnp.int32, (RANK, 128), 1)
    across = jnp.sum(jnp.where(rows == lanes, unit, 0.0), axis=0, keepdims=True)
    return gh * unit * across, gl * unit * across


def factor_block(mh, ml, first, count, begin, end):
    rows = lax.broadcasted_iota(jnp.int32, (count, 128), 0) + first
    lanes = lax.broadcasted_iota(jnp.int32, (count, 128), 1)
    half = jnp.where(lanes >= 64, 64, 0)
    column = lanes - half

    def step(k, carry):
        ah, al = mh[first:, :], ml[first:, :]
        rh, rl = mh[pl.ds(k, 1), :], ml[pl.ds(k, 1), :]
        index = half + k
        ch = jnp.take_along_axis(ah, index, axis=1)
        cl = jnp.take_along_axis(al, index, axis=1)
        dh = jnp.take_along_axis(jnp.broadcast_to(rh, (8, 128)), index[0:8], axis=1)[0:1]
        dl = jnp.take_along_axis(jnp.broadcast_to(rl, (8, 128)), index[0:8], axis=1)[0:1]
        inv = 1.0 / dh
        p, e = two_prod(dh, inv)
        inv_low = inv * (((1.0 - p) - e) - dl * inv)
        p, e = two_prod(ch, inv)
        t = e + (ch * inv_low + cl * inv)
        nh = p + t
        nl = t - (nh - p)
        later = rows > k
        nh = jnp.where(later, nh, 0.0)
        nl = jnp.where(later, nl, 0.0)
        here = column == k
        rh = jnp.where(here[0:1], 1.0, rh)
        rl = jnp.where(here[0:1], 0.0, rl)
        clear = here & later
        ah = jnp.where(clear, 0.0, ah)
        al = jnp.where(clear, 0.0, al)
        p, e = two_prod(nh, rh)
        q = e + (nh * rl + nl * rh)
        s, t = two_sum(ah, -p)
        t = t + (al - q)
        h = s + t
        mh[first:, :] = h
        ml[first:, :] = t - (h - s)
        return carry

    lax.fori_loop(begin, end, step, 0)


def factor_pair(mh, ml, begin, end):
    for first in range(begin, end, 8):
        factor_block(mh, ml, first, RANK - first, first, first + 8)


def inverse_of(mh):
    m = mh[...]
    rows = lax.broadcasted_iota(jnp.int32, (RANK, 128), 0)
    lanes = lax.broadcasted_iota(jnp.int32, (RANK, 128), 1)
    left = lanes < 64
    column = jnp.where(left, lanes, lanes - 64)
    diagonal = jnp.where(column == rows, m, 0.0)
    da = jnp.sum(jnp.where(left, diagonal, 0.0), axis=1, keepdims=True)
    db = jnp.sum(jnp.where(left, 0.0, diagonal), axis=1, keepdims=True)
    root = 1.0 / jnp.sqrt(jnp.where(left, da, db))
    return jnp.where(column < rows, m * root, jnp.where(column == rows, root, 0.0))


def exchange_kernel(nx, nz, ny, weight, grad, mom, right, w_out, m_out, q_out, prod_out, scale_out, s_v, g_v, r_v, part,
                    mate, ysend, yrecv, pt, pw, gp, gx, gz, ga, mh, ml, linv, tp, xrecv, zsend, zrecv, tfull, sq, load_sem,
                    w_sem, mate_send, mate_recv, y_send, y_recv, ag_send, ag_recv, fw_send, fw_recv, h_send, h_recv,
                    gx_send, gx_recv, gz_send, gz_recv, ga_send, ga_recv, tx_send, tx_recv, tz_send, tz_recv, az_send,
                    az_recv, ax_send, ax_recv, l_send, l_recv, sq_send, sq_recv):
    nr, nc = nx * nz, ny * 2
    mats = nc + 1
    last = mats - 1
    ff = 256 * nc
    row, col = lax.axis_index("row"), lax.axis_index("col")
    x, z = row // nz, row % nz
    y, k = col // 2, col % 2
    mate_id = (row, y * 2 + (1 - k))
    half = RANK // 2

    pending = []

    def finish():
        for c in pending:
            c.wait_send()

    def send(src, dst, sems, index, target):
        c = pltpu.make_async_remote_copy(src_ref=src, dst_ref=dst, send_sem=sems[0].at[index], recv_sem=sems[1].at[index],
                                         device_id=target, device_id_type=MESH)
        c.start()
        pending.append(c)
        return c

    def x_peer(i):
        return lax.rem(x + i, nx)

    def z_peer(i):
        return lax.rem(z + i, nz)

    def y_peer(i):
        return lax.rem(y + i, ny)

    far_first = sorted(range(1, nz), key=lambda i: -min(i, nz - i))

    load_right = pltpu.make_async_copy(right, r_v, load_sem.at[2 * mats])
    load_right.start()

    def loads(m):
        return (pltpu.make_async_copy(mom.at[m], s_v.at[m], load_sem.at[m]),
                pltpu.make_async_copy(grad.at[m], g_v.at[m], load_sem.at[mats + m]))

    turns = list(range(1, ny)) + [0]
    for m in [2 * y_peer(i) + (1 - k) for i in turns] + [last] + [2 * y_peer(i) + k for i in turns]:
        for c in loads(m):
            c.start()

    barrier = pltpu.get_barrier_semaphore()
    peers = [(row, lax.rem(col + i, nc)) for i in range(1, nc)]
    peers += [(x * nz + z_peer(i), col) for i in far_first]
    peers += [(x_peer(i) * nz + z, col) for i in range(1, nx)]
    for peer in peers:
        pl.semaphore_signal(barrier, inc=1, device_id=peer, device_id_type=MESH)
    load_right.wait()

    def power(m):
        for c in loads(m):
            c.wait()
        s = s_v[m] + g_v[m].astype(F32)
        s_v[m] = s
        part[m] = cut_product(nt, r_v[m], s)

    to_mate = {}
    mate_sems = (mate_send, mate_recv)
    for n, i in enumerate(turns):
        m = 2 * y_peer(i) + (1 - k)
        power(m)
        if n == 0:
            pl.semaphore_wait(barrier, len(peers))
        to_mate[i] = send(part.at[m], mate.at[i], mate_sems, i, mate_id)
    power(last)
    other_rows = pl.ds(pl.multiple_of((1 - k) * half, half), half)
    my_rows = pl.ds(pl.multiple_of(k * half, half), half)
    to_mate[ny] = send(part.at[last, other_rows], mate.at[ny, pl.ds(0, half)], mate_sems, ny, mate_id)
    load_weight = pltpu.make_async_copy(weight, w_out, w_sem)
    load_weight.start()

    own = 2 * y + k
    to_y = []
    for n, i in enumerate(turns):
        yd = y_peer(i)
        power(2 * yd + k)
        if n == 0:
            to_mate[ny].wait_recv()
            shared = part[last, my_rows, :] + mate[ny, 0:half, :]
        to_mate[i].wait_recv()
        if i == 0:
            yrecv[y, 0:RANK, :] = part[own] + mate[0]
            yrecv[y, RANK:, :] = shared
        else:
            ysend[i, 0:RANK, :] = part[2 * yd + k] + mate[i]
            ysend[i, RANK:, :] = shared
            to_y.append(send(ysend.at[i], yrecv.at[y], (y_send, y_recv), i, (row, 2 * yd + k)))
    for c in to_y:
        c.wait_recv()
    total = yrecv[0]
    for i in range(1, ny):
        total = total + yrecv[i]
    pt[last, my_rows, :] = total[RANK:]
    swap = send(pt.at[last, my_rows], pt.at[last, my_rows], (h_send, h_recv), 0, mate_id)
    pt[own] = total[0:RANK]
    gather = [send(pt.at[own], pt.at[own], (ag_send, ag_recv), i, (row, 2 * y_peer(i) + k)) for i in range(1, ny)]
    forward = [send(pt.at[own], pt.at[own], (fw_send, fw_recv), 0, mate_id)]

    lanes = lax.broadcasted_iota(jnp.int32, (RANK, 128), 1)
    ah, al = exact_gram(total[0:RANK])
    swap.wait_recv()
    bh, bl = exact_gram(pt[last])
    gp[0] = jnp.where(lanes < 64, ah, pltpu.roll(bh, 64, 1))
    gp[1] = jnp.where(lanes < 64, al, pltpu.roll(bl, 64, 1))
    share = RANK // nx

    def rows_of(d):
        return pl.ds(pl.multiple_of(d * share, share), share)

    to_x = [send(gp.at[:, rows_of(x_peer(i))], gx.at[x], (gx_send, gx_recv), i, (x_peer(i) * nz + z, col))
            for i in range(1, nx)]
    gx[x] = gp[:, rows_of(x), :]

    for i in range(1, ny):
        gather[i - 1].wait_recv()
        m = 2 * y_peer(ny - i) + k
        forward.append(send(pt.at[m], pt.at[m], (fw_send, fw_recv), i, mate_id))

    def sum_pairs(ref, n):
        h, l = ref[0, 0], ref[0, 1]
        for i in range(1, n):
            h, l = add_pair(h, l, ref[i, 0], ref[i, 1])
        return h, l

    for c in to_x:
        c.wait_recv()
    h, l = sum_pairs(gx, nx)
    gz[z, 0] = h
    gz[z, 1] = l
    to_z = [send(gz.at[z], gz.at[z], (gz_send, gz_recv), i, (x * nz + z_peer(i), col)) for i in far_first]

    for c in forward:
        c.wait_recv()
    rows_t = tp.shape[1]
    for m in range(mats):
        t = cut_product(nn, pt[m], s_v[m])
        tp[0, m * RANK : (m + 1) * RANK, :] = t[:, 0:128]
        tp[1, m * RANK : (m + 1) * RANK, :] = t[:, 128:256]
    if rows_t > mats * RANK:
        tp[:, mats * RANK :, :] = jnp.zeros((2, rows_t - mats * RANK, 128), F32)

    piece = 2 * rows_t // nr
    per_half = nr // 2

    def piece_of(ref, d):
        return ref.at[d // per_half, pl.ds(pl.multiple_of((d % per_half) * piece, piece), piece)]

    hops = far_first + [0]
    t_x = {}
    for j in hops:
        zd = z_peer(j)
        for i in range(1, nx):
            xd = x_peer(i)
            t_x[i, j] = send(piece_of(tp, xd * nz + zd), xrecv.at[i, j], (tx_send, tx_recv), (i, j), (xd * nz + z, col))
    for m in range(mats):
        pw[m] = jnp.transpose(pt[m])

    for c in to_z:
        c.wait_recv()
    h, l = sum_pairs(gz, nz)
    ga[x, 0] = h
    ga[x, 1] = l
    to_a = [send(ga.at[x], ga.at[x], (ga_send, ga_recv), i, (x_peer(i) * nz + z, col)) for i in range(1, nx)]

    t_z = []
    for j in hops:
        zd = z_peer(j)
        acc = piece_of(tp, x * nz + zd)[...]
        for i in range(1, nx):
            t_x[i, j].wait_recv()
            acc = acc + xrecv[i, j]
        if j == 0:
            zrecv[0] = acc
        else:
            zsend[j] = acc
            t_z.append(send(zsend.at[j], zrecv.at[j], (tz_send, tz_recv), j, (x * nz + zd, col)))

    for c in to_a:
        c.wait_recv()
    for i in range(nx):
        mh[i * share : (i + 1) * share, :] = ga[i, 0]
        ml[i * share : (i + 1) * share, :] = ga[i, 1]
    factor_pair(mh, ml, 0, 32)

    for c in t_z:
        c.wait_recv()
    acc = zrecv[0]
    for j in range(1, nz):
        acc = acc + zrecv[j]
    mine = piece_of(tfull, row)
    mine[...] = acc
    a_z = {j: send(mine, mine, (az_send, az_recv), j, (x * nz + z_peer(j), col)) for j in far_first}
    a_x = []

    def pass_on(j):
        p = piece_of(tfull, x * nz + z_peer(nz - j))
        for i in range(1, nx):
            a_x.append(send(p, p, (ax_send, ax_recv), (i, j), (x_peer(i) * nz + z, col)))

    pass_on(0)
    factor_pair(mh, ml, 32, RANK)

    linv[own] = inverse_of(mh)
    spread = [send(linv.at[own], linv.at[own], (l_send, l_recv), i, (row, lax.rem(col + i, nc))) for i in range(1, nc)]
    for j in reversed(far_first):
        a_z[j].wait_recv()
        pass_on(j)
    linv[last] = pltpu.roll(linv[own], 64, 1)
    for c in spread:
        c.wait_recv()
    left = lax.broadcasted_iota(jnp.int32, (pw.shape[1], 3 * RANK), 1) < 2 * RANK
    for m in range(mats):
        li = linv[m][:, 0:RANK]
        q = nt(pw[m], jnp.concatenate([li, li, li], axis=0), HIGHEST)
        q1 = q.astype(BF16)
        q_out[m] = jnp.where(left, q1.astype(F32), q - q1.astype(F32)).astype(BF16)
    for c in a_x:
        c.wait_recv()

    squares = jnp.zeros((8, 128), F32)
    places = lax.broadcasted_iota(jnp.int32, (8, 256), 0)
    for pair in range(0, mats, 2):
        sqs = []
        for m in (pair, pair + 1):
            if m >= mats:
                sqs.append(jnp.zeros((RANK, 256), F32))
                continue
            at = slice(m * RANK, (m + 1) * RANK)
            t = jnp.concatenate([tfull[0, at, :], tfull[1, at, :]], axis=1)
            p = nn(linv[m][:, 0:RANK], t, HIGHEST)
            prod_out[m] = p
            sqs.append(p * p)
        ones = jnp.where(places == pair // 2, 1.0, 0.0)
        squares = squares + nt(ones, jnp.concatenate(sqs, axis=0), HIGHEST)
    sq[col] = squares
    to_all = [send(sq.at[col], sq.at[col], (sq_send, sq_recv), i, (row, lax.rem(col + i, nc))) for i in range(1, nc)]
    for m in range(mats):
        m_out[m] = s_v[m] - nn(q_out[m], stacked_pieces(prod_out[m] * (1.0 - DECAY)))
    for c in to_all:
        c.wait_recv()
    squares = sq[0]
    for i in range(1, nc):
        squares = squares + sq[i]
    scale_out[...] = jnp.transpose(1.0 / jnp.sqrt(squares * (1.0 / ff) + EPSILON))
    load_weight.wait()
    finish()


def stacked_pieces(p):
    p1 = p.astype(BF16)
    p2 = (p - p1.astype(F32)).astype(BF16)
    return jnp.concatenate([p1, p2, p1], axis=0)


def update_kernel(gain, w, mom, q, prod, scale, new_weight, new_mom, new_right, w_v, r_v, w_sem, m_sem, r_sem):
    mats = w.shape[0]
    move = pltpu.make_async_copy(mom, new_mom, m_sem)
    move.start()
    table = scale[...]
    moves = [move]
    for m in range(mats):
        column = table[(m % 2) * RANK : (m % 2 + 1) * RANK, m // 2 : m // 2 + 1]
        normed = prod[m] * column
        r_v[m] = normed
        c = pltpu.make_async_copy(r_v.at[m], new_right.at[m], r_sem.at[m])
        c.start()
        moves.append(c)
        w_v[m] = w[m] - nn(q[m], stacked_pieces(normed * gain))
        c = pltpu.make_async_copy(w_v.at[m], new_weight.at[m], w_sem.at[m])
        c.start()
        moves.append(c)
    for c in moves:
        c.wait()


def body(nx, nz, ny, depth, weight, grad, momentum, right):
    nr, nc = nx * nz, ny * 2
    mats, rows, cols = weight.shape
    ff = cols * nc
    rt = jnp.transpose(right, (1, 2, 0))
    piece = -(-2 * mats * RANK // nr)
    piece = -(-piece // 8) * 8
    rows_t = piece * nr // 2
    share = RANK // nx
    vmem = pl.BlockSpec(memory_space=pltpu.VMEM)
    hbm = pl.BlockSpec(memory_space=pltpu.HBM)
    dma = pltpu.SemaphoreType.DMA
    half = RANK // 2
    w, mom, q, prod, scale = pl.pallas_call(
        functools.partial(exchange_kernel, nx, nz, ny),
        out_shape=(
            jax.ShapeDtypeStruct((mats, rows, cols), F32),
            jax.ShapeDtypeStruct((mats, rows, cols), F32),
            jax.ShapeDtypeStruct((mats, rows, 3 * RANK), BF16),
            jax.ShapeDtypeStruct((mats, RANK, cols), F32),
            jax.ShapeDtypeStruct((128, 8), F32),
        ),
        in_specs=[hbm] * 4,
        out_specs=(vmem,) * 5,
        scratch_shapes=[
            pltpu.VMEM((mats, rows, cols), F32),
            pltpu.VMEM((mats, rows, cols), BF16),
            pltpu.VMEM((mats, RANK, cols), F32),
            pltpu.VMEM((mats, RANK, rows), F32),
            pltpu.VMEM((ny + 1, RANK, rows), F32),
            pltpu.VMEM((ny, RANK + half, rows), F32),
            pltpu.VMEM((ny, RANK + half, rows), F32),
            pltpu.VMEM((mats, RANK, rows), F32),
            pltpu.VMEM((mats, rows, RANK), F32),
            pltpu.VMEM((2, RANK, 128), F32),
            pltpu.VMEM((nx, 2, share, 128), F32),
            pltpu.VMEM((nz, 2, share, 128), F32),
            pltpu.VMEM((nx, 2, share, 128), F32),
            pltpu.VMEM((RANK, 128), F32),
            pltpu.VMEM((RANK, 128), F32),
            pltpu.VMEM((mats, RANK, 128), F32),
            pltpu.VMEM((2, rows_t, 128), F32),
            pltpu.VMEM((nx, nz, piece, 128), F32),
            pltpu.VMEM((nz, piece, 128), F32),
            pltpu.VMEM((nz, piece, 128), F32),
            pltpu.VMEM((2, rows_t, 128), F32),
            pltpu.VMEM((nc, 8, 128), F32),
            dma((2 * mats + 1,)),
            dma,
            dma((ny + 1,)), dma((ny + 1,)),
            dma((ny,)), dma((ny,)),
            dma((ny,)), dma((ny,)),
            dma((ny,)), dma((ny,)),
            dma((1,)), dma((1,)),
            dma((nx,)), dma((nx,)),
            dma((nz,)), dma((nz,)),
            dma((nx,)), dma((nx,)),
            dma((nx, nz)), dma((nx, nz)),
            dma((nz,)), dma((nz,)),
            dma((nz,)), dma((nz,)),
            dma((nx, nz)), dma((nx, nz)),
            dma((nc,)), dma((nc,)),
            dma((nc,)), dma((nc,)),
        ],
        compiler_params=pltpu.CompilerParams(
            collective_id=0, has_side_effects=True, vmem_limit_bytes=40 * 1024 * 1024
        ),
        name="exchange",
    )(*[pltpu.with_memory_space_constraint(v, pltpu.HBM) for v in (weight, grad, momentum, rt)])

    gain = math.sqrt(depth / ff)
    new_weight, new_momentum, new_right = pl.pallas_call(
        functools.partial(update_kernel, gain),
        out_shape=(
            jax.ShapeDtypeStruct(weight.shape, F32),
            jax.ShapeDtypeStruct(weight.shape, F32),
            jax.ShapeDtypeStruct((mats, RANK, cols), F32),
        ),
        in_specs=[vmem] * 5,
        out_specs=(hbm,) * 3,
        scratch_shapes=[
            pltpu.VMEM((mats, rows, cols), F32),
            pltpu.VMEM((mats, RANK, cols), F32),
            dma((mats,)),
            dma,
            dma((mats,)),
        ],
        compiler_params=pltpu.CompilerParams(vmem_limit_bytes=12 * 1024 * 1024),
        name="update",
    )(w, mom, q, prod, scale)
    return new_weight, new_momentum, jnp.transpose(new_right, (2, 0, 1))


def solution(mesh):
    nr, nc = mesh.shape["row"], mesh.shape["col"]
    nz = min(nr, 8)
    nx = nr // nz

    def run(weight, grad, momentum, right):
        return body(nx, nz, nc // 2, weight.shape[1] * nr, weight, grad, momentum, right)

    placed = P(None, "row", "col")
    return jax.shard_map(
        run,
        mesh=mesh,
        in_specs=(placed, placed, placed, P("col", None, None)),
        out_specs=(placed, placed, P("col", None, None)),
        check_vma=False,
    )
```

```python
import functools
import math

import jax
import jax.numpy as jnp
from jax import lax
from jax.experimental import pallas as pl
from jax.experimental.pallas import tpu as pltpu
from jax.sharding import PartitionSpec as P

MESH = pl.DeviceIdType.MESH
HIGHEST = lax.Precision.HIGHEST
F32 = jnp.float32
BF16 = jnp.bfloat16

EPSILON = 1e-06
DECAY = 0.95
RANK = 64


def two_sum(a, b):
    s = a + b
    back = s - a
    return s, (a - (s - back)) + (b - back)


def split(a):
    t = a * 4097.0
    high = t - (t - a)
    return high, a - high


def two_prod(a, b):
    p = a * b
    ah, al = split(a)
    bh, bl = split(b)
    return p, ((ah * bh - p) + ah * bl + al * bh) + al * bl


def add_pair(ah, al, bh, bl):
    s, t = two_sum(ah, bh)
    t = t + (al + bl)
    h = s + t
    return h, t - (h - s)


def nt(a, b, precision=None):
    return lax.dot_general(a, b, (((1,), (1,)), ((), ())), precision=precision, preferred_element_type=F32)


def nn(a, b, precision=None):
    return lax.dot_general(a, b, (((1,), (0,)), ((), ())), precision=precision, preferred_element_type=F32)


def tn(a, b, precision=None):
    return lax.dot_general(a, b, (((0,), (0,)), ((), ())), precision=precision, preferred_element_type=F32)


def cut(a):
    a1 = a.astype(BF16)
    rest = a - a1.astype(F32)
    a2 = rest.astype(BF16)
    return a1, a2, (rest - a2.astype(F32)).astype(BF16)


def cut_product(dot, a, b):
    a1, a2, a3 = cut(a)
    b1, b2, b3 = cut(b)
    p = dot(jnp.concatenate([a1, a2, a3], axis=0), b1)
    q = dot(jnp.concatenate([a1, a2], axis=0), b2)
    r = dot(a1, b3)
    return p[0:RANK] + ((p[RANK : 2 * RANK] + q[0:RANK]) + (p[2 * RANK :] + q[RANK:] + r))


def round_int(v):
    magic = 1.5 * 2.0**23
    return (v + magic) - magic


def exact_gram(x):
    top = jnp.maximum(jnp.max(jnp.abs(x), axis=1, keepdims=True), 1e-18)
    top = jnp.broadcast_to(top, (RANK, 128))
    power = jnp.floor(jnp.log(top) * (1.0 / math.log(2.0))) + 1.0
    unit = jnp.exp2(power - 7.0).astype(BF16).astype(F32)
    inverse = jnp.exp2(7.0 - power).astype(BF16).astype(F32)
    y = x * inverse[:, 0:1]
    slices = []
    for i in range(4):
        q = round_int(y)
        slices.append(q.astype(BF16))
        y = (y - q) * 256.0
    q = jnp.concatenate(slices, axis=0)
    e = nt(q, q)
    low = [e[RANK * a : RANK * (a + 1), 0:128] for a in range(4)]
    high = [e[RANK * a : RANK * (a + 1), 128:256] for a in range(4)]
    levels = [low[0], low[1], low[2] + high[0], low[3] + high[1], high[2], high[3]]
    s, t = levels[0], jnp.zeros_like(levels[0])
    for i in range(1, 6):
        s, err = two_sum(s, levels[i] * (2.0 ** (-8 * i)))
        t = t + err
    s2 = pltpu.roll(s, 64, 1) * (1.0 / 256.0)
    t2 = pltpu.roll(t, 64, 1) * (1.0 / 256.0)
    gh, gl = add_pair(s, t, s2, t2)
    rows = lax.broadcasted_iota(jnp.int32, (RANK, 128), 0)
    lanes = lax.broadcasted_iota(jnp.int32, (RANK, 128), 1)
    across = jnp.sum(jnp.where(rows == lanes, unit, 0.0), axis=0, keepdims=True)
    return gh * unit * across, gl * unit * across


def factor_block(mh, ml, first, count, begin, end):
    rows = lax.broadcasted_iota(jnp.int32, (count, 128), 0) + first
    lanes = lax.broadcasted_iota(jnp.int32, (count, 128), 1)
    half = jnp.where(lanes >= 64, 64, 0)
    column = lanes - half

    def step(k, carry):
        ah, al = mh[first:, :], ml[first:, :]
        rh, rl = mh[pl.ds(k, 1), :], ml[pl.ds(k, 1), :]
        index = half + k
        ch = jnp.take_along_axis(ah, index, axis=1)
        cl = jnp.take_along_axis(al, index, axis=1)
        dh = jnp.take_along_axis(jnp.broadcast_to(rh, (8, 128)), index[0:8], axis=1)[0:1]
        dl = jnp.take_along_axis(jnp.broadcast_to(rl, (8, 128)), index[0:8], axis=1)[0:1]
        inv = 1.0 / dh
        p, e = two_prod(dh, inv)
        inv_low = inv * (((1.0 - p) - e) - dl * inv)
        p, e = two_prod(ch, inv)
        t = e + (ch * inv_low + cl * inv)
        nh = p + t
        nl = t - (nh - p)
        later = rows > k
        nh = jnp.where(later, nh, 0.0)
        nl = jnp.where(later, nl, 0.0)
        here = column == k
        rh = jnp.where(here[0:1], 1.0, rh)
        rl = jnp.where(here[0:1], 0.0, rl)
        clear = here & later
        ah = jnp.where(clear, 0.0, ah)
        al = jnp.where(clear, 0.0, al)
        p, e = two_prod(nh, rh)
        q = e + (nh * rl + nl * rh)
        s, t = two_sum(ah, -p)
        t = t + (al - q)
        h = s + t
        mh[first:, :] = h
        ml[first:, :] = t - (h - s)
        return carry

    lax.fori_loop(begin, end, step, 0)


def factor_pair(mh, ml, begin, end):
    for first in range(begin, end, 8):
        factor_block(mh, ml, first, RANK - first, first, first + 8)


def inverse_of(mh):
    m = mh[...]
    rows = lax.broadcasted_iota(jnp.int32, (RANK, 128), 0)
    lanes = lax.broadcasted_iota(jnp.int32, (RANK, 128), 1)
    left = lanes < 64
    column = jnp.where(left, lanes, lanes - 64)
    diagonal = jnp.where(column == rows, m, 0.0)
    da = jnp.sum(jnp.where(left, diagonal, 0.0), axis=1, keepdims=True)
    db = jnp.sum(jnp.where(left, 0.0, diagonal), axis=1, keepdims=True)
    root = 1.0 / jnp.sqrt(jnp.where(left, da, db))
    return jnp.where(column < rows, m * root, jnp.where(column == rows, root, 0.0))


def exchange_kernel(nx, nz, ny, weight, grad, mom, right, w_out, m_out, q_out, prod_out, scale_out, s_v, g_v, r_v, part,
                    mate, ysend, yrecv, pt, pw, gp, gx, gz, ga, mh, ml, linv, tp, xrecv, zsend, zrecv, tfull, sq, load_sem,
                    w_sem, mate_send, mate_recv, y_send, y_recv, ag_send, ag_recv, fw_send, fw_recv, h_send, h_recv,
                    gx_send, gx_recv, gz_send, gz_recv, ga_send, ga_recv, tx_send, tx_recv, tz_send, tz_recv, az_send,
                    az_recv, ax_send, ax_recv, l_send, l_recv, sq_send, sq_recv):
    nr, nc = nx * nz, ny * 2
    mats = nc + 1
    last = mats - 1
    ff = 256 * nc
    row, col = lax.axis_index("row"), lax.axis_index("col")
    x, z = row // nz, row % nz
    y, k = col // 2, col % 2
    mate_id = (row, y * 2 + (1 - k))
    half = RANK // 2

    pending = []

    def finish():
        for c in pending:
            c.wait_send()

    def send(src, dst, sems, index, target):
        c = pltpu.make_async_remote_copy(src_ref=src, dst_ref=dst, send_sem=sems[0].at[index], recv_sem=sems[1].at[index],
                                         device_id=target, device_id_type=MESH)
        c.start()
        pending.append(c)
        return c

    def x_peer(i):
        return lax.rem(x + i, nx)

    def z_peer(i):
        return lax.rem(z + i, nz)

    def y_peer(i):
        return lax.rem(y + i, ny)

    far_first = sorted(range(1, nz), key=lambda i: -min(i, nz - i))

    load_right = pltpu.make_async_copy(right, r_v, load_sem.at[2 * mats])
    load_right.start()

    def loads(m):
        return (pltpu.make_async_copy(mom.at[m], s_v.at[m], load_sem.at[m]),
                pltpu.make_async_copy(grad.at[m], g_v.at[m], load_sem.at[mats + m]))

    turns = list(range(1, ny)) + [0]
    for m in [2 * y_peer(i) + (1 - k) for i in turns] + [last] + [2 * y_peer(i) + k for i in turns]:
        for c in loads(m):
            c.start()

    barrier = pltpu.get_barrier_semaphore()
    peers = [(row, lax.rem(col + i, nc)) for i in range(1, nc)]
    peers += [(x * nz + z_peer(i), col) for i in far_first]
    peers += [(x_peer(i) * nz + z, col) for i in range(1, nx)]
    for peer in peers:
        pl.semaphore_signal(barrier, inc=1, device_id=peer, device_id_type=MESH)
    load_right.wait()

    def power(m):
        for c in loads(m):
            c.wait()
        s = s_v[m] + g_v[m].astype(F32)
        s_v[m] = s
        part[m] = cut_product(nt, r_v[m], s)

    to_mate = {}
    mate_sems = (mate_send, mate_recv)
    for n, i in enumerate(turns):
        m = 2 * y_peer(i) + (1 - k)
        power(m)
    power(last)
    pl.semaphore_wait(barrier, len(peers))
    for i in turns:
        to_mate[i] = send(part.at[2 * y_peer(i) + (1 - k)], mate.at[i], mate_sems, i, mate_id)
    other_rows = pl.ds(pl.multiple_of((1 - k) * half, half), half)
    my_rows = pl.ds(pl.multiple_of(k * half, half), half)
    to_mate[ny] = send(part.at[last, other_rows], mate.at[ny, pl.ds(0, half)], mate_sems, ny, mate_id)
    load_weight = pltpu.make_async_copy(weight, w_out, w_sem)
    load_weight.start()

    own = 2 * y + k
    to_y = []
    for n, i in enumerate(turns):
        yd = y_peer(i)
        power(2 * yd + k)
        if n == 0:
            to_mate[ny].wait_recv()
            shared = part[last, my_rows, :] + mate[ny, 0:half, :]
        to_mate[i].wait_recv()
        if i == 0:
            yrecv[y, 0:RANK, :] = part[own] + mate[0]
            yrecv[y, RANK:, :] = shared
        else:
            ysend[i, 0:RANK, :] = part[2 * yd + k] + mate[i]
            ysend[i, RANK:, :] = shared
            to_y.append(send(ysend.at[i], yrecv.at[y], (y_send, y_recv), i, (row, 2 * yd + k)))
    for c in to_y:
        c.wait_recv()
    total = yrecv[0]
    for i in range(1, ny):
        total = total + yrecv[i]
    pt[last, my_rows, :] = total[RANK:]
    swap = send(pt.at[last, my_rows], pt.at[last, my_rows], (h_send, h_recv), 0, mate_id)
    pt[own] = total[0:RANK]
    gather = [send(pt.at[own], pt.at[own], (ag_send, ag_recv), i, (row, 2 * y_peer(i) + k)) for i in range(1, ny)]
    forward = {0: send(pt.at[own], pt.at[own], (fw_send, fw_recv), 0, mate_id)}

    lanes = lax.broadcasted_iota(jnp.int32, (RANK, 128), 1)
    ah, al = exact_gram(total[0:RANK])
    swap.wait_recv()
    bh, bl = exact_gram(pt[last])
    gp[0] = jnp.where(lanes < 64, ah, pltpu.roll(bh, 64, 1))
    gp[1] = jnp.where(lanes < 64, al, pltpu.roll(bl, 64, 1))
    share = RANK // nx

    def rows_of(d):
        return pl.ds(pl.multiple_of(d * share, share), share)

    to_x = [send(gp.at[:, rows_of(x_peer(i))], gx.at[x], (gx_send, gx_recv), i, (x_peer(i) * nz + z, col))
            for i in range(1, nx)]
    gx[x] = gp[:, rows_of(x), :]

    pairs = tp.shape[0]
    depth = tp.shape[2]
    t_x = {}

    def times(m, q, e):
        t = cut_product(nn, pt[m], s_v[m])
        at, to = e * RANK // depth, e * RANK % depth
        for h in range(2):
            tp[q, h * nx // 2 + at, to : to + RANK, :] = t[:, h * 128 : (h + 1) * 128]

    def block_out(turn, q):
        for i in range(1, nx):
            t_x[turn, i] = send(tp.at[q, x_peer(i)], xrecv.at[turn, i], (tx_send, tx_recv), (turn, i),
                                (x_peer(i) * nz + z, col))

    def times_pair(d):
        q = y_peer(d)
        times(2 * q, q, 0)
        times(2 * q + 1, q, 1)
        block_out(d, q)

    arrivals = sorted(range(1, ny), key=lambda d: min(d, ny - d))

    def pass_power(d):
        gather[ny - d - 1].wait_recv()
        m = 2 * y_peer(d) + k
        forward[d] = send(pt.at[m], pt.at[m], (fw_send, fw_recv), d, mate_id)

    at, to = RANK // depth, RANK % depth
    for h in range(2):
        tp[pairs - 1, h * nx // 2 + at, to : to + RANK, :] = jnp.zeros((RANK, 128), F32)
    times(last, pairs - 1, 0)
    block_out(ny, pairs - 1)
    forward[0].wait_recv()
    times_pair(0)
    for d in arrivals[:-1]:
        pass_power(d)

    def sum_pairs(ref, n):
        h, l = ref[0, 0], ref[0, 1]
        for i in range(1, n):
            h, l = add_pair(h, l, ref[i, 0], ref[i, 1])
        return h, l

    for c in to_x:
        c.wait_recv()
    h, l = sum_pairs(gx, nx)
    gz[z, 0] = h
    gz[z, 1] = l
    to_z = [send(gz.at[z], gz.at[z], (gz_send, gz_recv), i, (x * nz + z_peer(i), col)) for i in far_first]
    for n, d in enumerate(arrivals):
        if n == ny - 2:
            pass_power(d)
        forward[d].wait_recv()
        times_pair(d)
    for m in range(mats):
        pw[m] = jnp.transpose(pt[m])

    for d in [ny, 0] + arrivals:
        q = pairs - 1 if d == ny else y_peer(d)
        acc = tp[q, x]
        for i in range(1, nx):
            t_x[d, i].wait_recv()
            acc = acc + xrecv[d, i]
        zsend[q] = acc.reshape(zsend.shape[1:])
    t_z = [send(zsend.at[:, z_peer(j)], zrecv.at[j], (tz_send, tz_recv), j, (x * nz + z_peer(j), col)) for j in far_first]
    zrecv[0] = zsend[:, z]

    for c in to_z:
        c.wait_recv()
    h, l = sum_pairs(gz, nz)
    ga[x, 0] = h
    ga[x, 1] = l
    to_a = [send(ga.at[x], ga.at[x], (ga_send, ga_recv), i, (x_peer(i) * nz + z, col)) for i in range(1, nx)]

    for c in t_z:
        c.wait_recv()
    acc = zrecv[0]
    for j in range(1, nz):
        acc = acc + zrecv[j]
    tfull[:, x, z] = acc
    a_z = {j: send(tfull.at[:, x, z], tfull.at[:, x, z], (az_send, az_recv), j, (x * nz + z_peer(j), col))
           for j in far_first}
    a_x = []

    def pass_on(j):
        p = tfull.at[:, x, z_peer(nz - j)] if j else tfull.at[:, x, z]
        for i in range(1, nx):
            a_x.append(send(p, p, (ax_send, ax_recv), (i, j), (x_peer(i) * nz + z, col)))

    pass_on(0)
    for c in to_a:
        c.wait_recv()
    for i in range(nx):
        mh[i * share : (i + 1) * share, :] = ga[i, 0]
        ml[i * share : (i + 1) * share, :] = ga[i, 1]
    near_first = far_first[::-1]
    early = (nz - 1) // 2
    factor_pair(mh, ml, 0, 32)
    for j in near_first[:early]:
        a_z[j].wait_recv()
        pass_on(j)
    factor_pair(mh, ml, 32, 48)
    for j in near_first[early:]:
        a_z[j].wait_recv()
        pass_on(j)
    factor_pair(mh, ml, 48, RANK)

    linv[own] = inverse_of(mh)
    spread = [send(linv.at[own], linv.at[own], (l_send, l_recv), i, (row, lax.rem(col + i, nc))) for i in range(1, nc)]
    linv[last] = pltpu.roll(linv[own], 64, 1)
    for c in spread:
        c.wait_recv()
    left = lax.broadcasted_iota(jnp.int32, (pw.shape[1], 3 * RANK), 1) < 2 * RANK
    for m in range(mats):
        li = linv[m][:, 0:RANK]
        q = nt(pw[m], jnp.concatenate([li, li, li], axis=0), HIGHEST)
        q1 = q.astype(BF16)
        q_out[m] = jnp.where(left, q1.astype(F32), q - q1.astype(F32)).astype(BF16)
    for c in a_x:
        c.wait_recv()

    squares = jnp.zeros((8, 128), F32)
    places = lax.broadcasted_iota(jnp.int32, (8, 256), 0)
    for pair in range(0, mats, 2):
        sqs = []
        for m in (pair, pair + 1):
            if m >= mats:
                sqs.append(jnp.zeros((RANK, 256), F32))
                continue
            at, to = (m % 2) * RANK // depth, (m % 2) * RANK % depth
            t = jnp.concatenate([tfull[m // 2, h * nx // 2 + at].reshape(depth, 128)[to : to + RANK] for h in range(2)], axis=1)
            p = nn(linv[m][:, 0:RANK], t, HIGHEST)
            prod_out[m] = p
            sqs.append(p * p)
        ones = jnp.where(places == pair // 2, 1.0, 0.0)
        squares = squares + nt(ones, jnp.concatenate(sqs, axis=0), HIGHEST)
    sq[col] = squares
    to_all = [send(sq.at[col], sq.at[col], (sq_send, sq_recv), i, (row, lax.rem(col + i, nc))) for i in range(1, nc)]
    for m in range(mats):
        m_out[m] = s_v[m] - nn(q_out[m], stacked_pieces(prod_out[m] * (1.0 - DECAY)))
    for c in to_all:
        c.wait_recv()
    squares = sq[0]
    for i in range(1, nc):
        squares = squares + sq[i]
    scale_out[...] = jnp.transpose(1.0 / jnp.sqrt(squares * (1.0 / ff) + EPSILON))
    load_weight.wait()
    finish()


def stacked_pieces(p):
    p1 = p.astype(BF16)
    p2 = (p - p1.astype(F32)).astype(BF16)
    return jnp.concatenate([p1, p2, p1], axis=0)


def update_kernel(gain, w, mom, q, prod, scale, new_weight, new_mom, new_right, w_v, r_v, w_sem, m_sem, r_sem):
    mats = w.shape[0]
    move = pltpu.make_async_copy(mom, new_mom, m_sem)
    move.start()
    table = scale[...]
    moves = [move]
    for m in range(mats):
        column = table[(m % 2) * RANK : (m % 2 + 1) * RANK, m // 2 : m // 2 + 1]
        normed = prod[m] * column
        r_v[m] = normed
        c = pltpu.make_async_copy(r_v.at[m], new_right.at[m], r_sem.at[m])
        c.start()
        moves.append(c)
        w_v[m] = w[m] - nn(q[m], stacked_pieces(normed * gain))
        c = pltpu.make_async_copy(w_v.at[m], new_weight.at[m], w_sem.at[m])
        c.start()
        moves.append(c)
    for c in moves:
        c.wait()


def body(nx, nz, ny, depth, weight, grad, momentum, right):
    nr, nc = nx * nz, ny * 2
    mats, rows, cols = weight.shape
    ff = cols * nc
    rt = jnp.transpose(right, (1, 2, 0))
    pairs = (mats + 1) // 2
    block = 256 // nx
    tile = block // nz
    share = RANK // nx
    vmem = pl.BlockSpec(memory_space=pltpu.VMEM)
    hbm = pl.BlockSpec(memory_space=pltpu.HBM)
    dma = pltpu.SemaphoreType.DMA
    half = RANK // 2
    w, mom, q, prod, scale = pl.pallas_call(
        functools.partial(exchange_kernel, nx, nz, ny),
        out_shape=(
            jax.ShapeDtypeStruct((mats, rows, cols), F32),
            jax.ShapeDtypeStruct((mats, rows, cols), F32),
            jax.ShapeDtypeStruct((mats, rows, 3 * RANK), BF16),
            jax.ShapeDtypeStruct((mats, RANK, cols), F32),
            jax.ShapeDtypeStruct((128, 8), F32),
        ),
        in_specs=[hbm] * 4,
        out_specs=(vmem,) * 5,
        scratch_shapes=[
            pltpu.VMEM((mats, rows, cols), F32),
            pltpu.VMEM((mats, rows, cols), BF16),
            pltpu.VMEM((mats, RANK, cols), F32),
            pltpu.VMEM((mats, RANK, rows), F32),
            pltpu.VMEM((ny + 1, RANK, rows), F32),
            pltpu.VMEM((ny, RANK + half, rows), F32),
            pltpu.VMEM((ny, RANK + half, rows), F32),
            pltpu.VMEM((mats, RANK, rows), F32),
            pltpu.VMEM((mats, rows, RANK), F32),
            pltpu.VMEM((2, RANK, 128), F32),
            pltpu.VMEM((nx, 2, share, 128), F32),
            pltpu.VMEM((nz, 2, share, 128), F32),
            pltpu.VMEM((nx, 2, share, 128), F32),
            pltpu.VMEM((RANK, 128), F32),
            pltpu.VMEM((RANK, 128), F32),
            pltpu.VMEM((mats, RANK, 128), F32),
            pltpu.VMEM((pairs, nx, block, 128), F32),
            pltpu.VMEM((pairs, nx, block, 128), F32),
            pltpu.VMEM((pairs, nz, tile, 128), F32),
            pltpu.VMEM((nz, pairs, tile, 128), F32),
            pltpu.VMEM((pairs, nx, nz, tile, 128), F32),
            pltpu.VMEM((nc, 8, 128), F32),
            dma((2 * mats + 1,)),
            dma,
            dma((ny + 1,)), dma((ny + 1,)),
            dma((ny,)), dma((ny,)),
            dma((ny,)), dma((ny,)),
            dma((ny,)), dma((ny,)),
            dma((1,)), dma((1,)),
            dma((nx,)), dma((nx,)),
            dma((nz,)), dma((nz,)),
            dma((nx,)), dma((nx,)),
            dma((pairs, nx)), dma((pairs, nx)),
            dma((nz,)), dma((nz,)),
            dma((nz,)), dma((nz,)),
            dma((nx, nz)), dma((nx, nz)),
            dma((nc,)), dma((nc,)),
            dma((nc,)), dma((nc,)),
        ],
        compiler_params=pltpu.CompilerParams(
            collective_id=0, has_side_effects=True, vmem_limit_bytes=40 * 1024 * 1024
        ),
        name="exchange",
    )(*[pltpu.with_memory_space_constraint(v, pltpu.HBM) for v in (weight, grad, momentum, rt)])

    gain = math.sqrt(depth / ff)
    new_weight, new_momentum, new_right = pl.pallas_call(
        functools.partial(update_kernel, gain),
        out_shape=(
            jax.ShapeDtypeStruct(weight.shape, F32),
            jax.ShapeDtypeStruct(weight.shape, F32),
            jax.ShapeDtypeStruct((mats, RANK, cols), F32),
        ),
        in_specs=[vmem] * 5,
        out_specs=(hbm,) * 3,
        scratch_shapes=[
            pltpu.VMEM((mats, rows, cols), F32),
            pltpu.VMEM((mats, RANK, cols), F32),
            dma((mats,)),
            dma,
            dma((mats,)),
        ],
        compiler_params=pltpu.CompilerParams(vmem_limit_bytes=12 * 1024 * 1024),
        name="update",
    )(w, mom, q, prod, scale)
    return new_weight, new_momentum, jnp.transpose(new_right, (2, 0, 1))


def solution(mesh):
    nr, nc = mesh.shape["row"], mesh.shape["col"]
    nz = min(nr, 8)
    nx = nr // nz

    def run(weight, grad, momentum, right):
        return body(nx, nz, nc // 2, weight.shape[1] * nr, weight, grad, momentum, right)

    placed = P(None, "row", "col")
    return jax.shard_map(
        run,
        mesh=mesh,
        in_specs=(placed, placed, placed, P("col", None, None)),
        out_specs=(placed, placed, P("col", None, None)),
        check_vma=False,
    )
```

```python
import functools
import math

import jax
import jax.numpy as jnp
from jax import lax
from jax.experimental import pallas as pl
from jax.experimental.pallas import tpu as pltpu
from jax.sharding import PartitionSpec as P

MESH = pl.DeviceIdType.MESH
HIGHEST = lax.Precision.HIGHEST
F32 = jnp.float32
BF16 = jnp.bfloat16

EPSILON = 1e-06
DECAY = 0.95
RANK = 64


def two_sum(a, b):
    s = a + b
    back = s - a
    return s, (a - (s - back)) + (b - back)


def split(a):
    t = a * 4097.0
    high = t - (t - a)
    return high, a - high


def two_prod(a, b):
    p = a * b
    ah, al = split(a)
    bh, bl = split(b)
    return p, ((ah * bh - p) + ah * bl + al * bh) + al * bl


def add_pair(ah, al, bh, bl):
    s, t = two_sum(ah, bh)
    t = t + (al + bl)
    h = s + t
    return h, t - (h - s)


def nt(a, b, precision=None):
    return lax.dot_general(a, b, (((1,), (1,)), ((), ())), precision=precision, preferred_element_type=F32)


def nn(a, b, precision=None):
    return lax.dot_general(a, b, (((1,), (0,)), ((), ())), precision=precision, preferred_element_type=F32)


def tn(a, b, precision=None):
    return lax.dot_general(a, b, (((0,), (0,)), ((), ())), precision=precision, preferred_element_type=F32)


def cut(a):
    a1 = a.astype(BF16)
    rest = a - a1.astype(F32)
    a2 = rest.astype(BF16)
    return a1, a2, (rest - a2.astype(F32)).astype(BF16)


def cut_product(dot, a, b):
    a1, a2, a3 = cut(a)
    b1, b2, b3 = cut(b)
    p = dot(jnp.concatenate([a1, a2, a3], axis=0), b1)
    q = dot(jnp.concatenate([a1, a2], axis=0), b2)
    r = dot(a1, b3)
    return p[0:RANK] + ((p[RANK : 2 * RANK] + q[0:RANK]) + (p[2 * RANK :] + q[RANK:] + r))


def round_int(v):
    magic = 1.5 * 2.0**23
    return (v + magic) - magic


def exact_gram(x):
    top = jnp.maximum(jnp.max(jnp.abs(x), axis=1, keepdims=True), 1e-18)
    top = jnp.broadcast_to(top, (RANK, 128))
    power = jnp.floor(jnp.log(top) * (1.0 / math.log(2.0))) + 1.0
    unit = jnp.exp2(power - 7.0).astype(BF16).astype(F32)
    inverse = jnp.exp2(7.0 - power).astype(BF16).astype(F32)
    y = x * inverse[:, 0:1]
    slices = []
    for i in range(4):
        q = round_int(y)
        slices.append(q.astype(BF16))
        y = (y - q) * 256.0
    q = jnp.concatenate(slices, axis=0)
    e = nt(q, q)
    low = [e[RANK * a : RANK * (a + 1), 0:128] for a in range(4)]
    high = [e[RANK * a : RANK * (a + 1), 128:256] for a in range(4)]
    levels = [low[0], low[1], low[2] + high[0], low[3] + high[1], high[2], high[3]]
    s, t = levels[0], jnp.zeros_like(levels[0])
    for i in range(1, 6):
        s, err = two_sum(s, levels[i] * (2.0 ** (-8 * i)))
        t = t + err
    s2 = pltpu.roll(s, 64, 1) * (1.0 / 256.0)
    t2 = pltpu.roll(t, 64, 1) * (1.0 / 256.0)
    gh, gl = add_pair(s, t, s2, t2)
    rows = lax.broadcasted_iota(jnp.int32, (RANK, 128), 0)
    lanes = lax.broadcasted_iota(jnp.int32, (RANK, 128), 1)
    across = jnp.sum(jnp.where(rows == lanes, unit, 0.0), axis=0, keepdims=True)
    return gh * unit * across, gl * unit * across


def mul_pair(ah, al, bh, bl):
    p, e = two_prod(ah, bh)
    return p, e + (ah * bl + al * bh)


def factor_block(mh, ml, first):
    count = RANK - first
    rows = lax.broadcasted_iota(jnp.int32, (count, 128), 0) + first
    lanes = lax.broadcasted_iota(jnp.int32, (count, 128), 1)
    half = jnp.where(lanes >= 64, 64, 0)
    column = lanes - half
    h, l = mh[first:, :], ml[first:, :]

    def lane(v, k):
        return jnp.take_along_axis(jnp.broadcast_to(v, (8, 128)), half[0:8] + k, axis=1)[0:1]

    for k in range(first, first + 8, 2):
        i = k - first
        r1h, r1l = h[i : i + 1], l[i : i + 1]
        r2h, r2l = h[i + 1 : i + 2], l[i + 1 : i + 2]
        ah, al = lane(r1h, k), lane(r1l, k)
        bh, bl = lane(r1h, k + 1), lane(r1l, k + 1)
        ch, cl = lane(r2h, k + 1), lane(r2l, k + 1)
        p1, e1 = mul_pair(ah, al, ch, cl)
        p2, e2 = mul_pair(bh, bl, bh, bl)
        dh, dl = add_pair(p1, e1, -p2, -e2)
        inv = 1.0 / dh
        p, e = two_prod(dh, inv)
        inv_low = inv * (((1.0 - p) - e) - dl * inv)
        p1, e1 = mul_pair(r1h, r1l, ch, cl)
        p2, e2 = mul_pair(r2h, r2l, bh, bl)
        t1h, t1l = add_pair(p1, e1, -p2, -e2)
        p1, e1 = mul_pair(r2h, r2l, ah, al)
        p2, e2 = mul_pair(r1h, r1l, bh, bl)
        t2h, t2l = add_pair(p1, e1, -p2, -e2)
        n1h, n1l = mul_pair(t1h, t1l, inv, inv_low)
        n2h, n2l = mul_pair(t2h, t2l, inv, inv_low)
        later = rows > k + 1

        def spread(v):
            out = jnp.take_along_axis(jnp.broadcast_to(v, (count, 128)), half + rows, axis=1)
            return jnp.where(later, out, 0.0)

        n1h, n1l, n2h, n2l = spread(n1h), spread(n1l), spread(n2h), spread(n2l)
        here1, here2 = column == k, column == k + 1
        here = here1 | here2
        r1h = jnp.where(here1[0:1], 1.0, jnp.where(here2[0:1], 0.0, r1h))
        r2h = jnp.where(here2[0:1], 1.0, jnp.where(here1[0:1], 0.0, r2h))
        r1l = jnp.where(here[0:1], 0.0, r1l)
        r2l = jnp.where(here[0:1], 0.0, r2l)
        clear = here & later
        h = jnp.where(clear, 0.0, h)
        l = jnp.where(clear, 0.0, l)
        p, q = mul_pair(n1h, n1l, r1h, r1l)
        s, t = two_sum(h, -p)
        p2, q2 = mul_pair(n2h, n2l, r2h, r2l)
        s, t2 = two_sum(s, -p2)
        t = (t + t2) + (l - (q + q2))
        h = s + t
        l = t - (h - s)
    mh[first:, :] = h
    ml[first:, :] = l


def factor_pair(mh, ml, begin, end):
    for first in range(begin, end, 8):
        factor_block(mh, ml, first)


def inverse_of(mh, ml):
    m = mh[...]
    rows = lax.broadcasted_iota(jnp.int32, (RANK, 128), 0)
    lanes = lax.broadcasted_iota(jnp.int32, (RANK, 128), 1)
    left = lanes < 64
    column = jnp.where(left, lanes, lanes - 64)
    odd = (rows & 1) == 1

    def pick(v, mask):
        v = jnp.where(mask, v, 0.0)
        a = jnp.sum(jnp.where(left, v, 0.0), axis=1, keepdims=True)
        b = jnp.sum(jnp.where(left, 0.0, v), axis=1, keepdims=True)
        return jnp.where(left, a, b)

    same, next_to = column == rows, column == (rows ^ 1)
    ch, cl = pick(m, same), pick(ml[...], same)
    bh, bl = pick(m, next_to), pick(ml[...], next_to)
    ah, al = pltpu.roll(ch, 1, 0), pltpu.roll(cl, 1, 0)
    inv = 1.0 / ah
    p, e = two_prod(ah, inv)
    rh, rl = mul_pair(bh, bl, inv, inv * (((1.0 - p) - e) - al * inv))
    p, e = mul_pair(rh, rl, bh, bl)
    ph, _ = add_pair(ch, cl, -p, -e)
    root = 1.0 / jnp.sqrt(jnp.where(odd, ph, ch))
    ratio = jnp.where(odd, rh, 0.0)
    unit = jnp.where(column < rows - (rows & 1), m, jnp.where(column == rows, 1.0, 0.0))
    return (unit - ratio * pltpu.roll(unit, 1, 0)) * root


def exchange_kernel(nx, nz, ny, weight, grad, mom, right, w_out, m_out, q_out, prod_out, scale_out, s_v, g_v, r_v, part,
                    mate, ysend, yrecv, pt, pw, gp, gx, gz, ga, mh, ml, linv, tp, xrecv, zsend, zrecv, tfull, sq, load_sem,
                    w_sem, mate_send, mate_recv, y_send, y_recv, ag_send, ag_recv, fw_send, fw_recv, h_send, h_recv,
                    gx_send, gx_recv, gz_send, gz_recv, ga_send, ga_recv, tx_send, tx_recv, tz_send, tz_recv, az_send,
                    az_recv, ax_send, ax_recv, l_send, l_recv, sq_send, sq_recv):
    nr, nc = nx * nz, ny * 2
    mats = nc + 1
    last = mats - 1
    ff = 256 * nc
    row, col = lax.axis_index("row"), lax.axis_index("col")
    x, z = row // nz, row % nz
    y, k = col // 2, col % 2
    mate_id = (row, y * 2 + (1 - k))
    half = RANK // 2

    pending = []

    def finish():
        for c in pending:
            c.wait_send()

    def send(src, dst, sems, index, target):
        c = pltpu.make_async_remote_copy(src_ref=src, dst_ref=dst, send_sem=sems[0].at[index], recv_sem=sems[1].at[index],
                                         device_id=target, device_id_type=MESH)
        c.start()
        pending.append(c)
        return c

    def x_peer(i):
        return lax.rem(x + i, nx)

    def z_peer(i):
        return lax.rem(z + i, nz)

    def y_peer(i):
        return lax.rem(y + i, ny)

    far_first = sorted(range(1, nz), key=lambda i: -min(i, nz - i))

    load_right = pltpu.make_async_copy(right, r_v, load_sem.at[2 * mats])
    load_right.start()

    def loads(m):
        return (pltpu.make_async_copy(mom.at[m], s_v.at[m], load_sem.at[m]),
                pltpu.make_async_copy(grad.at[m], g_v.at[m], load_sem.at[mats + m]))

    turns = list(range(1, ny)) + [0]
    for m in [2 * y_peer(i) + (1 - k) for i in turns] + [last] + [2 * y_peer(i) + k for i in turns]:
        for c in loads(m):
            c.start()

    barrier = pltpu.get_barrier_semaphore()
    peers = [(row, lax.rem(col + i, nc)) for i in range(1, nc)]
    peers += [(x * nz + z_peer(i), col) for i in far_first]
    peers += [(x_peer(i) * nz + z, col) for i in range(1, nx)]
    for peer in peers:
        pl.semaphore_signal(barrier, inc=1, device_id=peer, device_id_type=MESH)
    load_right.wait()

    def power(m):
        for c in loads(m):
            c.wait()
        s = s_v[m] + g_v[m].astype(F32)
        s_v[m] = s
        part[m] = cut_product(nt, r_v[m], s)

    to_mate = {}
    mate_sems = (mate_send, mate_recv)
    for n, i in enumerate(turns):
        m = 2 * y_peer(i) + (1 - k)
        power(m)
    power(last)
    pl.semaphore_wait(barrier, len(peers))
    for i in turns:
        to_mate[i] = send(part.at[2 * y_peer(i) + (1 - k)], mate.at[i], mate_sems, i, mate_id)
    other_rows = pl.ds(pl.multiple_of((1 - k) * half, half), half)
    my_rows = pl.ds(pl.multiple_of(k * half, half), half)
    to_mate[ny] = send(part.at[last, other_rows], mate.at[ny, pl.ds(0, half)], mate_sems, ny, mate_id)
    load_weight = pltpu.make_async_copy(weight, w_out, w_sem)
    load_weight.start()

    own = 2 * y + k
    to_y = []
    for n, i in enumerate(turns):
        yd = y_peer(i)
        power(2 * yd + k)
        if n == 0:
            to_mate[ny].wait_recv()
            shared = part[last, my_rows, :] + mate[ny, 0:half, :]
        to_mate[i].wait_recv()
        if i == 0:
            yrecv[y, 0:RANK, :] = part[own] + mate[0]
            yrecv[y, RANK:, :] = shared
        else:
            ysend[i, 0:RANK, :] = part[2 * yd + k] + mate[i]
            ysend[i, RANK:, :] = shared
            to_y.append(send(ysend.at[i], yrecv.at[y], (y_send, y_recv), i, (row, 2 * yd + k)))
    for c in to_y:
        c.wait_recv()
    total = yrecv[0]
    for i in range(1, ny):
        total = total + yrecv[i]
    pt[last, my_rows, :] = total[RANK:]
    swap = send(pt.at[last, my_rows], pt.at[last, my_rows], (h_send, h_recv), 0, mate_id)
    pt[own] = total[0:RANK]
    gather = [send(pt.at[own], pt.at[own], (ag_send, ag_recv), i, (row, 2 * y_peer(i) + k)) for i in range(1, ny)]
    forward = {0: send(pt.at[own], pt.at[own], (fw_send, fw_recv), 0, mate_id)}

    lanes = lax.broadcasted_iota(jnp.int32, (RANK, 128), 1)
    ah, al = exact_gram(total[0:RANK])
    swap.wait_recv()
    bh, bl = exact_gram(pt[last])
    gp[0] = jnp.where(lanes < 64, ah, pltpu.roll(bh, 64, 1))
    gp[1] = jnp.where(lanes < 64, al, pltpu.roll(bl, 64, 1))
    share = RANK // nx

    def rows_of(d):
        return pl.ds(pl.multiple_of(d * share, share), share)

    to_x = [send(gp.at[:, rows_of(x_peer(i))], gx.at[x], (gx_send, gx_recv), i, (x_peer(i) * nz + z, col))
            for i in range(1, nx)]
    gx[x] = gp[:, rows_of(x), :]

    pairs = tp.shape[0]
    depth = tp.shape[2]
    t_x = {}

    def times(m, q, e):
        t = cut_product(nn, pt[m], s_v[m])
        at, to = e * RANK // depth, e * RANK % depth
        for h in range(2):
            tp[q, h * nx // 2 + at, to : to + RANK, :] = t[:, h * 128 : (h + 1) * 128]

    def block_out(turn, q):
        for i in range(1, nx):
            t_x[turn, i] = send(tp.at[q, x_peer(i)], xrecv.at[turn, i], (tx_send, tx_recv), (turn, i),
                                (x_peer(i) * nz + z, col))

    def times_pair(d):
        q = y_peer(d)
        times(2 * q, q, 0)
        times(2 * q + 1, q, 1)
        block_out(d, q)

    arrivals = sorted(range(1, ny), key=lambda d: min(d, ny - d))

    def pass_power(d):
        gather[ny - d - 1].wait_recv()
        m = 2 * y_peer(d) + k
        forward[d] = send(pt.at[m], pt.at[m], (fw_send, fw_recv), d, mate_id)

    at, to = RANK // depth, RANK % depth
    for h in range(2):
        tp[pairs - 1, h * nx // 2 + at, to : to + RANK, :] = jnp.zeros((RANK, 128), F32)
    times(last, pairs - 1, 0)
    block_out(ny, pairs - 1)
    forward[0].wait_recv()
    times_pair(0)
    for d in arrivals[:-1]:
        pass_power(d)

    def sum_pairs(ref, n):
        h, l = ref[0, 0], ref[0, 1]
        for i in range(1, n):
            h, l = add_pair(h, l, ref[i, 0], ref[i, 1])
        return h, l

    for c in to_x:
        c.wait_recv()
    h, l = sum_pairs(gx, nx)
    gz[z, 0] = h
    gz[z, 1] = l
    to_z = [send(gz.at[z], gz.at[z], (gz_send, gz_recv), i, (x * nz + z_peer(i), col)) for i in far_first]
    for n, d in enumerate(arrivals):
        if n == ny - 2:
            pass_power(d)
        forward[d].wait_recv()
        times_pair(d)
    for m in range(mats):
        pw[m] = jnp.transpose(pt[m])

    for d in [ny, 0] + arrivals:
        q = pairs - 1 if d == ny else y_peer(d)
        acc = tp[q, x]
        for i in range(1, nx):
            t_x[d, i].wait_recv()
            acc = acc + xrecv[d, i]
        zsend[q] = acc.reshape(zsend.shape[1:])
    t_z = [send(zsend.at[:, z_peer(j)], zrecv.at[j], (tz_send, tz_recv), j, (x * nz + z_peer(j), col)) for j in far_first]
    zrecv[0] = zsend[:, z]

    for c in to_z:
        c.wait_recv()
    h, l = sum_pairs(gz, nz)
    ga[x, 0] = h
    ga[x, 1] = l
    to_a = [send(ga.at[x], ga.at[x], (ga_send, ga_recv), i, (x_peer(i) * nz + z, col)) for i in range(1, nx)]

    for c in t_z:
        c.wait_recv()
    acc = zrecv[0]
    for j in range(1, nz):
        acc = acc + zrecv[j]
    tfull[:, x, z] = acc
    a_z = {j: send(tfull.at[:, x, z], tfull.at[:, x, z], (az_send, az_recv), j, (x * nz + z_peer(j), col))
           for j in far_first}
    a_x = []

    def pass_on(j):
        p = tfull.at[:, x, z_peer(nz - j)] if j else tfull.at[:, x, z]
        for i in range(1, nx):
            a_x.append(send(p, p, (ax_send, ax_recv), (i, j), (x_peer(i) * nz + z, col)))

    pass_on(0)
    for c in to_a:
        c.wait_recv()
    for i in range(nx):
        mh[i * share : (i + 1) * share, :] = ga[i, 0]
        ml[i * share : (i + 1) * share, :] = ga[i, 1]
    near_first = far_first[::-1]

    def pass_next(n):
        for j in near_first[:n]:
            a_z[j].wait_recv()
            pass_on(j)
        del near_first[:n]

    factor_pair(mh, ml, 0, 32)
    pass_next(2)
    factor_pair(mh, ml, 32, 48)
    pass_next(2)
    factor_pair(mh, ml, 48, RANK)

    inverse = inverse_of(mh, ml)
    low = pltpu.roll(inverse[half:], 64, 1)
    first_lanes = lax.broadcasted_iota(jnp.int32, (half, 128), 1) < 64
    linv[own] = jnp.where(first_lanes, inverse[0:half], low)
    linv[last] = jnp.where(first_lanes, pltpu.roll(inverse[0:half], 64, 1), inverse[half:])
    spread = [send(linv.at[own], linv.at[own], (l_send, l_recv), i, (row, lax.rem(col + i, nc))) for i in range(1, nc)]
    pass_next(nz)

    def inverse_at(m):
        return jnp.concatenate([linv[m][:, 0:RANK], linv[m][:, RANK:]], axis=0)

    for c in spread + a_x:
        c.wait_recv()
    squares = jnp.zeros((8, 128), F32)
    places = lax.broadcasted_iota(jnp.int32, (8, 256), 0)
    for pair in range(0, mats, 2):
        sqs = []
        for m in (pair, pair + 1):
            if m >= mats:
                sqs.append(jnp.zeros((RANK, 256), F32))
                continue
            at, to = (m % 2) * RANK // depth, (m % 2) * RANK % depth
            t = jnp.concatenate([tfull[m // 2, h * nx // 2 + at].reshape(depth, 128)[to : to + RANK] for h in range(2)], axis=1)
            p = nn(inverse_at(m), t, HIGHEST)
            prod_out[m] = p
            sqs.append(p * p)
        ones = jnp.where(places == pair // 2, 1.0, 0.0)
        squares = squares + nt(ones, jnp.concatenate(sqs, axis=0), HIGHEST)
    sq[col] = squares
    to_all = [send(sq.at[col], sq.at[col], (sq_send, sq_recv), i, (row, lax.rem(col + i, nc))) for i in range(1, nc)]
    left = lax.broadcasted_iota(jnp.int32, (pw.shape[1], 3 * RANK), 1) < 2 * RANK
    for m in range(mats):
        li = inverse_at(m)
        q = nt(pw[m], jnp.concatenate([li, li, li], axis=0), HIGHEST)
        q1 = q.astype(BF16)
        pieces = jnp.where(left, q1.astype(F32), q - q1.astype(F32)).astype(BF16)
        q_out[m] = pieces
        m_out[m] = s_v[m] - nn(pieces, stacked_pieces(prod_out[m] * (1.0 - DECAY)))
    for c in to_all:
        c.wait_recv()
    squares = sq[0]
    for i in range(1, nc):
        squares = squares + sq[i]
    scale_out[...] = jnp.transpose(1.0 / jnp.sqrt(squares * (1.0 / ff) + EPSILON))
    load_weight.wait()
    finish()


def stacked_pieces(p):
    p1 = p.astype(BF16)
    p2 = (p - p1.astype(F32)).astype(BF16)
    return jnp.concatenate([p1, p2, p1], axis=0)


def update_kernel(gain, w, mom, q, prod, scale, new_weight, new_mom, new_right, w_v, r_v, w_sem, m_sem, r_sem):
    mats = w.shape[0]
    move = pltpu.make_async_copy(mom, new_mom, m_sem)
    move.start()
    table = scale[...]
    moves = [move]
    for m in range(mats):
        column = table[(m % 2) * RANK : (m % 2 + 1) * RANK, m // 2 : m // 2 + 1]
        normed = prod[m] * column
        r_v[m] = normed
        c = pltpu.make_async_copy(r_v.at[m], new_right.at[m], r_sem.at[m])
        c.start()
        moves.append(c)
        w_v[m] = w[m] - nn(q[m], stacked_pieces(normed * gain))
        c = pltpu.make_async_copy(w_v.at[m], new_weight.at[m], w_sem.at[m])
        c.start()
        moves.append(c)
    for c in moves:
        c.wait()


def body(nx, nz, ny, depth, weight, grad, momentum, right):
    nr, nc = nx * nz, ny * 2
    mats, rows, cols = weight.shape
    ff = cols * nc
    rt = jnp.transpose(right, (1, 2, 0))
    pairs = (mats + 1) // 2
    block = 256 // nx
    tile = block // nz
    share = RANK // nx
    vmem = pl.BlockSpec(memory_space=pltpu.VMEM)
    hbm = pl.BlockSpec(memory_space=pltpu.HBM)
    dma = pltpu.SemaphoreType.DMA
    half = RANK // 2
    w, mom, q, prod, scale = pl.pallas_call(
        functools.partial(exchange_kernel, nx, nz, ny),
        out_shape=(
            jax.ShapeDtypeStruct((mats, rows, cols), F32),
            jax.ShapeDtypeStruct((mats, rows, cols), F32),
            jax.ShapeDtypeStruct((mats, rows, 3 * RANK), BF16),
            jax.ShapeDtypeStruct((mats, RANK, cols), F32),
            jax.ShapeDtypeStruct((128, 8), F32),
        ),
        in_specs=[hbm] * 4,
        out_specs=(vmem,) * 5,
        scratch_shapes=[
            pltpu.VMEM((mats, rows, cols), F32),
            pltpu.VMEM((mats, rows, cols), BF16),
            pltpu.VMEM((mats, RANK, cols), F32),
            pltpu.VMEM((mats, RANK, rows), F32),
            pltpu.VMEM((ny + 1, RANK, rows), F32),
            pltpu.VMEM((ny, RANK + half, rows), F32),
            pltpu.VMEM((ny, RANK + half, rows), F32),
            pltpu.VMEM((mats, RANK, rows), F32),
            pltpu.VMEM((mats, rows, RANK), F32),
            pltpu.VMEM((2, RANK, 128), F32),
            pltpu.VMEM((nx, 2, share, 128), F32),
            pltpu.VMEM((nz, 2, share, 128), F32),
            pltpu.VMEM((nx, 2, share, 128), F32),
            pltpu.VMEM((RANK, 128), F32),
            pltpu.VMEM((RANK, 128), F32),
            pltpu.VMEM((mats, half, 128), F32),
            pltpu.VMEM((pairs, nx, block, 128), F32),
            pltpu.VMEM((pairs, nx, block, 128), F32),
            pltpu.VMEM((pairs, nz, tile, 128), F32),
            pltpu.VMEM((nz, pairs, tile, 128), F32),
            pltpu.VMEM((pairs, nx, nz, tile, 128), F32),
            pltpu.VMEM((nc, 8, 128), F32),
            dma((2 * mats + 1,)),
            dma,
            dma((ny + 1,)), dma((ny + 1,)),
            dma((ny,)), dma((ny,)),
            dma((ny,)), dma((ny,)),
            dma((ny,)), dma((ny,)),
            dma((1,)), dma((1,)),
            dma((nx,)), dma((nx,)),
            dma((nz,)), dma((nz,)),
            dma((nx,)), dma((nx,)),
            dma((pairs, nx)), dma((pairs, nx)),
            dma((nz,)), dma((nz,)),
            dma((nz,)), dma((nz,)),
            dma((nx, nz)), dma((nx, nz)),
            dma((nc,)), dma((nc,)),
            dma((nc,)), dma((nc,)),
        ],
        compiler_params=pltpu.CompilerParams(
            collective_id=0, has_side_effects=True, vmem_limit_bytes=40 * 1024 * 1024
        ),
        name="exchange",
    )(*[pltpu.with_memory_space_constraint(v, pltpu.HBM) for v in (weight, grad, momentum, rt)])

    gain = math.sqrt(depth / ff)
    new_weight, new_momentum, new_right = pl.pallas_call(
        functools.partial(update_kernel, gain),
        out_shape=(
            jax.ShapeDtypeStruct(weight.shape, F32),
            jax.ShapeDtypeStruct(weight.shape, F32),
            jax.ShapeDtypeStruct((mats, RANK, cols), F32),
        ),
        in_specs=[vmem] * 5,
        out_specs=(hbm,) * 3,
        scratch_shapes=[
            pltpu.VMEM((mats, rows, cols), F32),
            pltpu.VMEM((mats, RANK, cols), F32),
            dma((mats,)),
            dma,
            dma((mats,)),
        ],
        compiler_params=pltpu.CompilerParams(vmem_limit_bytes=12 * 1024 * 1024),
        name="update",
    )(w, mom, q, prod, scale)
    return new_weight, new_momentum, jnp.transpose(new_right, (2, 0, 1))


def solution(mesh):
    nr, nc = mesh.shape["row"], mesh.shape["col"]
    nz = min(nr, 8)
    nx = nr // nz

    def run(weight, grad, momentum, right):
        return body(nx, nz, nc // 2, weight.shape[1] * nr, weight, grad, momentum, right)

    placed = P(None, "row", "col")
    return jax.shard_map(
        run,
        mesh=mesh,
        in_specs=(placed, placed, placed, P("col", None, None)),
        out_specs=(placed, placed, P("col", None, None)),
        check_vma=False,
    )
```

```python
import functools
import math

import jax
import jax.numpy as jnp
from jax import lax
from jax.experimental import pallas as pl
from jax.experimental.pallas import tpu as pltpu
from jax.sharding import PartitionSpec as P

MESH = pl.DeviceIdType.MESH
F32 = jnp.float32
BF16 = jnp.bfloat16

EPSILON = 1e-06
DECAY = 0.95
RANK = 64


def two_sum(a, b):
    s = a + b
    back = s - a
    return s, (a - (s - back)) + (b - back)


def split(a):
    t = a * 4097.0
    high = t - (t - a)
    return high, a - high


def two_prod(a, b):
    p = a * b
    ah, al = split(a)
    bh, bl = split(b)
    return p, ((ah * bh - p) + ah * bl + al * bh) + al * bl


def add_pair(ah, al, bh, bl):
    s, t = two_sum(ah, bh)
    t = t + (al + bl)
    h = s + t
    return h, t - (h - s)


def nt(a, b, precision=None):
    return lax.dot_general(a, b, (((1,), (1,)), ((), ())), precision=precision, preferred_element_type=F32)


def nn(a, b, precision=None):
    return lax.dot_general(a, b, (((1,), (0,)), ((), ())), precision=precision, preferred_element_type=F32)


def tn(a, b, precision=None):
    return lax.dot_general(a, b, (((0,), (0,)), ((), ())), precision=precision, preferred_element_type=F32)


def cut(a):
    a1 = a.astype(BF16)
    rest = a - a1.astype(F32)
    a2 = rest.astype(BF16)
    return a1, a2, (rest - a2.astype(F32)).astype(BF16)


def cut_product(dot, a, b):
    a1, a2, a3 = cut(a)
    b1, b2, b3 = cut(b)
    p = dot(jnp.concatenate([a1, a2, a3], axis=0), b1)
    q = dot(jnp.concatenate([a1, a2], axis=0), b2)
    r = dot(a1, b3)
    return p[0:RANK] + ((p[RANK : 2 * RANK] + q[0:RANK]) + (p[2 * RANK :] + q[RANK:] + r))


def six_left(a):
    a1, a2, a3 = cut(a)
    return jnp.concatenate([a1, a2, a1, a3, a2, a1], axis=1)


def six_right(a, axis):
    a1, a2, a3 = cut(a)
    return jnp.concatenate([a1, a1, a2, a1, a2, a3], axis=axis)


def round_int(v):
    magic = 1.5 * 2.0**23
    return (v + magic) - magic


def exact_gram(x):
    top = jnp.maximum(jnp.max(jnp.abs(x), axis=1, keepdims=True), 1e-18)
    top = jnp.broadcast_to(top, (RANK, 128))
    power = jnp.floor(jnp.log(top) * (1.0 / math.log(2.0))) + 1.0
    unit = jnp.exp2(power - 7.0).astype(BF16).astype(F32)
    inverse = jnp.exp2(7.0 - power).astype(BF16).astype(F32)
    y = x * inverse[:, 0:1]
    slices = []
    for i in range(4):
        q = round_int(y)
        slices.append(q.astype(BF16))
        y = (y - q) * 256.0
    q = jnp.concatenate(slices, axis=0)
    e = nt(q, q)
    low = [e[RANK * a : RANK * (a + 1), 0:128] for a in range(4)]
    high = [e[RANK * a : RANK * (a + 1), 128:256] for a in range(4)]
    levels = [low[0], low[1], low[2] + high[0], low[3] + high[1], high[2], high[3]]
    s, t = levels[0], jnp.zeros_like(levels[0])
    for i in range(1, 6):
        s, err = two_sum(s, levels[i] * (2.0 ** (-8 * i)))
        t = t + err
    s2 = pltpu.roll(s, 64, 1) * (1.0 / 256.0)
    t2 = pltpu.roll(t, 64, 1) * (1.0 / 256.0)
    gh, gl = add_pair(s, t, s2, t2)
    rows = lax.broadcasted_iota(jnp.int32, (RANK, 128), 0)
    lanes = lax.broadcasted_iota(jnp.int32, (RANK, 128), 1)
    across = jnp.sum(jnp.where(rows == lanes, unit, 0.0), axis=0, keepdims=True)
    return gh * unit * across, gl * unit * across


def mul_pair(ah, al, bh, bl):
    p, e = two_prod(ah, bh)
    return p, e + (ah * bl + al * bh)


def sub_pairs(h, l, m1, r1, m2, r2):
    p, q = mul_pair(*m1, *r1)
    s, e = two_sum(h, -p)
    p2, q2 = mul_pair(*m2, *r2)
    s, e2 = two_sum(s, -p2)
    e = (e + e2) + (l - (q + q2))
    h = s + e
    return h, e - (h - s)


def cross(a, b, c, d):
    p1, e1 = mul_pair(*a, *b)
    p2, e2 = mul_pair(*c, *d)
    return add_pair(p1, e1, -p2, -e2)


def factor_block(mh, ml, first):
    tiles = (RANK - first) // 8
    rows = lax.broadcasted_iota(jnp.int32, (8, 128), 0)
    lanes = lax.broadcasted_iota(jnp.int32, (8, 128), 1)
    half = jnp.where(lanes >= 64, 64, 0)
    column = lanes - half
    m = [(mh[first + 8 * t : first + 8 * t + 8, :], ml[first + 8 * t : first + 8 * t + 8, :]) for t in range(tiles)]

    def row(v, i):
        return tuple(jnp.broadcast_to(part[i : i + 1], (8, 128)) for part in v)

    def masked(mask, v):
        return tuple(jnp.where(mask, part, 0.0) for part in v)

    own = [tuple(jnp.take_along_axis(part, half + (first + j), axis=1) for part in m[0]) for j in range(8)]
    steps = []
    for i in range(0, 8, 2):
        k = first + i
        c1, c2 = own[i], own[i + 1]
        a, b, c = row(c1, i), row(c2, i), row(c2, i + 1)
        dh, dl = cross(a, c, b, b)
        inv = 1.0 / dh
        p, e = two_prod(dh, inv)
        inv = (inv, inv * (((1.0 - p) - e) - dl * inv))
        later = rows > i + 1
        n1 = masked(later, mul_pair(*cross(c1, c, c2, b), *inv))
        n2 = masked(later, mul_pair(*cross(c2, a, c1, b), *inv))
        for j in range(i + 2, 8):
            own[j] = sub_pairs(*own[j], n1, row(own[j], i), n2, row(own[j], i + 1))
        r1, r2 = row(m[0], i), row(m[0], i + 1)
        w1 = mul_pair(*cross(r1, c, r2, b), *inv)
        w2 = mul_pair(*cross(r2, a, r1, b), *inv)
        here1, here2 = column == k, column == k + 1
        here = here1 | here2
        r1 = (jnp.where(here1, 1.0, jnp.where(here2, 0.0, r1[0])), jnp.where(here, 0.0, r1[1]))
        r2 = (jnp.where(here2, 1.0, jnp.where(here1, 0.0, r2[0])), jnp.where(here, 0.0, r2[1]))
        m[0] = sub_pairs(*masked(jnp.logical_not(here & later), m[0]), n1, r1, n2, r2)
        steps.append((here, w1, w2, r1, r2))
    for t in range(1, tiles):
        index = half + (rows + (first + 8 * t))

        def spread(v):
            return tuple(jnp.take_along_axis(part, index, axis=1) for part in v)

        for here, w1, w2, r1, r2 in steps:
            m[t] = sub_pairs(*masked(jnp.logical_not(here), m[t]), spread(w1), r1, spread(w2), r2)
    for t in range(tiles):
        mh[first + 8 * t : first + 8 * t + 8, :] = m[t][0]
        ml[first + 8 * t : first + 8 * t + 8, :] = m[t][1]


def factor_pair(mh, ml, begin, end):
    for first in range(begin, end, 8):
        factor_block(mh, ml, first)


def inverse_of(mh, ml):
    m = mh[...]
    rows = lax.broadcasted_iota(jnp.int32, (RANK, 128), 0)
    lanes = lax.broadcasted_iota(jnp.int32, (RANK, 128), 1)
    left = lanes < 64
    column = jnp.where(left, lanes, lanes - 64)
    odd = (rows & 1) == 1

    def pick(v, mask):
        v = jnp.where(mask, v, 0.0)
        a = jnp.sum(jnp.where(left, v, 0.0), axis=1, keepdims=True)
        b = jnp.sum(jnp.where(left, 0.0, v), axis=1, keepdims=True)
        return jnp.where(left, a, b)

    same, next_to = column == rows, column == (rows ^ 1)
    ch, cl = pick(m, same), pick(ml[...], same)
    bh, bl = pick(m, next_to), pick(ml[...], next_to)
    ah, al = pltpu.roll(ch, 1, 0), pltpu.roll(cl, 1, 0)
    inv = 1.0 / ah
    p, e = two_prod(ah, inv)
    rh, rl = mul_pair(bh, bl, inv, inv * (((1.0 - p) - e) - al * inv))
    p, e = mul_pair(rh, rl, bh, bl)
    ph, _ = add_pair(ch, cl, -p, -e)
    root = 1.0 / jnp.sqrt(jnp.where(odd, ph, ch))
    ratio = jnp.where(odd, rh, 0.0)
    unit = jnp.where(column < rows - (rows & 1), m, jnp.where(column == rows, 1.0, 0.0))
    return (unit - ratio * pltpu.roll(unit, 1, 0)) * root


def exchange_kernel(nx, nz, ny, weight, grad, mom, right, w_out, m_out, q_out, prod_out, scale_out, s_v, g_v, r_v, part,
                    mate, ysend, yrecv, pt, pw, gp, gx, gz, ga, mh, ml, linv, tp, xrecv, zsend, zrecv, tfull, sq, load_sem,
                    w_sem, mate_send, mate_recv, y_send, y_recv, ag_send, ag_recv, fw_send, fw_recv, h_send, h_recv,
                    gx_send, gx_recv, gz_send, gz_recv, ga_send, ga_recv, tx_send, tx_recv, tz_send, tz_recv, az_send,
                    az_recv, ax_send, ax_recv, l_send, l_recv, sq_send, sq_recv):
    nr, nc = nx * nz, ny * 2
    mats = nc + 1
    last = mats - 1
    ff = 256 * nc
    row, col = lax.axis_index("row"), lax.axis_index("col")
    x, z = row // nz, row % nz
    y, k = col // 2, col % 2
    mate_id = (row, y * 2 + (1 - k))
    half = RANK // 2

    pending = []

    def finish():
        for c in pending:
            c.wait_send()

    def send(src, dst, sems, index, target):
        c = pltpu.make_async_remote_copy(src_ref=src, dst_ref=dst, send_sem=sems[0].at[index], recv_sem=sems[1].at[index],
                                         device_id=target, device_id_type=MESH)
        c.start()
        pending.append(c)
        return c

    def x_peer(i):
        return lax.rem(x + i, nx)

    def z_peer(i):
        return lax.rem(z + i, nz)

    def y_peer(i):
        return lax.rem(y + i, ny)

    far_first = sorted(range(1, nz), key=lambda i: -min(i, nz - i))

    load_right = pltpu.make_async_copy(right, r_v, load_sem.at[2 * mats])
    load_right.start()

    def loads(m):
        return (pltpu.make_async_copy(mom.at[m], s_v.at[m], load_sem.at[m]),
                pltpu.make_async_copy(grad.at[m], g_v.at[m], load_sem.at[mats + m]))

    turns = list(range(1, ny)) + [0]
    for m in [2 * y_peer(i) + (1 - k) for i in turns] + [last] + [2 * y_peer(i) + k for i in turns]:
        for c in loads(m):
            c.start()

    barrier = pltpu.get_barrier_semaphore()
    peers = [(row, lax.rem(col + i, nc)) for i in range(1, nc)]
    peers += [(x * nz + z_peer(i), col) for i in far_first]
    peers += [(x_peer(i) * nz + z, col) for i in range(1, nx)]
    for peer in peers:
        pl.semaphore_signal(barrier, inc=1, device_id=peer, device_id_type=MESH)
    load_right.wait()

    def power(m):
        for c in loads(m):
            c.wait()
        s = s_v[m] + g_v[m].astype(F32)
        s_v[m] = s
        part[m] = cut_product(nt, r_v[m], s)

    to_mate = {}
    mate_sems = (mate_send, mate_recv)
    for n, i in enumerate(turns):
        m = 2 * y_peer(i) + (1 - k)
        power(m)
    power(last)
    pl.semaphore_wait(barrier, len(peers))
    for i in turns:
        to_mate[i] = send(part.at[2 * y_peer(i) + (1 - k)], mate.at[i], mate_sems, i, mate_id)
    other_rows = pl.ds(pl.multiple_of((1 - k) * half, half), half)
    my_rows = pl.ds(pl.multiple_of(k * half, half), half)
    to_mate[ny] = send(part.at[last, other_rows], mate.at[ny, pl.ds(0, half)], mate_sems, ny, mate_id)
    load_weight = pltpu.make_async_copy(weight, w_out, w_sem)
    load_weight.start()

    own = 2 * y + k
    to_y = []
    for n, i in enumerate(turns):
        yd = y_peer(i)
        power(2 * yd + k)
        if n == 0:
            to_mate[ny].wait_recv()
            shared = part[last, my_rows, :] + mate[ny, 0:half, :]
        to_mate[i].wait_recv()
        if i == 0:
            yrecv[y, 0:RANK, :] = part[own] + mate[0]
            yrecv[y, RANK:, :] = shared
        else:
            ysend[i, 0:RANK, :] = part[2 * yd + k] + mate[i]
            ysend[i, RANK:, :] = shared
            to_y.append(send(ysend.at[i], yrecv.at[y], (y_send, y_recv), i, (row, 2 * yd + k)))
    for c in to_y:
        c.wait_recv()
    total = yrecv[0]
    for i in range(1, ny):
        total = total + yrecv[i]
    pt[last, my_rows, :] = total[RANK:]
    swap = send(pt.at[last, my_rows], pt.at[last, my_rows], (h_send, h_recv), 0, mate_id)
    pt[own] = total[0:RANK]
    gather = [send(pt.at[own], pt.at[own], (ag_send, ag_recv), i, (row, 2 * y_peer(i) + k)) for i in range(1, ny)]
    forward = {0: send(pt.at[own], pt.at[own], (fw_send, fw_recv), 0, mate_id)}

    lanes = lax.broadcasted_iota(jnp.int32, (RANK, 128), 1)
    ah, al = exact_gram(total[0:RANK])
    swap.wait_recv()
    bh, bl = exact_gram(pt[last])
    gp[0] = jnp.where(lanes < 64, ah, pltpu.roll(bh, 64, 1))
    gp[1] = jnp.where(lanes < 64, al, pltpu.roll(bl, 64, 1))
    share = RANK // nx

    def rows_of(d):
        return pl.ds(pl.multiple_of(d * share, share), share)

    to_x = [send(gp.at[:, rows_of(x_peer(i))], gx.at[x], (gx_send, gx_recv), i, (x_peer(i) * nz + z, col))
            for i in range(1, nx)]
    gx[x] = gp[:, rows_of(x), :]

    pairs = tp.shape[0]
    depth = tp.shape[2]
    t_x = {}

    def times(m, q, e):
        t = cut_product(nn, pt[m], s_v[m])
        at, to = e * RANK // depth, e * RANK % depth
        for h in range(2):
            tp[q, h * nx // 2 + at, to : to + RANK, :] = t[:, h * 128 : (h + 1) * 128]

    def block_out(turn, q):
        for i in range(1, nx):
            t_x[turn, i] = send(tp.at[q, x_peer(i)], xrecv.at[turn, i], (tx_send, tx_recv), (turn, i),
                                (x_peer(i) * nz + z, col))

    def times_pair(d):
        q = y_peer(d)
        times(2 * q, q, 0)
        times(2 * q + 1, q, 1)
        block_out(d, q)

    arrivals = sorted(range(1, ny), key=lambda d: min(d, ny - d))

    def pass_power(d):
        gather[ny - d - 1].wait_recv()
        m = 2 * y_peer(d) + k
        forward[d] = send(pt.at[m], pt.at[m], (fw_send, fw_recv), d, mate_id)

    at, to = RANK // depth, RANK % depth
    for h in range(2):
        tp[pairs - 1, h * nx // 2 + at, to : to + RANK, :] = jnp.zeros((RANK, 128), F32)
    times(last, pairs - 1, 0)
    block_out(ny, pairs - 1)
    forward[0].wait_recv()
    times_pair(0)
    for d in arrivals[:-1]:
        pass_power(d)

    def sum_pairs(ref, n):
        h, l = ref[0, 0], ref[0, 1]
        for i in range(1, n):
            h, l = add_pair(h, l, ref[i, 0], ref[i, 1])
        return h, l

    for c in to_x:
        c.wait_recv()
    h, l = sum_pairs(gx, nx)
    gz[z, 0] = h
    gz[z, 1] = l
    to_z = [send(gz.at[z], gz.at[z], (gz_send, gz_recv), i, (x * nz + z_peer(i), col)) for i in far_first]
    for n, d in enumerate(arrivals):
        if n == ny - 2:
            pass_power(d)
        forward[d].wait_recv()
        times_pair(d)
    for m in range(mats):
        pw[m] = six_right(jnp.transpose(pt[m]), 1)

    for d in [ny, 0] + arrivals:
        q = pairs - 1 if d == ny else y_peer(d)
        acc = tp[q, x]
        for i in range(1, nx):
            t_x[d, i].wait_recv()
            acc = acc + xrecv[d, i]
        zsend[:, q] = acc.reshape(nz, *zsend.shape[2:])
    t_z = [send(zsend.at[z_peer(j)], zrecv.at[j], (tz_send, tz_recv), j, (x * nz + z_peer(j), col)) for j in far_first]
    zrecv[0] = zsend[z]

    for c in to_z:
        c.wait_recv()
    h, l = sum_pairs(gz, nz)
    ga[x, 0] = h
    ga[x, 1] = l
    to_a = [send(ga.at[x], ga.at[x], (ga_send, ga_recv), i, (x_peer(i) * nz + z, col)) for i in range(1, nx)]

    for c in t_z:
        c.wait_recv()
    acc = zrecv[0]
    for j in range(1, nz):
        acc = acc + zrecv[j]
    tfull[x, z] = acc
    a_z = {j: send(tfull.at[x, z], tfull.at[x, z], (az_send, az_recv), j, (x * nz + z_peer(j), col))
           for j in far_first}
    a_x = []

    def pass_on(j):
        p = tfull.at[x, z_peer(nz - j)] if j else tfull.at[x, z]
        for i in range(1, nx):
            a_x.append(send(p, p, (ax_send, ax_recv), (i, j), (x_peer(i) * nz + z, col)))

    pass_on(0)
    for c in to_a:
        c.wait_recv()
    for i in range(nx):
        mh[i * share : (i + 1) * share, :] = ga[i, 0]
        ml[i * share : (i + 1) * share, :] = ga[i, 1]
    near_first = far_first[::-1]

    def pass_next(n):
        for j in near_first[:n]:
            a_z[j].wait_recv()
            pass_on(j)
        del near_first[:n]

    factor_pair(mh, ml, 0, 32)
    pass_next(2)
    factor_pair(mh, ml, 32, 48)
    pass_next(2)
    factor_pair(mh, ml, 48, RANK)

    inverse = inverse_of(mh, ml)
    low = pltpu.roll(inverse[half:], 64, 1)
    first_lanes = lax.broadcasted_iota(jnp.int32, (half, 128), 1) < 64
    linv[own] = jnp.where(first_lanes, inverse[0:half], low)
    linv[last] = jnp.where(first_lanes, pltpu.roll(inverse[0:half], 64, 1), inverse[half:])
    spread = [send(linv.at[own], linv.at[own], (l_send, l_recv), i, (row, lax.rem(col + i, nc))) for i in range(1, nc)]
    pass_next(nz)

    def inverse_at(m):
        return six_left(jnp.concatenate([linv[m][:, 0:RANK], linv[m][:, RANK:]], axis=0))

    for c in spread + a_x:
        c.wait_recv()
    squares = jnp.zeros((16, 128), F32)
    places = lax.broadcasted_iota(jnp.int32, (16, 256), 0)
    inverses = [inverse_at(m) for m in range(mats)]
    for pair in range(0, mats, 2):
        sqs = []
        for m in (pair, pair + 1):
            if m >= mats:
                sqs.append(jnp.zeros((RANK, 256), F32))
                continue
            at, to = (m % 2) * RANK // depth, (m % 2) * RANK % depth
            t = jnp.concatenate([tfull[h * nx // 2 + at, :, m // 2].reshape(depth, 128)[to : to + RANK] for h in range(2)], axis=1)
            p = nn(inverses[m], six_right(t, 0))
            prod_out[m] = p
            sqs.append(p * p)
        ones = jnp.where(places == pair // 2, 1.0, 0.0).astype(BF16)
        both = jnp.concatenate(sqs, axis=0)
        high = both.astype(BF16)
        squares = squares + nt(ones, high) + nt(ones, (both - high.astype(F32)).astype(BF16))
    sq[col] = squares[0:8]
    to_all = [send(sq.at[col], sq.at[col], (sq_send, sq_recv), i, (row, lax.rem(col + i, nc))) for i in range(1, nc)]
    left = lax.broadcasted_iota(jnp.int32, (pw.shape[1], 3 * RANK), 1) < 2 * RANK
    for m in range(mats):
        q = nt(pw[m], jnp.concatenate([inverses[m]] * 3, axis=0))
        q1 = q.astype(BF16)
        pieces = jnp.where(left, q1.astype(F32), q - q1.astype(F32)).astype(BF16)
        q_out[m] = pieces
        m_out[m] = s_v[m] - nn(pieces, stacked_pieces(prod_out[m] * (1.0 - DECAY)))
    for c in to_all:
        c.wait_recv()
    squares = sq[0]
    for i in range(1, nc):
        squares = squares + sq[i]
    scale_out[...] = jnp.transpose(1.0 / jnp.sqrt(squares * (1.0 / ff) + EPSILON))
    load_weight.wait()
    finish()


def stacked_pieces(p):
    p1 = p.astype(BF16)
    p2 = (p - p1.astype(F32)).astype(BF16)
    return jnp.concatenate([p1, p2, p1], axis=0)


def update_kernel(gain, w, mom, q, prod, scale, new_weight, new_mom, new_right, w_v, r_v, w_sem, m_sem, r_sem):
    mats = w.shape[0]
    move = pltpu.make_async_copy(mom, new_mom, m_sem)
    move.start()
    table = scale[...]
    moves = [move]
    for m in range(mats):
        column = table[(m % 2) * RANK : (m % 2 + 1) * RANK, m // 2 : m // 2 + 1]
        normed = prod[m] * column
        r_v[m] = normed
        c = pltpu.make_async_copy(r_v.at[m], new_right.at[m], r_sem.at[m])
        c.start()
        moves.append(c)
        w_v[m] = w[m] - nn(q[m], stacked_pieces(normed * gain))
        c = pltpu.make_async_copy(w_v.at[m], new_weight.at[m], w_sem.at[m])
        c.start()
        moves.append(c)
    for c in moves:
        c.wait()


def body(nx, nz, ny, depth, weight, grad, momentum, right):
    nr, nc = nx * nz, ny * 2
    mats, rows, cols = weight.shape
    ff = cols * nc
    rt = jnp.transpose(right, (1, 2, 0))
    pairs = (mats + 1) // 2
    block = 256 // nx
    tile = block // nz
    share = RANK // nx
    vmem = pl.BlockSpec(memory_space=pltpu.VMEM)
    hbm = pl.BlockSpec(memory_space=pltpu.HBM)
    dma = pltpu.SemaphoreType.DMA
    half = RANK // 2
    w, mom, q, prod, scale = pl.pallas_call(
        functools.partial(exchange_kernel, nx, nz, ny),
        out_shape=(
            jax.ShapeDtypeStruct((mats, rows, cols), F32),
            jax.ShapeDtypeStruct((mats, rows, cols), F32),
            jax.ShapeDtypeStruct((mats, rows, 3 * RANK), BF16),
            jax.ShapeDtypeStruct((mats, RANK, cols), F32),
            jax.ShapeDtypeStruct((128, 8), F32),
        ),
        in_specs=[hbm] * 4,
        out_specs=(vmem,) * 5,
        scratch_shapes=[
            pltpu.VMEM((mats, rows, cols), F32),
            pltpu.VMEM((mats, rows, cols), BF16),
            pltpu.VMEM((mats, RANK, cols), F32),
            pltpu.VMEM((mats, RANK, rows), F32),
            pltpu.VMEM((ny + 1, RANK, rows), F32),
            pltpu.VMEM((ny, RANK + half, rows), F32),
            pltpu.VMEM((ny, RANK + half, rows), F32),
            pltpu.VMEM((mats, RANK, rows), F32),
            pltpu.VMEM((mats, rows, 6 * RANK), BF16),
            pltpu.VMEM((2, RANK, 128), F32),
            pltpu.VMEM((nx, 2, share, 128), F32),
            pltpu.VMEM((nz, 2, share, 128), F32),
            pltpu.VMEM((nx, 2, share, 128), F32),
            pltpu.VMEM((RANK, 128), F32),
            pltpu.VMEM((RANK, 128), F32),
            pltpu.VMEM((mats, half, 128), F32),
            pltpu.VMEM((pairs, nx, block, 128), F32),
            pltpu.VMEM((pairs, nx, block, 128), F32),
            pltpu.VMEM((nz, pairs, tile, 128), F32),
            pltpu.VMEM((nz, pairs, tile, 128), F32),
            pltpu.VMEM((nx, nz, pairs, tile, 128), F32),
            pltpu.VMEM((nc, 8, 128), F32),
            dma((2 * mats + 1,)),
            dma,
            dma((ny + 1,)), dma((ny + 1,)),
            dma((ny,)), dma((ny,)),
            dma((ny,)), dma((ny,)),
            dma((ny,)), dma((ny,)),
            dma((1,)), dma((1,)),
            dma((nx,)), dma((nx,)),
            dma((nz,)), dma((nz,)),
            dma((nx,)), dma((nx,)),
            dma((pairs, nx)), dma((pairs, nx)),
            dma((nz,)), dma((nz,)),
            dma((nz,)), dma((nz,)),
            dma((nx, nz)), dma((nx, nz)),
            dma((nc,)), dma((nc,)),
            dma((nc,)), dma((nc,)),
        ],
        compiler_params=pltpu.CompilerParams(
            collective_id=0, has_side_effects=True, vmem_limit_bytes=40 * 1024 * 1024
        ),
        name="exchange",
    )(*[pltpu.with_memory_space_constraint(v, pltpu.HBM) for v in (weight, grad, momentum, rt)])

    gain = math.sqrt(depth / ff)
    new_weight, new_momentum, new_right = pl.pallas_call(
        functools.partial(update_kernel, gain),
        out_shape=(
            jax.ShapeDtypeStruct(weight.shape, F32),
            jax.ShapeDtypeStruct(weight.shape, F32),
            jax.ShapeDtypeStruct((mats, RANK, cols), F32),
        ),
        in_specs=[vmem] * 5,
        out_specs=(hbm,) * 3,
        scratch_shapes=[
            pltpu.VMEM((mats, rows, cols), F32),
            pltpu.VMEM((mats, RANK, cols), F32),
            dma((mats,)),
            dma,
            dma((mats,)),
        ],
        compiler_params=pltpu.CompilerParams(vmem_limit_bytes=12 * 1024 * 1024),
        name="update",
    )(w, mom, q, prod, scale)
    return new_weight, new_momentum, jnp.transpose(new_right, (2, 0, 1))


def solution(mesh):
    nr, nc = mesh.shape["row"], mesh.shape["col"]
    nz = min(nr, 8)
    nx = nr // nz

    def run(weight, grad, momentum, right):
        return body(nx, nz, nc // 2, weight.shape[1] * nr, weight, grad, momentum, right)

    placed = P(None, "row", "col")
    return jax.shard_map(
        run,
        mesh=mesh,
        in_specs=(placed, placed, placed, P("col", None, None)),
        out_specs=(placed, placed, P("col", None, None)),
        check_vma=False,
    )
```

```python
import functools
import math

import jax
import jax.numpy as jnp
from jax import lax
from jax.experimental import pallas as pl
from jax.experimental.pallas import tpu as pltpu
from jax.sharding import PartitionSpec as P

MESH = pl.DeviceIdType.MESH
F32 = jnp.float32
BF16 = jnp.bfloat16

EPSILON = 1e-06
DECAY = 0.95
RANK = 64


def two_sum(a, b):
    s = a + b
    back = s - a
    return s, (a - (s - back)) + (b - back)


def split(a):
    t = a * 4097.0
    high = t - (t - a)
    return high, a - high


def two_prod(a, b):
    p = a * b
    ah, al = split(a)
    bh, bl = split(b)
    return p, ((ah * bh - p) + ah * bl + al * bh) + al * bl


def add_pair(ah, al, bh, bl):
    s, t = two_sum(ah, bh)
    t = t + (al + bl)
    h = s + t
    return h, t - (h - s)


def nt(a, b, precision=None):
    return lax.dot_general(a, b, (((1,), (1,)), ((), ())), precision=precision, preferred_element_type=F32)


def nn(a, b, precision=None):
    return lax.dot_general(a, b, (((1,), (0,)), ((), ())), precision=precision, preferred_element_type=F32)


def tn(a, b, precision=None):
    return lax.dot_general(a, b, (((0,), (0,)), ((), ())), precision=precision, preferred_element_type=F32)


def cut(a):
    a1 = a.astype(BF16)
    rest = a - a1.astype(F32)
    a2 = rest.astype(BF16)
    return a1, a2, (rest - a2.astype(F32)).astype(BF16)


def cut_product(dot, a, b):
    a1, a2, a3 = cut(a)
    b1, b2, b3 = cut(b)
    p = dot(jnp.concatenate([a1, a2, a3], axis=0), b1)
    q = dot(jnp.concatenate([a1, a2], axis=0), b2)
    r = dot(a1, b3)
    return p[0:RANK] + ((p[RANK : 2 * RANK] + q[0:RANK]) + (p[2 * RANK :] + q[RANK:] + r))


def six_left(a):
    a1, a2, a3 = cut(a)
    return jnp.concatenate([a1, a2, a1, a3, a2, a1], axis=1)


def six_right(a, axis):
    a1, a2, a3 = cut(a)
    return jnp.concatenate([a1, a1, a2, a1, a2, a3], axis=axis)


def round_int(v):
    magic = 1.5 * 2.0**23
    return (v + magic) - magic


def exact_gram(x):
    top = jnp.maximum(jnp.max(jnp.abs(x), axis=1, keepdims=True), 1e-18)
    top = jnp.broadcast_to(top, (RANK, 128))
    power = jnp.floor(jnp.log(top) * (1.0 / math.log(2.0))) + 1.0
    unit = jnp.exp2(power - 7.0).astype(BF16).astype(F32)
    inverse = jnp.exp2(7.0 - power).astype(BF16).astype(F32)
    y = x * inverse[:, 0:1]
    slices = []
    for i in range(4):
        q = round_int(y)
        slices.append(q.astype(BF16))
        y = (y - q) * 256.0
    q = jnp.concatenate(slices, axis=0)
    e = nt(q, q)
    low = [e[RANK * a : RANK * (a + 1), 0:128] for a in range(4)]
    high = [e[RANK * a : RANK * (a + 1), 128:256] for a in range(4)]
    levels = [low[0], low[1], low[2] + high[0], low[3] + high[1], high[2], high[3]]
    s, t = levels[0], jnp.zeros_like(levels[0])
    for i in range(1, 6):
        s, err = two_sum(s, levels[i] * (2.0 ** (-8 * i)))
        t = t + err
    s2 = pltpu.roll(s, 64, 1) * (1.0 / 256.0)
    t2 = pltpu.roll(t, 64, 1) * (1.0 / 256.0)
    gh, gl = add_pair(s, t, s2, t2)
    rows = lax.broadcasted_iota(jnp.int32, (RANK, 128), 0)
    lanes = lax.broadcasted_iota(jnp.int32, (RANK, 128), 1)
    across = jnp.sum(jnp.where(rows == lanes, unit, 0.0), axis=0, keepdims=True)
    return gh * unit * across, gl * unit * across


def mul_pair(ah, al, bh, bl):
    p, e = two_prod(ah, bh)
    return p, e + (ah * bl + al * bh)


def sub_pairs(h, l, m1, r1, m2, r2):
    p, q = mul_pair(*m1, *r1)
    s, e = two_sum(h, -p)
    p2, q2 = mul_pair(*m2, *r2)
    s, e2 = two_sum(s, -p2)
    e = (e + e2) + (l - (q + q2))
    h = s + e
    return h, e - (h - s)


def cross(a, b, c, d):
    p1, e1 = mul_pair(*a, *b)
    p2, e2 = mul_pair(*c, *d)
    return add_pair(p1, e1, -p2, -e2)


def factor_block(mh, ml, first):
    tiles = (RANK - first) // 8
    rows = lax.broadcasted_iota(jnp.int32, (8, 128), 0)
    lanes = lax.broadcasted_iota(jnp.int32, (8, 128), 1)
    half = jnp.where(lanes >= 64, 64, 0)
    column = lanes - half
    m = [(mh[first + 8 * t : first + 8 * t + 8, :], ml[first + 8 * t : first + 8 * t + 8, :]) for t in range(tiles)]

    def row(v, i):
        return tuple(jnp.broadcast_to(part[i : i + 1], (8, 128)) for part in v)

    def masked(mask, v):
        return tuple(jnp.where(mask, part, 0.0) for part in v)

    own = [tuple(jnp.take_along_axis(part, half + (first + j), axis=1) for part in m[0]) for j in range(8)]
    steps = []
    for i in range(0, 8, 2):
        k = first + i
        c1, c2 = own[i], own[i + 1]
        a, b, c = row(c1, i), row(c2, i), row(c2, i + 1)
        dh, dl = cross(a, c, b, b)
        inv = 1.0 / dh
        p, e = two_prod(dh, inv)
        inv = (inv, inv * (((1.0 - p) - e) - dl * inv))
        later = rows > i + 1
        n1 = masked(later, mul_pair(*cross(c1, c, c2, b), *inv))
        n2 = masked(later, mul_pair(*cross(c2, a, c1, b), *inv))
        for j in range(i + 2, 8):
            own[j] = sub_pairs(*own[j], n1, row(own[j], i), n2, row(own[j], i + 1))
        r1, r2 = row(m[0], i), row(m[0], i + 1)
        w1 = mul_pair(*cross(r1, c, r2, b), *inv)
        w2 = mul_pair(*cross(r2, a, r1, b), *inv)
        here1, here2 = column == k, column == k + 1
        here = here1 | here2
        r1 = (jnp.where(here1, 1.0, jnp.where(here2, 0.0, r1[0])), jnp.where(here, 0.0, r1[1]))
        r2 = (jnp.where(here2, 1.0, jnp.where(here1, 0.0, r2[0])), jnp.where(here, 0.0, r2[1]))
        m[0] = sub_pairs(*masked(jnp.logical_not(here & later), m[0]), n1, r1, n2, r2)
        steps.append((here, w1, w2, r1, r2))
    for t in range(1, tiles):
        index = half + (rows + (first + 8 * t))

        def spread(v):
            return tuple(jnp.take_along_axis(part, index, axis=1) for part in v)

        for here, w1, w2, r1, r2 in steps:
            m[t] = sub_pairs(*masked(jnp.logical_not(here), m[t]), spread(w1), r1, spread(w2), r2)
    for t in range(tiles):
        mh[first + 8 * t : first + 8 * t + 8, :] = m[t][0]
        ml[first + 8 * t : first + 8 * t + 8, :] = m[t][1]


def factor_pair(mh, ml, begin, end):
    for first in range(begin, end, 8):
        factor_block(mh, ml, first)


def inverse_of(mh, ml):
    m = mh[...]
    rows = lax.broadcasted_iota(jnp.int32, (RANK, 128), 0)
    lanes = lax.broadcasted_iota(jnp.int32, (RANK, 128), 1)
    left = lanes < 64
    column = jnp.where(left, lanes, lanes - 64)
    odd = (rows & 1) == 1

    def pick(v, mask):
        v = jnp.where(mask, v, 0.0)
        a = jnp.sum(jnp.where(left, v, 0.0), axis=1, keepdims=True)
        b = jnp.sum(jnp.where(left, 0.0, v), axis=1, keepdims=True)
        return jnp.where(left, a, b)

    same, next_to = column == rows, column == (rows ^ 1)
    ch, cl = pick(m, same), pick(ml[...], same)
    bh, bl = pick(m, next_to), pick(ml[...], next_to)
    ah, al = pltpu.roll(ch, 1, 0), pltpu.roll(cl, 1, 0)
    inv = 1.0 / ah
    p, e = two_prod(ah, inv)
    rh, rl = mul_pair(bh, bl, inv, inv * (((1.0 - p) - e) - al * inv))
    p, e = mul_pair(rh, rl, bh, bl)
    ph, _ = add_pair(ch, cl, -p, -e)
    root = 1.0 / jnp.sqrt(jnp.where(odd, ph, ch))
    ratio = jnp.where(odd, rh, 0.0)
    unit = jnp.where(column < rows - (rows & 1), m, jnp.where(column == rows, 1.0, 0.0))
    return (unit - ratio * pltpu.roll(unit, 1, 0)) * root


def exchange_kernel(nx, nz, ny, weight, grad, mom, right, w_out, m_out, q_out, prod_out, scale_out, s_v, g_v, r_v, part,
                    mate, ysend, yrecv, pt, pw, gp, gx, gz, ga, mh, ml, linv, tp, xrecv, zsend, zrecv, tfull, sq, load_sem,
                    w_sem, mate_send, mate_recv, y_send, y_recv, ag_send, ag_recv, fw_send, fw_recv, h_send, h_recv,
                    gx_send, gx_recv, gz_send, gz_recv, ga_send, ga_recv, tx_send, tx_recv, tz_send, tz_recv, az_send,
                    az_recv, ax_send, ax_recv, l_send, l_recv, sq_send, sq_recv):
    nr, nc = nx * nz, ny * 2
    mats = nc + 1
    last = mats - 1
    ff = 256 * nc
    row, col = lax.axis_index("row"), lax.axis_index("col")
    x, z = row // nz, row % nz
    y, k = col // 2, col % 2
    mate_id = (row, y * 2 + (1 - k))
    half = RANK // 2

    pending = []

    def finish():
        for c in pending:
            c.wait_send()

    def send(src, dst, sems, index, target):
        c = pltpu.make_async_remote_copy(src_ref=src, dst_ref=dst, send_sem=sems[0].at[index], recv_sem=sems[1].at[index],
                                         device_id=target, device_id_type=MESH)
        c.start()
        pending.append(c)
        return c

    def x_peer(i):
        return lax.rem(x + i, nx)

    def z_peer(i):
        return lax.rem(z + i, nz)

    def y_peer(i):
        return lax.rem(y + i, ny)

    far_first = sorted(range(1, nz), key=lambda i: -min(i, nz - i))

    load_right = pltpu.make_async_copy(right, r_v, load_sem.at[2 * mats])
    load_right.start()

    def loads(m):
        return (pltpu.make_async_copy(mom.at[m], s_v.at[m], load_sem.at[m]),
                pltpu.make_async_copy(grad.at[m], g_v.at[m], load_sem.at[mats + m]))

    turns = list(range(1, ny)) + [0]
    for m in [2 * y_peer(i) + (1 - k) for i in turns] + [last] + [2 * y_peer(i) + k for i in turns]:
        for c in loads(m):
            c.start()

    barrier = pltpu.get_barrier_semaphore()
    peers = [(row, lax.rem(col + i, nc)) for i in range(1, nc)]
    peers += [(x * nz + z_peer(i), col) for i in far_first]
    peers += [(x_peer(i) * nz + z, col) for i in range(1, nx)]
    for peer in peers:
        pl.semaphore_signal(barrier, inc=1, device_id=peer, device_id_type=MESH)
    load_right.wait()

    def power(m):
        for c in loads(m):
            c.wait()
        s = s_v[m] + g_v[m].astype(F32)
        s_v[m] = s
        part[m] = cut_product(nt, r_v[m], s)

    to_mate = {}
    mate_sems = (mate_send, mate_recv)
    for n, i in enumerate(turns):
        m = 2 * y_peer(i) + (1 - k)
        power(m)
    power(last)
    pl.semaphore_wait(barrier, len(peers))
    for i in turns:
        to_mate[i] = send(part.at[2 * y_peer(i) + (1 - k)], mate.at[i], mate_sems, i, mate_id)
    other_rows = pl.ds(pl.multiple_of((1 - k) * half, half), half)
    my_rows = pl.ds(pl.multiple_of(k * half, half), half)
    to_mate[ny] = send(part.at[last, other_rows], mate.at[ny, pl.ds(0, half)], mate_sems, ny, mate_id)
    load_weight = pltpu.make_async_copy(weight, w_out, w_sem)
    load_weight.start()

    own = 2 * y + k
    to_y = []
    for n, i in enumerate(turns):
        yd = y_peer(i)
        power(2 * yd + k)
        if n == 0:
            to_mate[ny].wait_recv()
            shared = part[last, my_rows, :] + mate[ny, 0:half, :]
        to_mate[i].wait_recv()
        if i == 0:
            yrecv[y, 0:RANK, :] = part[own] + mate[0]
            yrecv[y, RANK:, :] = shared
        else:
            ysend[i, 0:RANK, :] = part[2 * yd + k] + mate[i]
            ysend[i, RANK:, :] = shared
            to_y.append(send(ysend.at[i], yrecv.at[y], (y_send, y_recv), i, (row, 2 * yd + k)))
    for c in to_y:
        c.wait_recv()
    total = yrecv[0]
    for i in range(1, ny):
        total = total + yrecv[i]
    pt[last, my_rows, :] = total[RANK:]
    swap = send(pt.at[last, my_rows], pt.at[last, my_rows], (h_send, h_recv), 0, mate_id)
    pt[own] = total[0:RANK]
    gather = [send(pt.at[own], pt.at[own], (ag_send, ag_recv), i, (row, 2 * y_peer(i) + k)) for i in range(1, ny)]
    forward = {0: send(pt.at[own], pt.at[own], (fw_send, fw_recv), 0, mate_id)}

    lanes = lax.broadcasted_iota(jnp.int32, (RANK, 128), 1)
    ah, al = exact_gram(total[0:RANK])
    swap.wait_recv()
    bh, bl = exact_gram(pt[last])
    gp[0] = jnp.where(lanes < 64, ah, pltpu.roll(bh, 64, 1))
    gp[1] = jnp.where(lanes < 64, al, pltpu.roll(bl, 64, 1))
    share = RANK // nx

    def rows_of(d):
        return pl.ds(pl.multiple_of(d * share, share), share)

    to_x = [send(gp.at[:, rows_of(x_peer(i))], gx.at[x], (gx_send, gx_recv), i, (x_peer(i) * nz + z, col))
            for i in range(1, nx)]
    gx[x] = gp[:, rows_of(x), :]

    pairs = tp.shape[0]
    depth = tp.shape[2]
    t_x = {}

    def times(m, q, e):
        t = cut_product(nn, pt[m], s_v[m])
        at, to = e * RANK // depth, e * RANK % depth
        for h in range(2):
            tp[q, h * nx // 2 + at, to : to + RANK, :] = t[:, h * 128 : (h + 1) * 128]

    def block_out(turn, q):
        for i in range(1, nx):
            t_x[turn, i] = send(tp.at[q, x_peer(i)], xrecv.at[turn, i], (tx_send, tx_recv), (turn, i),
                                (x_peer(i) * nz + z, col))

    def times_pair(d):
        q = y_peer(d)
        times(2 * q, q, 0)
        times(2 * q + 1, q, 1)
        block_out(d, q)

    arrivals = sorted(range(1, ny), key=lambda d: min(d, ny - d))

    def pass_power(d):
        gather[ny - d - 1].wait_recv()
        m = 2 * y_peer(d) + k
        forward[d] = send(pt.at[m], pt.at[m], (fw_send, fw_recv), d, mate_id)

    at, to = RANK // depth, RANK % depth
    for h in range(2):
        tp[pairs - 1, h * nx // 2 + at, to : to + RANK, :] = jnp.zeros((RANK, 128), F32)
    times(last, pairs - 1, 0)
    block_out(ny, pairs - 1)
    forward[0].wait_recv()
    times_pair(0)
    for d in arrivals[:-1]:
        pass_power(d)

    def sum_pairs(ref, n):
        h, l = ref[0, 0], ref[0, 1]
        for i in range(1, n):
            h, l = add_pair(h, l, ref[i, 0], ref[i, 1])
        return h, l

    for c in to_x:
        c.wait_recv()
    h, l = sum_pairs(gx, nx)
    gz[z, 0] = h
    gz[z, 1] = l
    to_z = [send(gz.at[z], gz.at[z], (gz_send, gz_recv), i, (x * nz + z_peer(i), col)) for i in far_first]
    for n, d in enumerate(arrivals):
        if n == ny - 2:
            pass_power(d)
        forward[d].wait_recv()
        times_pair(d)
    turn_order = [ny, 0] + arrivals
    cut_at = (len(turn_order) + 1) // 2
    groups = [turn_order[:cut_at], turn_order[cut_at:]]

    def pair_of(d):
        return pairs - 1 if d == ny else y_peer(d)

    def sum_over_x(g):
        for n, d in enumerate(groups[g]):
            acc = tp[pair_of(d), x]
            for i in range(1, nx):
                t_x[d, i].wait_recv()
                acc = acc + xrecv[d, i]
            zsend[g][:, n] = acc.reshape(nz, *zsend[g].shape[2:])
        zrecv[g][0] = zsend[g][z]
        return [send(zsend[g].at[z_peer(j)], zrecv[g].at[j], (tz_send, tz_recv), (g, j), (x * nz + z_peer(j), col))
                for j in far_first]

    t_z = [sum_over_x(0)]
    for m in range(mats):
        pw[m] = six_right(jnp.transpose(pt[m]), 1)
    t_z.append(sum_over_x(1))

    for c in to_z:
        c.wait_recv()
    h, l = sum_pairs(gz, nz)
    ga[x, 0] = h
    ga[x, 1] = l
    to_a = [send(ga.at[x], ga.at[x], (ga_send, ga_recv), i, (x_peer(i) * nz + z, col)) for i in range(1, nx)]

    a_z, a_x = {}, []

    def pass_on(g, j):
        if j:
            a_z[g, j].wait_recv()
        p = tfull[g].at[x, z_peer(nz - j)] if j else tfull[g].at[x, z]
        for i in range(1, nx):
            a_x.append(send(p, p, (ax_send, ax_recv), (g, i, j), (x_peer(i) * nz + z, col)))

    for g in range(2):
        for c in t_z[g]:
            c.wait_recv()
        acc = zrecv[g][0]
        for j in range(1, nz):
            acc = acc + zrecv[g][j]
        tfull[g][x, z] = acc
        for j in far_first:
            a_z[g, j] = send(tfull[g].at[x, z], tfull[g].at[x, z], (az_send, az_recv), (g, j), (x * nz + z_peer(j), col))
        pass_on(g, 0)

    for c in to_a:
        c.wait_recv()
    for i in range(nx):
        mh[i * share : (i + 1) * share, :] = ga[i, 0]
        ml[i * share : (i + 1) * share, :] = ga[i, 1]
    near_first = far_first[::-1]
    near = near_first[:4]
    rest = near_first[4:]
    factor_pair(mh, ml, 0, 32)
    for j in near:
        pass_on(0, j)
    factor_pair(mh, ml, 32, 48)
    for j in rest:
        pass_on(0, j)
    factor_pair(mh, ml, 48, RANK)
    inverse = inverse_of(mh, ml)
    low = pltpu.roll(inverse[half:], 64, 1)
    first_lanes = lax.broadcasted_iota(jnp.int32, (half, 128), 1) < 64
    linv[own] = jnp.where(first_lanes, inverse[0:half], low)
    linv[last] = jnp.where(first_lanes, pltpu.roll(inverse[0:half], 64, 1), inverse[half:])
    spread = [send(linv.at[own], linv.at[own], (l_send, l_recv), i, (row, lax.rem(col + i, nc))) for i in range(1, nc)]
    for j in near_first:
        pass_on(1, j)
    for c in spread:
        c.wait_recv()
    inverses = {}
    for d in turn_order:
        for e in range(1 if d == ny else 2):
            packed = linv[2 * pair_of(d) + e]
            inverses[d, e] = six_left(jnp.concatenate([packed[:, 0:RANK], packed[:, RANK:]], axis=0))
    for c in a_x:
        c.wait_recv()

    squares = jnp.zeros((16, 128), F32)
    places = lax.broadcasted_iota(jnp.int32, (16, 256), 0)
    for g in range(2):
        for n, d in enumerate(groups[g]):
            sqs = []
            for e in range(2):
                if (d, e) not in inverses:
                    sqs.append(jnp.zeros((RANK, 256), F32))
                    continue
                at, to = e * RANK // depth, e * RANK % depth
                t = jnp.concatenate([tfull[g][h * nx // 2 + at, :, n].reshape(depth, 128)[to : to + RANK]
                                     for h in range(2)], axis=1)
                p = nn(inverses[d, e], six_right(t, 0))
                prod_out[2 * pair_of(d) + e] = p
                sqs.append(p * p)
            ones = jnp.where(places == pair_of(d), 1.0, 0.0).astype(BF16)
            both = jnp.concatenate(sqs, axis=0)
            high = both.astype(BF16)
            squares = squares + nt(ones, high) + nt(ones, (both - high.astype(F32)).astype(BF16))
    sq[col] = squares[0:8]
    to_all = [send(sq.at[col], sq.at[col], (sq_send, sq_recv), i, (row, lax.rem(col + i, nc))) for i in range(1, nc)]
    left = lax.broadcasted_iota(jnp.int32, (pw.shape[1], 3 * RANK), 1) < 2 * RANK
    for d, e in inverses:
        m = 2 * pair_of(d) + e
        q = nt(pw[m], jnp.concatenate([inverses[d, e]] * 3, axis=0))
        q1 = q.astype(BF16)
        pieces = jnp.where(left, q1.astype(F32), q - q1.astype(F32)).astype(BF16)
        q_out[m] = pieces
        m_out[m] = s_v[m] - nn(pieces, stacked_pieces(prod_out[m] * (1.0 - DECAY)))
    for c in to_all:
        c.wait_recv()
    squares = sq[0]
    for i in range(1, nc):
        squares = squares + sq[i]
    scale_out[...] = jnp.transpose(1.0 / jnp.sqrt(squares * (1.0 / ff) + EPSILON))
    load_weight.wait()
    finish()


def stacked_pieces(p):
    p1 = p.astype(BF16)
    p2 = (p - p1.astype(F32)).astype(BF16)
    return jnp.concatenate([p1, p2, p1], axis=0)


def update_kernel(gain, w, mom, q, prod, scale, new_weight, new_mom, new_right, w_v, r_v, w_sem, m_sem, r_sem):
    mats = w.shape[0]
    move = pltpu.make_async_copy(mom, new_mom, m_sem)
    move.start()
    table = scale[...]
    moves = [move]
    for m in range(mats):
        column = table[(m % 2) * RANK : (m % 2 + 1) * RANK, m // 2 : m // 2 + 1]
        normed = prod[m] * column
        r_v[m] = normed
        c = pltpu.make_async_copy(r_v.at[m], new_right.at[m], r_sem.at[m])
        c.start()
        moves.append(c)
        w_v[m] = w[m] - nn(q[m], stacked_pieces(normed * gain))
        c = pltpu.make_async_copy(w_v.at[m], new_weight.at[m], w_sem.at[m])
        c.start()
        moves.append(c)
    for c in moves:
        c.wait()


def body(nx, nz, ny, depth, weight, grad, momentum, right):
    nr, nc = nx * nz, ny * 2
    mats, rows, cols = weight.shape
    ff = cols * nc
    rt = jnp.transpose(right, (1, 2, 0))
    pairs = (mats + 1) // 2
    sizes = ((pairs + 1) // 2, pairs // 2)
    block = 256 // nx
    tile = block // nz
    share = RANK // nx
    vmem = pl.BlockSpec(memory_space=pltpu.VMEM)
    hbm = pl.BlockSpec(memory_space=pltpu.HBM)
    dma = pltpu.SemaphoreType.DMA
    half = RANK // 2
    w, mom, q, prod, scale = pl.pallas_call(
        functools.partial(exchange_kernel, nx, nz, ny),
        out_shape=(
            jax.ShapeDtypeStruct((mats, rows, cols), F32),
            jax.ShapeDtypeStruct((mats, rows, cols), F32),
            jax.ShapeDtypeStruct((mats, rows, 3 * RANK), BF16),
            jax.ShapeDtypeStruct((mats, RANK, cols), F32),
            jax.ShapeDtypeStruct((128, 8), F32),
        ),
        in_specs=[hbm] * 4,
        out_specs=(vmem,) * 5,
        scratch_shapes=[
            pltpu.VMEM((mats, rows, cols), F32),
            pltpu.VMEM((mats, rows, cols), BF16),
            pltpu.VMEM((mats, RANK, cols), F32),
            pltpu.VMEM((mats, RANK, rows), F32),
            pltpu.VMEM((ny + 1, RANK, rows), F32),
            pltpu.VMEM((ny, RANK + half, rows), F32),
            pltpu.VMEM((ny, RANK + half, rows), F32),
            pltpu.VMEM((mats, RANK, rows), F32),
            pltpu.VMEM((mats, rows, 6 * RANK), BF16),
            pltpu.VMEM((2, RANK, 128), F32),
            pltpu.VMEM((nx, 2, share, 128), F32),
            pltpu.VMEM((nz, 2, share, 128), F32),
            pltpu.VMEM((nx, 2, share, 128), F32),
            pltpu.VMEM((RANK, 128), F32),
            pltpu.VMEM((RANK, 128), F32),
            pltpu.VMEM((mats, half, 128), F32),
            pltpu.VMEM((pairs, nx, block, 128), F32),
            pltpu.VMEM((pairs, nx, block, 128), F32),
            [pltpu.VMEM((nz, n, tile, 128), F32) for n in sizes],
            [pltpu.VMEM((nz, n, tile, 128), F32) for n in sizes],
            [pltpu.VMEM((nx, nz, n, tile, 128), F32) for n in sizes],
            pltpu.VMEM((nc, 8, 128), F32),
            dma((2 * mats + 1,)),
            dma,
            dma((ny + 1,)), dma((ny + 1,)),
            dma((ny,)), dma((ny,)),
            dma((ny,)), dma((ny,)),
            dma((ny,)), dma((ny,)),
            dma((1,)), dma((1,)),
            dma((nx,)), dma((nx,)),
            dma((nz,)), dma((nz,)),
            dma((nx,)), dma((nx,)),
            dma((pairs, nx)), dma((pairs, nx)),
            dma((2, nz)), dma((2, nz)),
            dma((2, nz)), dma((2, nz)),
            dma((2, nx, nz)), dma((2, nx, nz)),
            dma((nc,)), dma((nc,)),
            dma((nc,)), dma((nc,)),
        ],
        compiler_params=pltpu.CompilerParams(
            collective_id=0, has_side_effects=True, vmem_limit_bytes=40 * 1024 * 1024
        ),
        name="exchange",
    )(*[pltpu.with_memory_space_constraint(v, pltpu.HBM) for v in (weight, grad, momentum, rt)])

    gain = math.sqrt(depth / ff)
    new_weight, new_momentum, new_right = pl.pallas_call(
        functools.partial(update_kernel, gain),
        out_shape=(
            jax.ShapeDtypeStruct(weight.shape, F32),
            jax.ShapeDtypeStruct(weight.shape, F32),
            jax.ShapeDtypeStruct((mats, RANK, cols), F32),
        ),
        in_specs=[vmem] * 5,
        out_specs=(hbm,) * 3,
        scratch_shapes=[
            pltpu.VMEM((mats, rows, cols), F32),
            pltpu.VMEM((mats, RANK, cols), F32),
            dma((mats,)),
            dma,
            dma((mats,)),
        ],
        compiler_params=pltpu.CompilerParams(vmem_limit_bytes=12 * 1024 * 1024),
        name="update",
    )(w, mom, q, prod, scale)
    return new_weight, new_momentum, jnp.transpose(new_right, (2, 0, 1))


def solution(mesh):
    nr, nc = mesh.shape["row"], mesh.shape["col"]
    nz = min(nr, 8)
    nx = nr // nz

    def run(weight, grad, momentum, right):
        return body(nx, nz, nc // 2, weight.shape[1] * nr, weight, grad, momentum, right)

    placed = P(None, "row", "col")
    return jax.shard_map(
        run,
        mesh=mesh,
        in_specs=(placed, placed, placed, P("col", None, None)),
        out_specs=(placed, placed, P("col", None, None)),
        check_vma=False,
    )
```

```python
import functools
import math

import jax
import jax.numpy as jnp
from jax import lax
from jax.experimental import pallas as pl
from jax.experimental.pallas import tpu as pltpu
from jax.sharding import PartitionSpec as P

MESH = pl.DeviceIdType.MESH
F32 = jnp.float32
BF16 = jnp.bfloat16

EPSILON = 1e-06
DECAY = 0.95
RANK = 64


def two_sum(a, b):
    s = a + b
    back = s - a
    return s, (a - (s - back)) + (b - back)


def split(a):
    t = a * 4097.0
    high = t - (t - a)
    return high, a - high


def two_prod(a, b):
    p = a * b
    ah, al = split(a)
    bh, bl = split(b)
    return p, ((ah * bh - p) + ah * bl + al * bh) + al * bl


def add_pair(ah, al, bh, bl):
    s, t = two_sum(ah, bh)
    t = t + (al + bl)
    h = s + t
    return h, t - (h - s)


def nt(a, b, precision=None):
    return lax.dot_general(a, b, (((1,), (1,)), ((), ())), precision=precision, preferred_element_type=F32)


def nn(a, b, precision=None):
    return lax.dot_general(a, b, (((1,), (0,)), ((), ())), precision=precision, preferred_element_type=F32)


def tn(a, b, precision=None):
    return lax.dot_general(a, b, (((0,), (0,)), ((), ())), precision=precision, preferred_element_type=F32)


def cut(a):
    a1 = a.astype(BF16)
    rest = a - a1.astype(F32)
    a2 = rest.astype(BF16)
    return a1, a2, (rest - a2.astype(F32)).astype(BF16)


def cut_product(dot, a, b):
    a1, a2, a3 = cut(a)
    b1, b2, b3 = cut(b)
    p = dot(jnp.concatenate([a1, a2, a3], axis=0), b1)
    q = dot(jnp.concatenate([a1, a2], axis=0), b2)
    r = dot(a1, b3)
    return p[0:RANK] + ((p[RANK : 2 * RANK] + q[0:RANK]) + (p[2 * RANK :] + q[RANK:] + r))


def six_left(a):
    a1, a2, a3 = cut(a)
    return jnp.concatenate([a1, a2, a1, a3, a2, a1], axis=1)


def six_right(a, axis):
    a1, a2, a3 = cut(a)
    return jnp.concatenate([a1, a1, a2, a1, a2, a3], axis=axis)


def round_int(v):
    magic = 1.5 * 2.0**23
    return (v + magic) - magic


def exact_gram(x):
    top = jnp.maximum(jnp.max(jnp.abs(x), axis=1, keepdims=True), 1e-18)
    top = jnp.broadcast_to(top, (RANK, 128))
    power = jnp.floor(jnp.log(top) * (1.0 / math.log(2.0))) + 1.0
    unit = jnp.exp2(power - 7.0).astype(BF16).astype(F32)
    inverse = jnp.exp2(7.0 - power).astype(BF16).astype(F32)
    y = x * inverse[:, 0:1]
    slices = []
    for i in range(4):
        q = round_int(y)
        slices.append(q.astype(BF16))
        y = (y - q) * 256.0
    q = jnp.concatenate(slices, axis=0)
    e = nt(q, q)
    low = [e[RANK * a : RANK * (a + 1), 0:128] for a in range(4)]
    high = [e[RANK * a : RANK * (a + 1), 128:256] for a in range(4)]
    levels = [low[0], low[1], low[2] + high[0], low[3] + high[1], high[2], high[3]]
    s, t = levels[0], jnp.zeros_like(levels[0])
    for i in range(1, 6):
        s, err = two_sum(s, levels[i] * (2.0 ** (-8 * i)))
        t = t + err
    s2 = pltpu.roll(s, 64, 1) * (1.0 / 256.0)
    t2 = pltpu.roll(t, 64, 1) * (1.0 / 256.0)
    gh, gl = add_pair(s, t, s2, t2)
    rows = lax.broadcasted_iota(jnp.int32, (RANK, 128), 0)
    lanes = lax.broadcasted_iota(jnp.int32, (RANK, 128), 1)
    across = jnp.sum(jnp.where(rows == lanes, unit, 0.0), axis=0, keepdims=True)
    return gh * unit * across, gl * unit * across


def mul_pair(ah, al, bh, bl):
    p, e = two_prod(ah, bh)
    return p, e + (ah * bl + al * bh)


def sub_pairs(h, l, m1, r1, m2, r2):
    p, q = mul_pair(*m1, *r1)
    s, e = two_sum(h, -p)
    p2, q2 = mul_pair(*m2, *r2)
    s, e2 = two_sum(s, -p2)
    e = (e + e2) + (l - (q + q2))
    h = s + e
    return h, e - (h - s)


def cross(a, b, c, d):
    p1, e1 = mul_pair(*a, *b)
    p2, e2 = mul_pair(*c, *d)
    return add_pair(p1, e1, -p2, -e2)


def factor_block(mh, ml, first):
    tiles = (RANK - first) // 8
    rows = lax.broadcasted_iota(jnp.int32, (8, 128), 0)
    lanes = lax.broadcasted_iota(jnp.int32, (8, 128), 1)
    half = jnp.where(lanes >= 64, 64, 0)
    column = lanes - half
    m = [(mh[first + 8 * t : first + 8 * t + 8, :], ml[first + 8 * t : first + 8 * t + 8, :]) for t in range(tiles)]

    def row(v, i):
        return tuple(jnp.broadcast_to(part[i : i + 1], (8, 128)) for part in v)

    def masked(mask, v):
        return tuple(jnp.where(mask, part, 0.0) for part in v)

    own = [tuple(jnp.take_along_axis(part, half + (first + j), axis=1) for part in m[0]) for j in range(8)]
    steps = []
    for i in range(0, 8, 2):
        k = first + i
        c1, c2 = own[i], own[i + 1]
        a, b, c = row(c1, i), row(c2, i), row(c2, i + 1)
        dh, dl = cross(a, c, b, b)
        inv = 1.0 / dh
        p, e = two_prod(dh, inv)
        inv = (inv, inv * (((1.0 - p) - e) - dl * inv))
        later = rows > i + 1
        n1 = masked(later, mul_pair(*cross(c1, c, c2, b), *inv))
        n2 = masked(later, mul_pair(*cross(c2, a, c1, b), *inv))
        for j in range(i + 2, 8):
            own[j] = sub_pairs(*own[j], n1, row(own[j], i), n2, row(own[j], i + 1))
        r1, r2 = row(m[0], i), row(m[0], i + 1)
        w1 = mul_pair(*cross(r1, c, r2, b), *inv)
        w2 = mul_pair(*cross(r2, a, r1, b), *inv)
        here1, here2 = column == k, column == k + 1
        here = here1 | here2
        r1 = (jnp.where(here1, 1.0, jnp.where(here2, 0.0, r1[0])), jnp.where(here, 0.0, r1[1]))
        r2 = (jnp.where(here2, 1.0, jnp.where(here1, 0.0, r2[0])), jnp.where(here, 0.0, r2[1]))
        m[0] = sub_pairs(*masked(jnp.logical_not(here & later), m[0]), n1, r1, n2, r2)
        steps.append((here, w1, w2, r1, r2))
    for t in range(1, tiles):
        index = half + (rows + (first + 8 * t))

        def spread(v):
            return tuple(jnp.take_along_axis(part, index, axis=1) for part in v)

        for here, w1, w2, r1, r2 in steps:
            m[t] = sub_pairs(*masked(jnp.logical_not(here), m[t]), spread(w1), r1, spread(w2), r2)
    for t in range(tiles):
        mh[first + 8 * t : first + 8 * t + 8, :] = m[t][0]
        ml[first + 8 * t : first + 8 * t + 8, :] = m[t][1]


def factor_pair(mh, ml, begin, end):
    for first in range(begin, end, 8):
        factor_block(mh, ml, first)


def inverse_of(mh, ml):
    m = mh[...]
    rows = lax.broadcasted_iota(jnp.int32, (RANK, 128), 0)
    lanes = lax.broadcasted_iota(jnp.int32, (RANK, 128), 1)
    left = lanes < 64
    column = jnp.where(left, lanes, lanes - 64)
    odd = (rows & 1) == 1

    def pick(v, mask):
        v = jnp.where(mask, v, 0.0)
        a = jnp.sum(jnp.where(left, v, 0.0), axis=1, keepdims=True)
        b = jnp.sum(jnp.where(left, 0.0, v), axis=1, keepdims=True)
        return jnp.where(left, a, b)

    same, next_to = column == rows, column == (rows ^ 1)
    ch, cl = pick(m, same), pick(ml[...], same)
    bh, bl = pick(m, next_to), pick(ml[...], next_to)
    ah, al = pltpu.roll(ch, 1, 0), pltpu.roll(cl, 1, 0)
    inv = 1.0 / ah
    p, e = two_prod(ah, inv)
    rh, rl = mul_pair(bh, bl, inv, inv * (((1.0 - p) - e) - al * inv))
    p, e = mul_pair(rh, rl, bh, bl)
    ph, _ = add_pair(ch, cl, -p, -e)
    root = 1.0 / jnp.sqrt(jnp.where(odd, ph, ch))
    ratio = jnp.where(odd, rh, 0.0)
    unit = jnp.where(column < rows - (rows & 1), m, jnp.where(column == rows, 1.0, 0.0))
    return (unit - ratio * pltpu.roll(unit, 1, 0)) * root


def exchange_kernel(nx, nz, ny, weight, grad, mom, right, w_out, m_out, q_out, prod_out, scale_out, s_v, g_v, r_v, part,
                    mate, ysend, yrecv, pt, pw, gp, gx, gz, ga, mh, ml, linv, tp, xrecv, zsend, zrecv, tfull, sq, load_sem,
                    w_sem, mate_send, mate_recv, y_send, y_recv, ag_send, ag_recv, fw_send, fw_recv, h_send, h_recv,
                    gx_send, gx_recv, gz_send, gz_recv, ga_send, ga_recv, tx_send, tx_recv, tz_send, tz_recv, az_send,
                    az_recv, ax_send, ax_recv, l_send, l_recv, sq_send, sq_recv):
    nr, nc = nx * nz, ny * 2
    mats = nc + 1
    last = mats - 1
    ff = 256 * nc
    row, col = lax.axis_index("row"), lax.axis_index("col")
    x, z = row // nz, row % nz
    y, k = col // 2, col % 2
    mate_id = (row, y * 2 + (1 - k))
    half = RANK // 2

    pending = []

    def finish():
        for c in pending:
            c.wait_send()

    def send(src, dst, sems, index, target):
        c = pltpu.make_async_remote_copy(src_ref=src, dst_ref=dst, send_sem=sems[0].at[index], recv_sem=sems[1].at[index],
                                         device_id=target, device_id_type=MESH)
        c.start()
        pending.append(c)
        return c

    def x_peer(i):
        return lax.rem(x + i, nx)

    def z_peer(i):
        return lax.rem(z + i, nz)

    def y_peer(i):
        return lax.rem(y + i, ny)

    far_first = sorted(range(1, nz), key=lambda i: -min(i, nz - i))

    barrier = pltpu.get_barrier_semaphore()
    peers = [(x * nz + z_peer(i), col) for i in far_first]
    peers += [(row, lax.rem(col + i, nc)) for i in range(1, nc)]
    peers += [(x_peer(i) * nz + z, col) for i in range(1, nx)]
    for peer in peers:
        pl.semaphore_signal(barrier, inc=1, device_id=peer, device_id_type=MESH)
    load_right = pltpu.make_async_copy(right, r_v, load_sem.at[2 * mats])
    load_right.start()

    def loads(m):
        return (pltpu.make_async_copy(mom.at[m], s_v.at[m], load_sem.at[m]),
                pltpu.make_async_copy(grad.at[m], g_v.at[m], load_sem.at[mats + m]))

    turns = list(range(1, ny)) + [0]
    for m in [2 * y_peer(i) + (1 - k) for i in turns] + [last] + [2 * y_peer(i) + k for i in turns]:
        for c in loads(m):
            c.start()

    load_right.wait()

    def power(m):
        for c in loads(m):
            c.wait()
        s = s_v[m] + g_v[m].astype(F32)
        s_v[m] = s
        part[m] = cut_product(nt, r_v[m], s)

    to_mate = {}
    mate_sems = (mate_send, mate_recv)
    for n, i in enumerate(turns):
        m = 2 * y_peer(i) + (1 - k)
        power(m)
    power(last)
    pl.semaphore_wait(barrier, len(peers))
    for i in turns:
        to_mate[i] = send(part.at[2 * y_peer(i) + (1 - k)], mate.at[i], mate_sems, i, mate_id)
    other_rows = pl.ds(pl.multiple_of((1 - k) * half, half), half)
    my_rows = pl.ds(pl.multiple_of(k * half, half), half)
    to_mate[ny] = send(part.at[last, other_rows], mate.at[ny, pl.ds(0, half)], mate_sems, ny, mate_id)
    load_weight = pltpu.make_async_copy(weight, w_out, w_sem)
    load_weight.start()

    own = 2 * y + k
    to_y = []
    for n, i in enumerate(turns):
        yd = y_peer(i)
        power(2 * yd + k)
        if n == 0:
            to_mate[ny].wait_recv()
            shared = part[last, my_rows, :] + mate[ny, 0:half, :]
        to_mate[i].wait_recv()
        if i == 0:
            yrecv[y, 0:RANK, :] = part[own] + mate[0]
            yrecv[y, RANK:, :] = shared
        else:
            ysend[i, 0:RANK, :] = part[2 * yd + k] + mate[i]
            ysend[i, RANK:, :] = shared
            to_y.append(send(ysend.at[i], yrecv.at[y], (y_send, y_recv), i, (row, 2 * yd + k)))
    for c in to_y:
        c.wait_recv()
    total = yrecv[0]
    for i in range(1, ny):
        total = total + yrecv[i]
    pt[last, my_rows, :] = total[RANK:]
    swap = send(pt.at[last, my_rows], pt.at[last, my_rows], (h_send, h_recv), 0, mate_id)
    pt[own] = total[0:RANK]
    gather = [send(pt.at[own], pt.at[own], (ag_send, ag_recv), i, (row, 2 * y_peer(i) + k)) for i in range(1, ny)]
    forward = {0: send(pt.at[own], pt.at[own], (fw_send, fw_recv), 0, mate_id)}

    lanes = lax.broadcasted_iota(jnp.int32, (RANK, 128), 1)
    ah, al = exact_gram(total[0:RANK])
    swap.wait_recv()
    bh, bl = exact_gram(pt[last])
    gp[0] = jnp.where(lanes < 64, ah, pltpu.roll(bh, 64, 1))
    gp[1] = jnp.where(lanes < 64, al, pltpu.roll(bl, 64, 1))
    share = RANK // nx

    def rows_of(d):
        return pl.ds(pl.multiple_of(d * share, share), share)

    to_x = [send(gp.at[:, rows_of(x_peer(i))], gx.at[x], (gx_send, gx_recv), i, (x_peer(i) * nz + z, col))
            for i in range(1, nx)]
    gx[x] = gp[:, rows_of(x), :]

    pairs = tp.shape[0]
    depth = tp.shape[2]
    t_x = {}

    def times(m, q, e):
        t = cut_product(nn, pt[m], s_v[m])
        at, to = e * RANK // depth, e * RANK % depth
        for h in range(2):
            tp[q, h * nx // 2 + at, to : to + RANK, :] = t[:, h * 128 : (h + 1) * 128]

    def block_out(turn, q):
        for i in range(1, nx):
            t_x[turn, i] = send(tp.at[q, x_peer(i)], xrecv.at[turn, i], (tx_send, tx_recv), (turn, i),
                                (x_peer(i) * nz + z, col))

    def times_pair(d):
        q = y_peer(d)
        times(2 * q, q, 0)
        times(2 * q + 1, q, 1)
        block_out(d, q)

    arrivals = sorted(range(1, ny), key=lambda d: min(d, ny - d))

    def pass_power(d):
        gather[ny - d - 1].wait_recv()
        m = 2 * y_peer(d) + k
        forward[d] = send(pt.at[m], pt.at[m], (fw_send, fw_recv), d, mate_id)

    at, to = RANK // depth, RANK % depth
    for h in range(2):
        tp[pairs - 1, h * nx // 2 + at, to : to + RANK, :] = jnp.zeros((RANK, 128), F32)
    times(last, pairs - 1, 0)
    block_out(ny, pairs - 1)
    forward[0].wait_recv()
    times_pair(0)
    for d in arrivals:
        pass_power(d)
    forward[arrivals[0]].wait_recv()
    times_pair(arrivals[0])

    def sum_pairs(ref, n):
        h, l = ref[0, 0], ref[0, 1]
        for i in range(1, n):
            h, l = add_pair(h, l, ref[i, 0], ref[i, 1])
        return h, l

    for c in to_x:
        c.wait_recv()
    h, l = sum_pairs(gx, nx)
    gz[z, 0] = h
    gz[z, 1] = l
    to_z = [send(gz.at[z], gz.at[z], (gz_send, gz_recv), i, (x * nz + z_peer(i), col)) for i in far_first]
    for d in arrivals[1:]:
        forward[d].wait_recv()
        times_pair(d)
    turn_order = [ny, 0] + arrivals
    cut_at = (len(turn_order) + 1) // 2
    groups = [turn_order[:cut_at], turn_order[cut_at:]]

    def pair_of(d):
        return pairs - 1 if d == ny else y_peer(d)

    def sum_over_x(g):
        for n, d in enumerate(groups[g]):
            acc = tp[pair_of(d), x]
            for i in range(1, nx):
                t_x[d, i].wait_recv()
                acc = acc + xrecv[d, i]
            zsend[g][:, n] = acc.reshape(nz, *zsend[g].shape[2:])
        zrecv[g][0] = zsend[g][z]
        return [send(zsend[g].at[z_peer(j)], zrecv[g].at[j], (tz_send, tz_recv), (g, j), (x * nz + z_peer(j), col))
                for j in far_first]

    t_z = [sum_over_x(0)]
    for m in range(mats):
        pw[m] = six_right(jnp.transpose(pt[m]), 1)
    t_z.append(sum_over_x(1))

    for c in to_z:
        c.wait_recv()
    h, l = sum_pairs(gz, nz)
    ga[x, 0] = h
    ga[x, 1] = l
    to_a = [send(ga.at[x], ga.at[x], (ga_send, ga_recv), i, (x_peer(i) * nz + z, col)) for i in range(1, nx)]

    a_z, a_x = {}, ([], [])

    def pass_on(g, j):
        if j:
            a_z[g, j].wait_recv()
        p = tfull[g].at[x, z_peer(nz - j)] if j else tfull[g].at[x, z]
        for i in range(1, nx):
            a_x[g].append(send(p, p, (ax_send, ax_recv), (g, i, j), (x_peer(i) * nz + z, col)))

    for g in range(2):
        for c in t_z[g]:
            c.wait_recv()
        acc = zrecv[g][0]
        for j in range(1, nz):
            acc = acc + zrecv[g][j]
        tfull[g][x, z] = acc
        for j in far_first:
            a_z[g, j] = send(tfull[g].at[x, z], tfull[g].at[x, z], (az_send, az_recv), (g, j), (x * nz + z_peer(j), col))
        pass_on(g, 0)

    for c in to_a:
        c.wait_recv()
    for i in range(nx):
        mh[i * share : (i + 1) * share, :] = ga[i, 0]
        ml[i * share : (i + 1) * share, :] = ga[i, 1]
    near_first = far_first[::-1]
    near = near_first[:4]
    rest = near_first[4:]
    factor_pair(mh, ml, 0, 32)
    for j in near:
        pass_on(0, j)
    factor_pair(mh, ml, 32, 48)
    for j in rest:
        pass_on(0, j)
    factor_pair(mh, ml, 48, RANK)
    inverse = inverse_of(mh, ml)
    low = pltpu.roll(inverse[half:], 64, 1)
    first_lanes = lax.broadcasted_iota(jnp.int32, (half, 128), 1) < 64
    linv[own] = jnp.where(first_lanes, inverse[0:half], low)
    linv[last] = jnp.where(first_lanes, pltpu.roll(inverse[0:half], 64, 1), inverse[half:])
    spread = [send(linv.at[own], linv.at[own], (l_send, l_recv), i, (row, lax.rem(col + i, nc))) for i in range(1, nc)]
    for j in near_first:
        pass_on(1, j)
    for c in spread:
        c.wait_recv()
    inverses = {}
    for d in turn_order:
        for e in range(1 if d == ny else 2):
            packed = linv[2 * pair_of(d) + e]
            inverses[d, e] = six_left(jnp.concatenate([packed[:, 0:RANK], packed[:, RANK:]], axis=0))
    squares = jnp.zeros((16, 128), F32)
    places = lax.broadcasted_iota(jnp.int32, (16, 256), 0)
    for g in range(2):
        for c in a_x[g]:
            c.wait_recv()
        for n, d in enumerate(groups[g]):
            sqs = []
            for e in range(2):
                if (d, e) not in inverses:
                    sqs.append(jnp.zeros((RANK, 256), F32))
                    continue
                at, to = e * RANK // depth, e * RANK % depth
                t = jnp.concatenate([tfull[g][h * nx // 2 + at, :, n].reshape(depth, 128)[to : to + RANK]
                                     for h in range(2)], axis=1)
                p = nn(inverses[d, e], six_right(t, 0))
                prod_out[2 * pair_of(d) + e] = p
                sqs.append(p * p)
            ones = jnp.where(places == pair_of(d), 1.0, 0.0).astype(BF16)
            both = jnp.concatenate(sqs, axis=0)
            high = both.astype(BF16)
            squares = squares + nt(ones, high) + nt(ones, (both - high.astype(F32)).astype(BF16))
    sq[col] = squares[0:8]
    to_all = [send(sq.at[col], sq.at[col], (sq_send, sq_recv), i, (row, lax.rem(col + i, nc))) for i in range(1, nc)]
    left = lax.broadcasted_iota(jnp.int32, (pw.shape[1], 3 * RANK), 1) < 2 * RANK
    for d, e in inverses:
        m = 2 * pair_of(d) + e
        q = nt(pw[m], jnp.concatenate([inverses[d, e]] * 3, axis=0))
        q1 = q.astype(BF16)
        pieces = jnp.where(left, q1.astype(F32), q - q1.astype(F32)).astype(BF16)
        q_out[m] = pieces
        m_out[m] = s_v[m] - nn(pieces, stacked_pieces(prod_out[m] * (1.0 - DECAY)))
    for c in to_all:
        c.wait_recv()
    squares = sq[0]
    for i in range(1, nc):
        squares = squares + sq[i]
    scale_out[...] = jnp.transpose(1.0 / jnp.sqrt(squares * (1.0 / ff) + EPSILON))
    load_weight.wait()
    finish()


def stacked_pieces(p):
    p1 = p.astype(BF16)
    p2 = (p - p1.astype(F32)).astype(BF16)
    return jnp.concatenate([p1, p2, p1], axis=0)


def update_kernel(gain, w, mom, q, prod, scale, new_weight, new_mom, new_right, w_v, r_v, w_sem, m_sem, r_sem):
    mats = w.shape[0]
    move = pltpu.make_async_copy(mom, new_mom, m_sem)
    move.start()
    table = scale[...]
    moves = [move]
    for m in range(mats):
        column = table[(m % 2) * RANK : (m % 2 + 1) * RANK, m // 2 : m // 2 + 1]
        normed = prod[m] * column
        r_v[m] = normed
        c = pltpu.make_async_copy(r_v.at[m], new_right.at[m], r_sem.at[m])
        c.start()
        moves.append(c)
        w_v[m] = w[m] - nn(q[m], stacked_pieces(normed * gain))
        c = pltpu.make_async_copy(w_v.at[m], new_weight.at[m], w_sem.at[m])
        c.start()
        moves.append(c)
    for c in moves:
        c.wait()


def body(nx, nz, ny, depth, weight, grad, momentum, right):
    nr, nc = nx * nz, ny * 2
    mats, rows, cols = weight.shape
    ff = cols * nc
    rt = jnp.transpose(right, (1, 2, 0))
    pairs = (mats + 1) // 2
    sizes = ((pairs + 1) // 2, pairs // 2)
    block = 256 // nx
    tile = block // nz
    share = RANK // nx
    vmem = pl.BlockSpec(memory_space=pltpu.VMEM)
    hbm = pl.BlockSpec(memory_space=pltpu.HBM)
    dma = pltpu.SemaphoreType.DMA
    half = RANK // 2
    w, mom, q, prod, scale = pl.pallas_call(
        functools.partial(exchange_kernel, nx, nz, ny),
        out_shape=(
            jax.ShapeDtypeStruct((mats, rows, cols), F32),
            jax.ShapeDtypeStruct((mats, rows, cols), F32),
            jax.ShapeDtypeStruct((mats, rows, 3 * RANK), BF16),
            jax.ShapeDtypeStruct((mats, RANK, cols), F32),
            jax.ShapeDtypeStruct((128, 8), F32),
        ),
        in_specs=[hbm] * 4,
        out_specs=(vmem,) * 5,
        scratch_shapes=[
            pltpu.VMEM((mats, rows, cols), F32),
            pltpu.VMEM((mats, rows, cols), BF16),
            pltpu.VMEM((mats, RANK, cols), F32),
            pltpu.VMEM((mats, RANK, rows), F32),
            pltpu.VMEM((ny + 1, RANK, rows), F32),
            pltpu.VMEM((ny, RANK + half, rows), F32),
            pltpu.VMEM((ny, RANK + half, rows), F32),
            pltpu.VMEM((mats, RANK, rows), F32),
            pltpu.VMEM((mats, rows, 6 * RANK), BF16),
            pltpu.VMEM((2, RANK, 128), F32),
            pltpu.VMEM((nx, 2, share, 128), F32),
            pltpu.VMEM((nz, 2, share, 128), F32),
            pltpu.VMEM((nx, 2, share, 128), F32),
            pltpu.VMEM((RANK, 128), F32),
            pltpu.VMEM((RANK, 128), F32),
            pltpu.VMEM((mats, half, 128), F32),
            pltpu.VMEM((pairs, nx, block, 128), F32),
            pltpu.VMEM((pairs, nx, block, 128), F32),
            [pltpu.VMEM((nz, n, tile, 128), F32) for n in sizes],
            [pltpu.VMEM((nz, n, tile, 128), F32) for n in sizes],
            [pltpu.VMEM((nx, nz, n, tile, 128), F32) for n in sizes],
            pltpu.VMEM((nc, 8, 128), F32),
            dma((2 * mats + 1,)),
            dma,
            dma((ny + 1,)), dma((ny + 1,)),
            dma((ny,)), dma((ny,)),
            dma((ny,)), dma((ny,)),
            dma((ny,)), dma((ny,)),
            dma((1,)), dma((1,)),
            dma((nx,)), dma((nx,)),
            dma((nz,)), dma((nz,)),
            dma((nx,)), dma((nx,)),
            dma((pairs, nx)), dma((pairs, nx)),
            dma((2, nz)), dma((2, nz)),
            dma((2, nz)), dma((2, nz)),
            dma((2, nx, nz)), dma((2, nx, nz)),
            dma((nc,)), dma((nc,)),
            dma((nc,)), dma((nc,)),
        ],
        compiler_params=pltpu.CompilerParams(
            collective_id=0, has_side_effects=True, vmem_limit_bytes=40 * 1024 * 1024
        ),
        name="exchange",
    )(*[pltpu.with_memory_space_constraint(v, pltpu.HBM) for v in (weight, grad, momentum, rt)])

    gain = math.sqrt(depth / ff)
    new_weight, new_momentum, new_right = pl.pallas_call(
        functools.partial(update_kernel, gain),
        out_shape=(
            jax.ShapeDtypeStruct(weight.shape, F32),
            jax.ShapeDtypeStruct(weight.shape, F32),
            jax.ShapeDtypeStruct((mats, RANK, cols), F32),
        ),
        in_specs=[vmem] * 5,
        out_specs=(hbm,) * 3,
        scratch_shapes=[
            pltpu.VMEM((mats, rows, cols), F32),
            pltpu.VMEM((mats, RANK, cols), F32),
            dma((mats,)),
            dma,
            dma((mats,)),
        ],
        compiler_params=pltpu.CompilerParams(vmem_limit_bytes=12 * 1024 * 1024),
        name="update",
    )(w, mom, q, prod, scale)
    return new_weight, new_momentum, jnp.transpose(new_right, (2, 0, 1))


def solution(mesh):
    nr, nc = mesh.shape["row"], mesh.shape["col"]
    nz = min(nr, 8)
    nx = nr // nz

    def run(weight, grad, momentum, right):
        return body(nx, nz, nc // 2, weight.shape[1] * nr, weight, grad, momentum, right)

    placed = P(None, "row", "col")
    return jax.shard_map(
        run,
        mesh=mesh,
        in_specs=(placed, placed, placed, P("col", None, None)),
        out_specs=(placed, placed, P("col", None, None)),
        check_vma=False,
    )
```

```python
import functools
import math

import jax
import jax.numpy as jnp
from jax import lax
from jax.experimental import pallas as pl
from jax.experimental.pallas import tpu as pltpu
from jax.sharding import PartitionSpec as P

MESH = pl.DeviceIdType.MESH
F32 = jnp.float32
BF16 = jnp.bfloat16

EPSILON = 1e-06
DECAY = 0.95
RANK = 64


def two_sum(a, b):
    s = a + b
    back = s - a
    return s, (a - (s - back)) + (b - back)


def split(a):
    t = a * 4097.0
    high = t - (t - a)
    return high, a - high


def two_prod(a, b):
    p = a * b
    ah, al = split(a)
    bh, bl = split(b)
    return p, ((ah * bh - p) + ah * bl + al * bh) + al * bl


def add_pair(ah, al, bh, bl):
    s, t = two_sum(ah, bh)
    t = t + (al + bl)
    h = s + t
    return h, t - (h - s)


def nt(a, b, precision=None):
    return lax.dot_general(a, b, (((1,), (1,)), ((), ())), precision=precision, preferred_element_type=F32)


def nn(a, b, precision=None):
    return lax.dot_general(a, b, (((1,), (0,)), ((), ())), precision=precision, preferred_element_type=F32)


def tn(a, b, precision=None):
    return lax.dot_general(a, b, (((0,), (0,)), ((), ())), precision=precision, preferred_element_type=F32)


def cut(a):
    a1 = a.astype(BF16)
    rest = a - a1.astype(F32)
    a2 = rest.astype(BF16)
    return a1, a2, (rest - a2.astype(F32)).astype(BF16)


def cut_product(dot, a, b):
    a1, a2, a3 = cut(a)
    b1, b2, b3 = cut(b)
    p = dot(jnp.concatenate([a1, a2, a3], axis=0), b1)
    q = dot(jnp.concatenate([a1, a2], axis=0), b2)
    r = dot(a1, b3)
    return p[0:RANK] + ((p[RANK : 2 * RANK] + q[0:RANK]) + (p[2 * RANK :] + q[RANK:] + r))


def six_left(a):
    a1, a2, a3 = cut(a)
    return jnp.concatenate([a1, a2, a1, a3, a2, a1], axis=1)


def six_right(a, axis):
    a1, a2, a3 = cut(a)
    return jnp.concatenate([a1, a1, a2, a1, a2, a3], axis=axis)


def round_int(v):
    magic = 1.5 * 2.0**23
    return (v + magic) - magic


def exact_gram(x):
    top = jnp.maximum(jnp.max(jnp.abs(x), axis=1, keepdims=True), 1e-18)
    top = jnp.broadcast_to(top, (RANK, 128))
    power = jnp.floor(jnp.log(top) * (1.0 / math.log(2.0))) + 1.0
    unit = jnp.exp2(power - 7.0).astype(BF16).astype(F32)
    inverse = jnp.exp2(7.0 - power).astype(BF16).astype(F32)
    y = x * inverse[:, 0:1]
    slices = []
    for i in range(4):
        q = round_int(y)
        slices.append(q.astype(BF16))
        y = (y - q) * 256.0
    q = jnp.concatenate(slices, axis=0)
    e = nt(q, q)
    low = [e[RANK * a : RANK * (a + 1), 0:128] for a in range(4)]
    high = [e[RANK * a : RANK * (a + 1), 128:256] for a in range(4)]
    levels = [low[0], low[1], low[2] + high[0], low[3] + high[1], high[2], high[3]]
    s, t = levels[0], jnp.zeros_like(levels[0])
    for i in range(1, 6):
        s, err = two_sum(s, levels[i] * (2.0 ** (-8 * i)))
        t = t + err
    s2 = pltpu.roll(s, 64, 1) * (1.0 / 256.0)
    t2 = pltpu.roll(t, 64, 1) * (1.0 / 256.0)
    gh, gl = add_pair(s, t, s2, t2)
    rows = lax.broadcasted_iota(jnp.int32, (RANK, 128), 0)
    lanes = lax.broadcasted_iota(jnp.int32, (RANK, 128), 1)
    across = jnp.sum(jnp.where(rows == lanes, unit, 0.0), axis=0, keepdims=True)
    return gh * unit * across, gl * unit * across


def mul_pair(ah, al, bh, bl):
    p, e = two_prod(ah, bh)
    return p, e + (ah * bl + al * bh)


def sub_pairs(h, l, m1, r1, m2, r2):
    p, q = mul_pair(*m1, *r1)
    s, e = two_sum(h, -p)
    p2, q2 = mul_pair(*m2, *r2)
    s, e2 = two_sum(s, -p2)
    e = (e + e2) + (l - (q + q2))
    h = s + e
    return h, e - (h - s)


def cross(a, b, c, d):
    p1, e1 = mul_pair(*a, *b)
    p2, e2 = mul_pair(*c, *d)
    return add_pair(p1, e1, -p2, -e2)


def factor_block(mh, ml, first):
    tiles = (RANK - first) // 8
    rows = lax.broadcasted_iota(jnp.int32, (8, 128), 0)
    lanes = lax.broadcasted_iota(jnp.int32, (8, 128), 1)
    half = jnp.where(lanes >= 64, 64, 0)
    column = lanes - half
    m = [(mh[first + 8 * t : first + 8 * t + 8, :], ml[first + 8 * t : first + 8 * t + 8, :]) for t in range(tiles)]

    def row(v, i):
        return tuple(jnp.broadcast_to(part[i : i + 1], (8, 128)) for part in v)

    def masked(mask, v):
        return tuple(jnp.where(mask, part, 0.0) for part in v)

    own = [tuple(jnp.take_along_axis(part, half + (first + j), axis=1) for part in m[0]) for j in range(8)]
    steps = []
    for i in range(0, 8, 2):
        k = first + i
        c1, c2 = own[i], own[i + 1]
        a, b, c = row(c1, i), row(c2, i), row(c2, i + 1)
        dh, dl = cross(a, c, b, b)
        inv = 1.0 / dh
        p, e = two_prod(dh, inv)
        inv = (inv, inv * (((1.0 - p) - e) - dl * inv))
        later = rows > i + 1
        n1 = masked(later, mul_pair(*cross(c1, c, c2, b), *inv))
        n2 = masked(later, mul_pair(*cross(c2, a, c1, b), *inv))
        for j in range(i + 2, 8):
            own[j] = sub_pairs(*own[j], n1, row(own[j], i), n2, row(own[j], i + 1))
        r1, r2 = row(m[0], i), row(m[0], i + 1)
        w1 = mul_pair(*cross(r1, c, r2, b), *inv)
        w2 = mul_pair(*cross(r2, a, r1, b), *inv)
        here1, here2 = column == k, column == k + 1
        here = here1 | here2
        r1 = (jnp.where(here1, 1.0, jnp.where(here2, 0.0, r1[0])), jnp.where(here, 0.0, r1[1]))
        r2 = (jnp.where(here2, 1.0, jnp.where(here1, 0.0, r2[0])), jnp.where(here, 0.0, r2[1]))
        m[0] = sub_pairs(*masked(jnp.logical_not(here & later), m[0]), n1, r1, n2, r2)
        steps.append((here, w1, w2, r1, r2))
    for t in range(1, tiles):
        index = half + (rows + (first + 8 * t))

        def spread(v):
            return tuple(jnp.take_along_axis(part, index, axis=1) for part in v)

        for here, w1, w2, r1, r2 in steps:
            m[t] = sub_pairs(*masked(jnp.logical_not(here), m[t]), spread(w1), r1, spread(w2), r2)
    for t in range(tiles):
        mh[first + 8 * t : first + 8 * t + 8, :] = m[t][0]
        ml[first + 8 * t : first + 8 * t + 8, :] = m[t][1]


def factor_pair(mh, ml, begin, end):
    for first in range(begin, end, 8):
        factor_block(mh, ml, first)


def inverse_of(mh, ml):
    m = mh[...]
    rows = lax.broadcasted_iota(jnp.int32, (RANK, 128), 0)
    lanes = lax.broadcasted_iota(jnp.int32, (RANK, 128), 1)
    left = lanes < 64
    column = jnp.where(left, lanes, lanes - 64)
    odd = (rows & 1) == 1

    def pick(v, mask):
        v = jnp.where(mask, v, 0.0)
        a = jnp.sum(jnp.where(left, v, 0.0), axis=1, keepdims=True)
        b = jnp.sum(jnp.where(left, 0.0, v), axis=1, keepdims=True)
        return jnp.where(left, a, b)

    same, next_to = column == rows, column == (rows ^ 1)
    ch, cl = pick(m, same), pick(ml[...], same)
    bh, bl = pick(m, next_to), pick(ml[...], next_to)
    ah, al = pltpu.roll(ch, 1, 0), pltpu.roll(cl, 1, 0)
    inv = 1.0 / ah
    p, e = two_prod(ah, inv)
    rh, rl = mul_pair(bh, bl, inv, inv * (((1.0 - p) - e) - al * inv))
    p, e = mul_pair(rh, rl, bh, bl)
    ph, _ = add_pair(ch, cl, -p, -e)
    root = 1.0 / jnp.sqrt(jnp.where(odd, ph, ch))
    ratio = jnp.where(odd, rh, 0.0)
    unit = jnp.where(column < rows - (rows & 1), m, jnp.where(column == rows, 1.0, 0.0))
    return (unit - ratio * pltpu.roll(unit, 1, 0)) * root


def exchange_kernel(nx, nz, ny, weight, grad, mom, right, w_out, m_out, q_out, prod_out, scale_out, s_v, g_v, r_v, part,
                    mate, ysend, yrecv, pt, pw, gp, gx, gz, ga, mh, ml, linv, tp, xrecv, zsend, zrecv, tfull, sq, load_sem,
                    w_sem, mate_send, mate_recv, y_send, y_recv, ag_send, ag_recv, fw_send, fw_recv, h_send, h_recv,
                    gx_send, gx_recv, gz_send, gz_recv, ga_send, ga_recv, tx_send, tx_recv, tz_send, tz_recv, az_send,
                    az_recv, ax_send, ax_recv, l_send, l_recv, sq_send, sq_recv, near_sem, far_sem):
    nr, nc = nx * nz, ny * 2
    mats = nc + 1
    last = mats - 1
    ff = 256 * nc
    row, col = lax.axis_index("row"), lax.axis_index("col")
    x, z = row // nz, row % nz
    y, k = col // 2, col % 2
    mate_id = (row, y * 2 + (1 - k))
    half = RANK // 2

    pending = []

    def finish():
        for c in pending:
            c.wait_send()

    def send(src, dst, sems, index, target):
        c = pltpu.make_async_remote_copy(src_ref=src, dst_ref=dst, send_sem=sems[0].at[index], recv_sem=sems[1].at[index],
                                         device_id=target, device_id_type=MESH)
        c.start()
        pending.append(c)
        return c

    def x_peer(i):
        return lax.rem(x + i, nx)

    def z_peer(i):
        return lax.rem(z + i, nz)

    def y_peer(i):
        return lax.rem(y + i, ny)

    far_first = sorted(range(1, nz), key=lambda i: -min(i, nz - i))

    barrier = pltpu.get_barrier_semaphore()
    along_z = [(x * nz + z_peer(i), col) for i in (1, nz - 1)]
    along_x = [(x_peer(i) * nz + z, col) for i in (1, nx - 1)]
    two_off = [(x * nz + z_peer(i), col) for i in (2, nz - 2)]
    peers = along_z + along_x + [(row, lax.rem(col + i, nc)) for i in range(1, nc)]
    for peer in peers:
        pl.semaphore_signal(barrier, inc=1, device_id=peer, device_id_type=MESH)
    load_right = pltpu.make_async_copy(right, r_v, load_sem.at[2 * mats])
    load_right.start()

    def loads(m):
        return (pltpu.make_async_copy(mom.at[m], s_v.at[m], load_sem.at[m]),
                pltpu.make_async_copy(grad.at[m], g_v.at[m], load_sem.at[mats + m]))

    turns = list(range(1, ny)) + [0]
    for m in [2 * y_peer(i) + (1 - k) for i in turns] + [last] + [2 * y_peer(i) + k for i in turns]:
        for c in loads(m):
            c.start()

    load_right.wait()

    def power(m):
        for c in loads(m):
            c.wait()
        s = s_v[m] + g_v[m].astype(F32)
        s_v[m] = s
        part[m] = cut_product(nt, r_v[m], s)

    to_mate = {}
    mate_sems = (mate_send, mate_recv)
    for n, i in enumerate(turns):
        m = 2 * y_peer(i) + (1 - k)
        power(m)
    power(last)
    pl.semaphore_wait(barrier, len(peers))
    for i in turns:
        to_mate[i] = send(part.at[2 * y_peer(i) + (1 - k)], mate.at[i], mate_sems, i, mate_id)
    other_rows = pl.ds(pl.multiple_of((1 - k) * half, half), half)
    my_rows = pl.ds(pl.multiple_of(k * half, half), half)
    to_mate[ny] = send(part.at[last, other_rows], mate.at[ny, pl.ds(0, half)], mate_sems, ny, mate_id)
    for peer in along_z + along_x:
        pl.semaphore_signal(near_sem, inc=1, device_id=peer, device_id_type=MESH)
    load_weight = pltpu.make_async_copy(weight, w_out, w_sem)
    load_weight.start()

    own = 2 * y + k
    to_y = []
    for n, i in enumerate(turns):
        yd = y_peer(i)
        power(2 * yd + k)
        if n == 0:
            to_mate[ny].wait_recv()
            shared = part[last, my_rows, :] + mate[ny, 0:half, :]
        to_mate[i].wait_recv()
        if i == 0:
            yrecv[y, 0:RANK, :] = part[own] + mate[0]
            yrecv[y, RANK:, :] = shared
        else:
            ysend[i, 0:RANK, :] = part[2 * yd + k] + mate[i]
            ysend[i, RANK:, :] = shared
            to_y.append(send(ysend.at[i], yrecv.at[y], (y_send, y_recv), i, (row, 2 * yd + k)))
    pl.semaphore_wait(near_sem, len(along_z + along_x))
    for peer in two_off:
        pl.semaphore_signal(far_sem, inc=1, device_id=peer, device_id_type=MESH)
    for c in to_y:
        c.wait_recv()
    total = yrecv[0]
    for i in range(1, ny):
        total = total + yrecv[i]
    pt[last, my_rows, :] = total[RANK:]
    swap = send(pt.at[last, my_rows], pt.at[last, my_rows], (h_send, h_recv), 0, mate_id)
    pt[own] = total[0:RANK]
    gather = [send(pt.at[own], pt.at[own], (ag_send, ag_recv), i, (row, 2 * y_peer(i) + k)) for i in range(1, ny)]
    forward = {0: send(pt.at[own], pt.at[own], (fw_send, fw_recv), 0, mate_id)}

    lanes = lax.broadcasted_iota(jnp.int32, (RANK, 128), 1)
    ah, al = exact_gram(total[0:RANK])
    swap.wait_recv()
    bh, bl = exact_gram(pt[last])
    gp[0] = jnp.where(lanes < 64, ah, pltpu.roll(bh, 64, 1))
    gp[1] = jnp.where(lanes < 64, al, pltpu.roll(bl, 64, 1))
    share = RANK // nx

    def rows_of(d):
        return pl.ds(pl.multiple_of(d * share, share), share)

    to_x = [send(gp.at[:, rows_of(x_peer(i))], gx.at[x], (gx_send, gx_recv), i, (x_peer(i) * nz + z, col))
            for i in range(1, nx)]
    gx[x] = gp[:, rows_of(x), :]

    pl.semaphore_wait(far_sem, len(two_off))
    pairs = tp.shape[0]
    depth = tp.shape[2]
    t_x = {}

    def times(m, q, e):
        t = cut_product(nn, pt[m], s_v[m])
        at, to = e * RANK // depth, e * RANK % depth
        for h in range(2):
            tp[q, h * nx // 2 + at, to : to + RANK, :] = t[:, h * 128 : (h + 1) * 128]

    def block_out(turn, q):
        for i in range(1, nx):
            t_x[turn, i] = send(tp.at[q, x_peer(i)], xrecv.at[turn, i], (tx_send, tx_recv), (turn, i),
                                (x_peer(i) * nz + z, col))

    def times_pair(d):
        q = y_peer(d)
        times(2 * q, q, 0)
        times(2 * q + 1, q, 1)
        block_out(d, q)

    arrivals = sorted(range(1, ny), key=lambda d: min(d, ny - d))

    def pass_power(d):
        gather[ny - d - 1].wait_recv()
        m = 2 * y_peer(d) + k
        forward[d] = send(pt.at[m], pt.at[m], (fw_send, fw_recv), d, mate_id)

    at, to = RANK // depth, RANK % depth
    for h in range(2):
        tp[pairs - 1, h * nx // 2 + at, to : to + RANK, :] = jnp.zeros((RANK, 128), F32)
    times(last, pairs - 1, 0)
    block_out(ny, pairs - 1)
    forward[0].wait_recv()
    times_pair(0)
    for d in arrivals:
        pass_power(d)
    forward[arrivals[0]].wait_recv()
    times_pair(arrivals[0])

    def sum_pairs(ref, n):
        h, l = ref[0, 0], ref[0, 1]
        for i in range(1, n):
            h, l = add_pair(h, l, ref[i, 0], ref[i, 1])
        return h, l

    for c in to_x:
        c.wait_recv()
    h, l = sum_pairs(gx, nx)
    gz[z, 0] = h
    gz[z, 1] = l
    to_z = [send(gz.at[z], gz.at[z], (gz_send, gz_recv), i, (x * nz + z_peer(i), col)) for i in far_first]
    for d in arrivals[1:]:
        forward[d].wait_recv()
        times_pair(d)
    turn_order = [ny, 0] + arrivals
    cut_at = (len(turn_order) + 1) // 2
    groups = [turn_order[:cut_at], turn_order[cut_at:]]

    def pair_of(d):
        return pairs - 1 if d == ny else y_peer(d)

    def sum_over_x(g):
        for n, d in enumerate(groups[g]):
            acc = tp[pair_of(d), x]
            for i in range(1, nx):
                t_x[d, i].wait_recv()
                acc = acc + xrecv[d, i]
            zsend[g][:, n] = acc.reshape(nz, *zsend[g].shape[2:])
        zrecv[g][0] = zsend[g][z]
        return [send(zsend[g].at[z_peer(j)], zrecv[g].at[j], (tz_send, tz_recv), (g, j), (x * nz + z_peer(j), col))
                for j in far_first]

    t_z = [sum_over_x(0)]
    for m in range(mats):
        pw[m] = six_right(jnp.transpose(pt[m]), 1)
    t_z.append(sum_over_x(1))

    for c in to_z:
        c.wait_recv()
    h, l = sum_pairs(gz, nz)
    ga[x, 0] = h
    ga[x, 1] = l
    to_a = [send(ga.at[x], ga.at[x], (ga_send, ga_recv), i, (x_peer(i) * nz + z, col)) for i in range(1, nx)]

    a_z, a_x = {}, ([], [])

    def pass_on(g, j):
        if j:
            a_z[g, j].wait_recv()
        p = tfull[g].at[x, z_peer(nz - j)] if j else tfull[g].at[x, z]
        for i in range(1, nx):
            a_x[g].append(send(p, p, (ax_send, ax_recv), (g, i, j), (x_peer(i) * nz + z, col)))

    for g in range(2):
        for c in t_z[g]:
            c.wait_recv()
        acc = zrecv[g][0]
        for j in range(1, nz):
            acc = acc + zrecv[g][j]
        tfull[g][x, z] = acc
        for j in far_first:
            a_z[g, j] = send(tfull[g].at[x, z], tfull[g].at[x, z], (az_send, az_recv), (g, j), (x * nz + z_peer(j), col))
        pass_on(g, 0)

    for c in to_a:
        c.wait_recv()
    for i in range(nx):
        mh[i * share : (i + 1) * share, :] = ga[i, 0]
        ml[i * share : (i + 1) * share, :] = ga[i, 1]
    near_first = far_first[::-1]
    near = near_first[:4]
    rest = near_first[4:]
    factor_pair(mh, ml, 0, 32)
    for j in near:
        pass_on(0, j)
    factor_pair(mh, ml, 32, 48)
    for j in rest:
        pass_on(0, j)
    factor_pair(mh, ml, 48, RANK)
    inverse = inverse_of(mh, ml)
    low = pltpu.roll(inverse[half:], 64, 1)
    first_lanes = lax.broadcasted_iota(jnp.int32, (half, 128), 1) < 64
    linv[own] = jnp.where(first_lanes, inverse[0:half], low)
    linv[last] = jnp.where(first_lanes, pltpu.roll(inverse[0:half], 64, 1), inverse[half:])
    spread = [send(linv.at[own], linv.at[own], (l_send, l_recv), i, (row, lax.rem(col + i, nc))) for i in range(1, nc)]
    for j in near_first:
        pass_on(1, j)
    for c in spread:
        c.wait_recv()
    inverses = {}
    for d in turn_order:
        for e in range(1 if d == ny else 2):
            packed = linv[2 * pair_of(d) + e]
            inverses[d, e] = six_left(jnp.concatenate([packed[:, 0:RANK], packed[:, RANK:]], axis=0))
    squares = jnp.zeros((16, 128), F32)
    places = lax.broadcasted_iota(jnp.int32, (16, 256), 0)
    for g in range(2):
        for c in a_x[g]:
            c.wait_recv()
        for n, d in enumerate(groups[g]):
            sqs = []
            for e in range(2):
                if (d, e) not in inverses:
                    sqs.append(jnp.zeros((RANK, 256), F32))
                    continue
                at, to = e * RANK // depth, e * RANK % depth
                t = jnp.concatenate([tfull[g][h * nx // 2 + at, :, n].reshape(depth, 128)[to : to + RANK]
                                     for h in range(2)], axis=1)
                p = nn(inverses[d, e], six_right(t, 0))
                prod_out[2 * pair_of(d) + e] = p
                sqs.append(p * p)
            ones = jnp.where(places == pair_of(d), 1.0, 0.0).astype(BF16)
            both = jnp.concatenate(sqs, axis=0)
            high = both.astype(BF16)
            squares = squares + nt(ones, high) + nt(ones, (both - high.astype(F32)).astype(BF16))
    sq[col] = squares[0:8]
    to_all = [send(sq.at[col], sq.at[col], (sq_send, sq_recv), i, (row, lax.rem(col + i, nc))) for i in range(1, nc)]
    left = lax.broadcasted_iota(jnp.int32, (pw.shape[1], 3 * RANK), 1) < 2 * RANK
    for d, e in inverses:
        m = 2 * pair_of(d) + e
        q = nt(pw[m], jnp.concatenate([inverses[d, e]] * 3, axis=0))
        q1 = q.astype(BF16)
        pieces = jnp.where(left, q1.astype(F32), q - q1.astype(F32)).astype(BF16)
        q_out[m] = pieces
        m_out[m] = s_v[m] - nn(pieces, stacked_pieces(prod_out[m] * (1.0 - DECAY)))
    for c in to_all:
        c.wait_recv()
    squares = sq[0]
    for i in range(1, nc):
        squares = squares + sq[i]
    scale_out[...] = jnp.transpose(1.0 / jnp.sqrt(squares * (1.0 / ff) + EPSILON))
    load_weight.wait()
    finish()


def stacked_pieces(p):
    p1 = p.astype(BF16)
    p2 = (p - p1.astype(F32)).astype(BF16)
    return jnp.concatenate([p1, p2, p1], axis=0)


def update_kernel(gain, w, mom, q, prod, scale, new_weight, new_mom, new_right, w_v, r_v, w_sem, m_sem, r_sem):
    mats = w.shape[0]
    move = pltpu.make_async_copy(mom, new_mom, m_sem)
    move.start()
    table = scale[...]
    moves = [move]
    for m in range(mats):
        column = table[(m % 2) * RANK : (m % 2 + 1) * RANK, m // 2 : m // 2 + 1]
        normed = prod[m] * column
        r_v[m] = normed
        c = pltpu.make_async_copy(r_v.at[m], new_right.at[m], r_sem.at[m])
        c.start()
        moves.append(c)
        w_v[m] = w[m] - nn(q[m], stacked_pieces(normed * gain))
        c = pltpu.make_async_copy(w_v.at[m], new_weight.at[m], w_sem.at[m])
        c.start()
        moves.append(c)
    for c in moves:
        c.wait()


def body(nx, nz, ny, depth, weight, grad, momentum, right):
    nr, nc = nx * nz, ny * 2
    mats, rows, cols = weight.shape
    ff = cols * nc
    rt = jnp.transpose(right, (1, 2, 0))
    pairs = (mats + 1) // 2
    sizes = ((pairs + 1) // 2, pairs // 2)
    block = 256 // nx
    tile = block // nz
    share = RANK // nx
    vmem = pl.BlockSpec(memory_space=pltpu.VMEM)
    hbm = pl.BlockSpec(memory_space=pltpu.HBM)
    dma = pltpu.SemaphoreType.DMA
    half = RANK // 2
    w, mom, q, prod, scale = pl.pallas_call(
        functools.partial(exchange_kernel, nx, nz, ny),
        out_shape=(
            jax.ShapeDtypeStruct((mats, rows, cols), F32),
            jax.ShapeDtypeStruct((mats, rows, cols), F32),
            jax.ShapeDtypeStruct((mats, rows, 3 * RANK), BF16),
            jax.ShapeDtypeStruct((mats, RANK, cols), F32),
            jax.ShapeDtypeStruct((128, 8), F32),
        ),
        in_specs=[hbm] * 4,
        out_specs=(vmem,) * 5,
        scratch_shapes=[
            pltpu.VMEM((mats, rows, cols), F32),
            pltpu.VMEM((mats, rows, cols), BF16),
            pltpu.VMEM((mats, RANK, cols), F32),
            pltpu.VMEM((mats, RANK, rows), F32),
            pltpu.VMEM((ny + 1, RANK, rows), F32),
            pltpu.VMEM((ny, RANK + half, rows), F32),
            pltpu.VMEM((ny, RANK + half, rows), F32),
            pltpu.VMEM((mats, RANK, rows), F32),
            pltpu.VMEM((mats, rows, 6 * RANK), BF16),
            pltpu.VMEM((2, RANK, 128), F32),
            pltpu.VMEM((nx, 2, share, 128), F32),
            pltpu.VMEM((nz, 2, share, 128), F32),
            pltpu.VMEM((nx, 2, share, 128), F32),
            pltpu.VMEM((RANK, 128), F32),
            pltpu.VMEM((RANK, 128), F32),
            pltpu.VMEM((mats, half, 128), F32),
            pltpu.VMEM((pairs, nx, block, 128), F32),
            pltpu.VMEM((pairs, nx, block, 128), F32),
            [pltpu.VMEM((nz, n, tile, 128), F32) for n in sizes],
            [pltpu.VMEM((nz, n, tile, 128), F32) for n in sizes],
            [pltpu.VMEM((nx, nz, n, tile, 128), F32) for n in sizes],
            pltpu.VMEM((nc, 8, 128), F32),
            dma((2 * mats + 1,)),
            dma,
            dma((ny + 1,)), dma((ny + 1,)),
            dma((ny,)), dma((ny,)),
            dma((ny,)), dma((ny,)),
            dma((ny,)), dma((ny,)),
            dma((1,)), dma((1,)),
            dma((nx,)), dma((nx,)),
            dma((nz,)), dma((nz,)),
            dma((nx,)), dma((nx,)),
            dma((pairs, nx)), dma((pairs, nx)),
            dma((2, nz)), dma((2, nz)),
            dma((2, nz)), dma((2, nz)),
            dma((2, nx, nz)), dma((2, nx, nz)),
            dma((nc,)), dma((nc,)),
            dma((nc,)), dma((nc,)),
            pltpu.SemaphoreType.REGULAR,
            pltpu.SemaphoreType.REGULAR,
        ],
        compiler_params=pltpu.CompilerParams(
            collective_id=0, has_side_effects=True, vmem_limit_bytes=40 * 1024 * 1024
        ),
        name="exchange",
    )(*[pltpu.with_memory_space_constraint(v, pltpu.HBM) for v in (weight, grad, momentum, rt)])

    gain = math.sqrt(depth / ff)
    new_weight, new_momentum, new_right = pl.pallas_call(
        functools.partial(update_kernel, gain),
        out_shape=(
            jax.ShapeDtypeStruct(weight.shape, F32),
            jax.ShapeDtypeStruct(weight.shape, F32),
            jax.ShapeDtypeStruct((mats, RANK, cols), F32),
        ),
        in_specs=[vmem] * 5,
        out_specs=(hbm,) * 3,
        scratch_shapes=[
            pltpu.VMEM((mats, rows, cols), F32),
            pltpu.VMEM((mats, RANK, cols), F32),
            dma((mats,)),
            dma,
            dma((mats,)),
        ],
        compiler_params=pltpu.CompilerParams(vmem_limit_bytes=12 * 1024 * 1024),
        name="update",
    )(w, mom, q, prod, scale)
    return new_weight, new_momentum, jnp.transpose(new_right, (2, 0, 1))


def solution(mesh):
    nr, nc = mesh.shape["row"], mesh.shape["col"]
    nz = min(nr, 8)
    nx = nr // nz

    def run(weight, grad, momentum, right):
        return body(nx, nz, nc // 2, weight.shape[1] * nr, weight, grad, momentum, right)

    placed = P(None, "row", "col")
    return jax.shard_map(
        run,
        mesh=mesh,
        in_specs=(placed, placed, placed, P("col", None, None)),
        out_specs=(placed, placed, P("col", None, None)),
        check_vma=False,
    )
```

```python
import functools
import math

import jax
import jax.numpy as jnp
from jax import lax
from jax.experimental import pallas as pl
from jax.experimental.pallas import tpu as pltpu
from jax.sharding import PartitionSpec as P

MESH = pl.DeviceIdType.MESH
F32 = jnp.float32
BF16 = jnp.bfloat16

EPSILON = 1e-06
DECAY = 0.95
RANK = 64


def two_sum(a, b):
    s = a + b
    back = s - a
    return s, (a - (s - back)) + (b - back)


def split(a):
    t = a * 4097.0
    high = t - (t - a)
    return high, a - high


def two_prod(a, b):
    p = a * b
    ah, al = split(a)
    bh, bl = split(b)
    return p, ((ah * bh - p) + ah * bl + al * bh) + al * bl


def add_pair(ah, al, bh, bl):
    s, t = two_sum(ah, bh)
    t = t + (al + bl)
    h = s + t
    return h, t - (h - s)


def nt(a, b, precision=None):
    return lax.dot_general(a, b, (((1,), (1,)), ((), ())), precision=precision, preferred_element_type=F32)


def nn(a, b, precision=None):
    return lax.dot_general(a, b, (((1,), (0,)), ((), ())), precision=precision, preferred_element_type=F32)


def tn(a, b, precision=None):
    return lax.dot_general(a, b, (((0,), (0,)), ((), ())), precision=precision, preferred_element_type=F32)


def cut(a):
    a1 = a.astype(BF16)
    rest = a - a1.astype(F32)
    a2 = rest.astype(BF16)
    return a1, a2, (rest - a2.astype(F32)).astype(BF16)


def cut_product(dot, a, b):
    a1, a2, a3 = cut(a)
    b1, b2, b3 = cut(b)
    p = dot(jnp.concatenate([a1, a2, a3], axis=0), b1)
    q = dot(jnp.concatenate([a1, a2], axis=0), b2)
    r = dot(a1, b3)
    return p[0:RANK] + ((p[RANK : 2 * RANK] + q[0:RANK]) + (p[2 * RANK :] + q[RANK:] + r))


def six_left(a):
    a1, a2, a3 = cut(a)
    return jnp.concatenate([a1, a2, a1, a3, a2, a1], axis=1)


def six_right(a, axis):
    a1, a2, a3 = cut(a)
    return jnp.concatenate([a1, a1, a2, a1, a2, a3], axis=axis)


def round_int(v):
    magic = 1.5 * 2.0**23
    return (v + magic) - magic


def exact_gram(x):
    top = jnp.maximum(jnp.max(jnp.abs(x), axis=1, keepdims=True), 1e-18)
    top = jnp.broadcast_to(top, (RANK, 128))
    power = jnp.floor(jnp.log(top) * (1.0 / math.log(2.0))) + 1.0
    unit = jnp.exp2(power - 7.0).astype(BF16).astype(F32)
    inverse = jnp.exp2(7.0 - power).astype(BF16).astype(F32)
    y = x * inverse[:, 0:1]
    slices = []
    for i in range(4):
        q = round_int(y)
        slices.append(q.astype(BF16))
        y = (y - q) * 256.0
    q = jnp.concatenate(slices, axis=0)
    e = nt(q, q)
    low = [e[RANK * a : RANK * (a + 1), 0:128] for a in range(4)]
    high = [e[RANK * a : RANK * (a + 1), 128:256] for a in range(4)]
    levels = [low[0], low[1], low[2] + high[0], low[3] + high[1], high[2], high[3]]
    s, t = levels[0], jnp.zeros_like(levels[0])
    for i in range(1, 6):
        s, err = two_sum(s, levels[i] * (2.0 ** (-8 * i)))
        t = t + err
    s2 = pltpu.roll(s, 64, 1) * (1.0 / 256.0)
    t2 = pltpu.roll(t, 64, 1) * (1.0 / 256.0)
    gh, gl = add_pair(s, t, s2, t2)
    rows = lax.broadcasted_iota(jnp.int32, (RANK, 128), 0)
    lanes = lax.broadcasted_iota(jnp.int32, (RANK, 128), 1)
    across = jnp.sum(jnp.where(rows == lanes, unit, 0.0), axis=0, keepdims=True)
    return gh * unit * across, gl * unit * across


def mul_pair(ah, al, bh, bl):
    p, e = two_prod(ah, bh)
    return p, e + (ah * bl + al * bh)


def sub_pairs(h, l, m1, r1, m2, r2):
    p, q = mul_pair(*m1, *r1)
    s, e = two_sum(h, -p)
    p2, q2 = mul_pair(*m2, *r2)
    s, e2 = two_sum(s, -p2)
    e = (e + e2) + (l - (q + q2))
    h = s + e
    return h, e - (h - s)


def cross(a, b, c, d):
    p1, e1 = mul_pair(*a, *b)
    p2, e2 = mul_pair(*c, *d)
    return add_pair(p1, e1, -p2, -e2)


def factor_block(mh, ml, first):
    tiles = (RANK - first) // 8
    rows = lax.broadcasted_iota(jnp.int32, (8, 128), 0)
    lanes = lax.broadcasted_iota(jnp.int32, (8, 128), 1)
    half = jnp.where(lanes >= 64, 64, 0)
    column = lanes - half
    m = [(mh[first + 8 * t : first + 8 * t + 8, :], ml[first + 8 * t : first + 8 * t + 8, :]) for t in range(tiles)]

    def row(v, i):
        return tuple(jnp.broadcast_to(part[i : i + 1], (8, 128)) for part in v)

    def masked(mask, v):
        return tuple(jnp.where(mask, part, 0.0) for part in v)

    own = [tuple(jnp.take_along_axis(part, half + (first + j), axis=1) for part in m[0]) for j in range(8)]
    steps = []
    for i in range(0, 8, 2):
        k = first + i
        c1, c2 = own[i], own[i + 1]
        a, b, c = row(c1, i), row(c2, i), row(c2, i + 1)
        dh, dl = cross(a, c, b, b)
        inv = 1.0 / dh
        p, e = two_prod(dh, inv)
        inv = (inv, inv * (((1.0 - p) - e) - dl * inv))
        later = rows > i + 1
        n1 = masked(later, mul_pair(*cross(c1, c, c2, b), *inv))
        n2 = masked(later, mul_pair(*cross(c2, a, c1, b), *inv))
        for j in range(i + 2, 8):
            own[j] = sub_pairs(*own[j], n1, row(own[j], i), n2, row(own[j], i + 1))
        r1, r2 = row(m[0], i), row(m[0], i + 1)
        w1 = mul_pair(*cross(r1, c, r2, b), *inv)
        w2 = mul_pair(*cross(r2, a, r1, b), *inv)
        here1, here2 = column == k, column == k + 1
        here = here1 | here2
        r1 = (jnp.where(here1, 1.0, jnp.where(here2, 0.0, r1[0])), jnp.where(here, 0.0, r1[1]))
        r2 = (jnp.where(here2, 1.0, jnp.where(here1, 0.0, r2[0])), jnp.where(here, 0.0, r2[1]))
        m[0] = sub_pairs(*masked(jnp.logical_not(here & later), m[0]), n1, r1, n2, r2)
        steps.append((here, w1, w2, r1, r2))
    for t in range(1, tiles):
        index = half + (rows + (first + 8 * t))

        def spread(v):
            return tuple(jnp.take_along_axis(part, index, axis=1) for part in v)

        for here, w1, w2, r1, r2 in steps:
            m[t] = sub_pairs(*masked(jnp.logical_not(here), m[t]), spread(w1), r1, spread(w2), r2)
    for t in range(tiles):
        mh[first + 8 * t : first + 8 * t + 8, :] = m[t][0]
        ml[first + 8 * t : first + 8 * t + 8, :] = m[t][1]


def factor_pair(mh, ml, begin, end):
    for first in range(begin, end, 8):
        factor_block(mh, ml, first)


def inverse_of(mh, ml):
    m = mh[...]
    rows = lax.broadcasted_iota(jnp.int32, (RANK, 128), 0)
    lanes = lax.broadcasted_iota(jnp.int32, (RANK, 128), 1)
    left = lanes < 64
    column = jnp.where(left, lanes, lanes - 64)
    odd = (rows & 1) == 1

    def pick(v, mask):
        v = jnp.where(mask, v, 0.0)
        a = jnp.sum(jnp.where(left, v, 0.0), axis=1, keepdims=True)
        b = jnp.sum(jnp.where(left, 0.0, v), axis=1, keepdims=True)
        return jnp.where(left, a, b)

    same, next_to = column == rows, column == (rows ^ 1)
    ch, cl = pick(m, same), pick(ml[...], same)
    bh, bl = pick(m, next_to), pick(ml[...], next_to)
    ah, al = pltpu.roll(ch, 1, 0), pltpu.roll(cl, 1, 0)
    inv = 1.0 / ah
    p, e = two_prod(ah, inv)
    rh, rl = mul_pair(bh, bl, inv, inv * (((1.0 - p) - e) - al * inv))
    p, e = mul_pair(rh, rl, bh, bl)
    ph, _ = add_pair(ch, cl, -p, -e)
    root = 1.0 / jnp.sqrt(jnp.where(odd, ph, ch))
    ratio = jnp.where(odd, rh, 0.0)
    unit = jnp.where(column < rows - (rows & 1), m, jnp.where(column == rows, 1.0, 0.0))
    return (unit - ratio * pltpu.roll(unit, 1, 0)) * root


def exchange_kernel(nx, nz, ny, weight, grad, mom, right, w_out, m_out, q_out, prod_out, scale_out, s_v, g_v, r_v, part,
                    mate, ysend, yrecv, pt, pw, gp, gx, gz, ga, mh, ml, linv, tp, xrecv, zsend, zrecv, tfull, sq, load_sem,
                    w_sem, mate_send, mate_recv, y_send, y_recv, ag_send, ag_recv, fw_send, fw_recv, h_send, h_recv,
                    gx_send, gx_recv, gz_send, gz_recv, ga_send, ga_recv, tx_send, tx_recv, tz_send, tz_recv, az_send,
                    az_recv, ax_send, ax_recv, l_send, l_recv, sq_send, sq_recv, near_sem, far_sem):
    nr, nc = nx * nz, ny * 2
    mats = nc + 1
    last = mats - 1
    ff = 256 * nc
    row, col = lax.axis_index("row"), lax.axis_index("col")
    x, z = row // nz, row % nz
    y, k = col // 2, col % 2
    mate_id = (row, y * 2 + (1 - k))
    half = RANK // 2

    pending = []

    def finish():
        for c in pending:
            c.wait_send()

    def send(src, dst, sems, index, target):
        c = pltpu.make_async_remote_copy(src_ref=src, dst_ref=dst, send_sem=sems[0].at[index], recv_sem=sems[1].at[index],
                                         device_id=target, device_id_type=MESH)
        c.start()
        pending.append(c)
        return c

    def x_peer(i):
        return lax.rem(x + i, nx)

    def z_peer(i):
        return lax.rem(z + i, nz)

    def y_peer(i):
        return lax.rem(y + i, ny)

    far_first = sorted(range(1, nz), key=lambda i: -min(i, nz - i))

    barrier = pltpu.get_barrier_semaphore()
    along_z = [(x * nz + z_peer(i), col) for i in (1, nz - 1)]
    along_x = [(x_peer(i) * nz + z, col) for i in (1, nx - 1)]
    two_off = [(x * nz + z_peer(i), col) for i in (2, nz - 2)]
    peers = along_z + along_x + [(row, lax.rem(col + i, nc)) for i in range(1, nc)]
    for peer in peers:
        pl.semaphore_signal(barrier, inc=1, device_id=peer, device_id_type=MESH)
    def loads(m):
        return (pltpu.make_async_copy(mom.at[m], s_v.at[m], load_sem.at[m]),
                pltpu.make_async_copy(grad.at[m], g_v.at[m], load_sem.at[mats + m]),
                pltpu.make_async_copy(right.at[m], r_v.at[m], load_sem.at[2 * mats + m]))

    far_y = sorted(range(1, ny), key=lambda i: -min(i, ny - i))
    turns = far_y + [0]
    for m in [2 * y_peer(i) + (1 - k) for i in turns] + [last] + [2 * y_peer(i) + k for i in turns]:
        for c in loads(m):
            c.start()


    def power(m):
        for c in loads(m):
            c.wait()
        s = s_v[m] + g_v[m].astype(F32)
        s_v[m] = s
        part[m] = cut_product(nt, r_v[m], s)

    to_mate = {}
    mate_sems = (mate_send, mate_recv)
    for n, i in enumerate(turns):
        m = 2 * y_peer(i) + (1 - k)
        power(m)
    power(last)
    pl.semaphore_wait(barrier, len(peers))
    for i in turns:
        to_mate[i] = send(part.at[2 * y_peer(i) + (1 - k)], mate.at[i], mate_sems, i, mate_id)
    other_rows = pl.ds(pl.multiple_of((1 - k) * half, half), half)
    my_rows = pl.ds(pl.multiple_of(k * half, half), half)
    to_mate[ny] = send(part.at[last, other_rows], mate.at[ny, pl.ds(0, half)], mate_sems, ny, mate_id)
    for peer in along_z + along_x:
        pl.semaphore_signal(near_sem, inc=1, device_id=peer, device_id_type=MESH)
    load_weight = pltpu.make_async_copy(weight, w_out, w_sem)
    load_weight.start()

    own = 2 * y + k
    to_y = []
    for n, i in enumerate(turns):
        yd = y_peer(i)
        power(2 * yd + k)
        if n == 0:
            to_mate[ny].wait_recv()
            shared = part[last, my_rows, :] + mate[ny, 0:half, :]
        to_mate[i].wait_recv()
        if i == 0:
            yrecv[y, 0:RANK, :] = part[own] + mate[0]
            yrecv[y, RANK:, :] = shared
        else:
            ysend[i, 0:RANK, :] = part[2 * yd + k] + mate[i]
            ysend[i, RANK:, :] = shared
            to_y.append(send(ysend.at[i], yrecv.at[y], (y_send, y_recv), i, (row, 2 * yd + k)))
    pl.semaphore_wait(near_sem, len(along_z + along_x))
    for peer in two_off:
        pl.semaphore_signal(far_sem, inc=1, device_id=peer, device_id_type=MESH)
    for c in to_y:
        c.wait_recv()
    total = yrecv[0]
    for i in range(1, ny):
        total = total + yrecv[i]
    pt[last, my_rows, :] = total[RANK:]
    swap = send(pt.at[last, my_rows], pt.at[last, my_rows], (h_send, h_recv), 0, mate_id)
    pt[own] = total[0:RANK]
    gather = {i: send(pt.at[own], pt.at[own], (ag_send, ag_recv), i, (row, 2 * y_peer(i) + k)) for i in far_y}
    forward = {0: send(pt.at[own], pt.at[own], (fw_send, fw_recv), 0, mate_id)}

    lanes = lax.broadcasted_iota(jnp.int32, (RANK, 128), 1)
    ah, al = exact_gram(total[0:RANK])
    swap.wait_recv()
    bh, bl = exact_gram(pt[last])
    gp[0] = jnp.where(lanes < 64, ah, pltpu.roll(bh, 64, 1))
    gp[1] = jnp.where(lanes < 64, al, pltpu.roll(bl, 64, 1))
    share = RANK // nx

    def rows_of(d):
        return pl.ds(pl.multiple_of(d * share, share), share)

    to_x = [send(gp.at[:, rows_of(x_peer(i))], gx.at[x], (gx_send, gx_recv), i, (x_peer(i) * nz + z, col))
            for i in range(1, nx)]
    gx[x] = gp[:, rows_of(x), :]

    pl.semaphore_wait(far_sem, len(two_off))
    pairs = tp.shape[0]
    depth = tp.shape[2]
    t_x = {}

    def times(m, q, e):
        t = cut_product(nn, pt[m], s_v[m])
        at, to = e * RANK // depth, e * RANK % depth
        for h in range(2):
            tp[q, h * nx // 2 + at, to : to + RANK, :] = t[:, h * 128 : (h + 1) * 128]

    def block_out(turn, q):
        for i in range(1, nx):
            t_x[turn, i] = send(tp.at[q, x_peer(i)], xrecv.at[turn, i], (tx_send, tx_recv), (turn, i),
                                (x_peer(i) * nz + z, col))

    def times_pair(d):
        q = y_peer(d)
        times(2 * q, q, 0)
        times(2 * q + 1, q, 1)
        block_out(d, q)

    arrivals = sorted(range(1, ny), key=lambda d: min(d, ny - d))

    def pass_power(d):
        gather[ny - d].wait_recv()
        m = 2 * y_peer(d) + k
        forward[d] = send(pt.at[m], pt.at[m], (fw_send, fw_recv), d, mate_id)

    at, to = RANK // depth, RANK % depth
    for h in range(2):
        tp[pairs - 1, h * nx // 2 + at, to : to + RANK, :] = jnp.zeros((RANK, 128), F32)
    times(last, pairs - 1, 0)
    block_out(ny, pairs - 1)
    forward[0].wait_recv()
    times_pair(0)
    for d in arrivals:
        pass_power(d)
    forward[arrivals[0]].wait_recv()
    times_pair(arrivals[0])

    def sum_pairs(ref, n):
        h, l = ref[0, 0], ref[0, 1]
        for i in range(1, n):
            h, l = add_pair(h, l, ref[i, 0], ref[i, 1])
        return h, l

    for c in to_x:
        c.wait_recv()
    h, l = sum_pairs(gx, nx)
    gz[z, 0] = h
    gz[z, 1] = l
    to_z = [send(gz.at[z], gz.at[z], (gz_send, gz_recv), i, (x * nz + z_peer(i), col)) for i in far_first]
    for d in arrivals[1:]:
        forward[d].wait_recv()
        times_pair(d)
    turn_order = [ny, 0] + arrivals
    cut_at = (len(turn_order) + 1) // 2
    groups = [turn_order[:cut_at], turn_order[cut_at:]]

    def pair_of(d):
        return pairs - 1 if d == ny else y_peer(d)

    def sum_over_x(g):
        for n, d in enumerate(groups[g]):
            acc = tp[pair_of(d), x]
            for i in range(1, nx):
                t_x[d, i].wait_recv()
                acc = acc + xrecv[d, i]
            zsend[g][:, n] = acc.reshape(nz, *zsend[g].shape[2:])
        zrecv[g][0] = zsend[g][z]
        return [send(zsend[g].at[z_peer(j)], zrecv[g].at[j], (tz_send, tz_recv), (g, j), (x * nz + z_peer(j), col))
                for j in far_first]

    t_z = [sum_over_x(0)]
    t_z.append(sum_over_x(1))

    for c in to_z:
        c.wait_recv()
    h, l = sum_pairs(gz, nz)
    ga[x, 0] = h
    ga[x, 1] = l
    to_a = [send(ga.at[x], ga.at[x], (ga_send, ga_recv), i, (x_peer(i) * nz + z, col)) for i in range(1, nx)]

    for m in range(mats):
        pw[m] = six_right(jnp.transpose(pt[m]), 1)
    a_z, a_x = {}, ([], [])

    def pass_on(g, j):
        if j:
            a_z[g, j].wait_recv()
        p = tfull[g].at[x, z_peer(nz - j)] if j else tfull[g].at[x, z]
        for i in range(1, nx):
            a_x[g].append(send(p, p, (ax_send, ax_recv), (g, i, j), (x_peer(i) * nz + z, col)))

    for g in range(2):
        for c in t_z[g]:
            c.wait_recv()
        acc = zrecv[g][0]
        for j in range(1, nz):
            acc = acc + zrecv[g][j]
        tfull[g][x, z] = acc
        for j in far_first:
            a_z[g, j] = send(tfull[g].at[x, z], tfull[g].at[x, z], (az_send, az_recv), (g, j), (x * nz + z_peer(j), col))
        pass_on(g, 0)

    for c in to_a:
        c.wait_recv()
    for i in range(nx):
        mh[i * share : (i + 1) * share, :] = ga[i, 0]
        ml[i * share : (i + 1) * share, :] = ga[i, 1]
    near_first = far_first[::-1]
    near = near_first[:4]
    rest = near_first[4:]
    factor_pair(mh, ml, 0, 32)
    for j in near:
        pass_on(0, j)
    factor_pair(mh, ml, 32, 48)
    for j in rest:
        pass_on(0, j)
    factor_pair(mh, ml, 48, RANK)
    inverse = inverse_of(mh, ml)
    low = pltpu.roll(inverse[half:], 64, 1)
    first_lanes = lax.broadcasted_iota(jnp.int32, (half, 128), 1) < 64
    linv[own] = jnp.where(first_lanes, inverse[0:half], low)
    linv[last] = jnp.where(first_lanes, pltpu.roll(inverse[0:half], 64, 1), inverse[half:])
    spread = [send(linv.at[own], linv.at[own], (l_send, l_recv), i, (row, lax.rem(col + i, nc))) for i in range(1, nc)]
    for j in near_first:
        pass_on(1, j)
    for c in spread:
        c.wait_recv()
    inverses = {}
    for d in turn_order:
        for e in range(1 if d == ny else 2):
            packed = linv[2 * pair_of(d) + e]
            inverses[d, e] = six_left(jnp.concatenate([packed[:, 0:RANK], packed[:, RANK:]], axis=0))
    squares = jnp.zeros((16, 128), F32)
    places = lax.broadcasted_iota(jnp.int32, (16, 256), 0)
    for g in range(2):
        for c in a_x[g]:
            c.wait_recv()
        for n, d in enumerate(groups[g]):
            sqs = []
            for e in range(2):
                if (d, e) not in inverses:
                    sqs.append(jnp.zeros((RANK, 256), F32))
                    continue
                at, to = e * RANK // depth, e * RANK % depth
                t = jnp.concatenate([tfull[g][h * nx // 2 + at, :, n].reshape(depth, 128)[to : to + RANK]
                                     for h in range(2)], axis=1)
                p = nn(inverses[d, e], six_right(t, 0))
                prod_out[2 * pair_of(d) + e] = p
                sqs.append(p * p)
            ones = jnp.where(places == pair_of(d), 1.0, 0.0).astype(BF16)
            both = jnp.concatenate(sqs, axis=0)
            high = both.astype(BF16)
            squares = squares + nt(ones, high) + nt(ones, (both - high.astype(F32)).astype(BF16))
    sq[col] = squares[0:8]
    to_all = [send(sq.at[col], sq.at[col], (sq_send, sq_recv), i, (row, lax.rem(col + i, nc))) for i in range(1, nc)]
    left = lax.broadcasted_iota(jnp.int32, (pw.shape[1], 3 * RANK), 1) < 2 * RANK
    for d, e in inverses:
        m = 2 * pair_of(d) + e
        q = nt(pw[m], jnp.concatenate([inverses[d, e]] * 3, axis=0))
        q1 = q.astype(BF16)
        pieces = jnp.where(left, q1.astype(F32), q - q1.astype(F32)).astype(BF16)
        q_out[m] = pieces
        m_out[m] = s_v[m] - nn(pieces, stacked_pieces(prod_out[m] * (1.0 - DECAY)))
    for c in to_all:
        c.wait_recv()
    squares = sq[0]
    for i in range(1, nc):
        squares = squares + sq[i]
    scale_out[...] = jnp.transpose(1.0 / jnp.sqrt(squares * (1.0 / ff) + EPSILON))
    load_weight.wait()
    finish()


def stacked_pieces(p):
    p1 = p.astype(BF16)
    p2 = (p - p1.astype(F32)).astype(BF16)
    return jnp.concatenate([p1, p2, p1], axis=0)


def update_kernel(gain, w, mom, q, prod, scale, new_weight, new_mom, new_right, w_v, r_v, w_sem, m_sem, r_sem):
    mats = w.shape[0]
    moves = [pltpu.make_async_copy(mom.at[m], new_mom.at[m], m_sem.at[m]) for m in range(mats)]
    for c in moves:
        c.start()
    table = scale[...]
    for m in range(mats):
        column = table[(m % 2) * RANK : (m % 2 + 1) * RANK, m // 2 : m // 2 + 1]
        normed = prod[m] * column
        r_v[m] = normed
        c = pltpu.make_async_copy(r_v.at[m], new_right.at[m], r_sem.at[m])
        c.start()
        moves.append(c)
        w_v[m] = w[m] - nn(q[m], stacked_pieces(normed * gain))
        c = pltpu.make_async_copy(w_v.at[m], new_weight.at[m], w_sem.at[m])
        c.start()
        moves.append(c)
    for c in moves:
        c.wait()


def body(nx, nz, ny, depth, weight, grad, momentum, right):
    nr, nc = nx * nz, ny * 2
    mats, rows, cols = weight.shape
    ff = cols * nc
    rt = jnp.transpose(right, (1, 2, 0))
    pairs = (mats + 1) // 2
    sizes = ((pairs + 1) // 2, pairs // 2)
    block = 256 // nx
    tile = block // nz
    share = RANK // nx
    vmem = pl.BlockSpec(memory_space=pltpu.VMEM)
    hbm = pl.BlockSpec(memory_space=pltpu.HBM)
    dma = pltpu.SemaphoreType.DMA
    half = RANK // 2
    w, mom, q, prod, scale = pl.pallas_call(
        functools.partial(exchange_kernel, nx, nz, ny),
        out_shape=(
            jax.ShapeDtypeStruct((mats, rows, cols), F32),
            jax.ShapeDtypeStruct((mats, rows, cols), F32),
            jax.ShapeDtypeStruct((mats, rows, 3 * RANK), BF16),
            jax.ShapeDtypeStruct((mats, RANK, cols), F32),
            jax.ShapeDtypeStruct((128, 8), F32),
        ),
        in_specs=[hbm] * 4,
        out_specs=(vmem,) * 5,
        scratch_shapes=[
            pltpu.VMEM((mats, rows, cols), F32),
            pltpu.VMEM((mats, rows, cols), BF16),
            pltpu.VMEM((mats, RANK, cols), F32),
            pltpu.VMEM((mats, RANK, rows), F32),
            pltpu.VMEM((ny + 1, RANK, rows), F32),
            pltpu.VMEM((ny, RANK + half, rows), F32),
            pltpu.VMEM((ny, RANK + half, rows), F32),
            pltpu.VMEM((mats, RANK, rows), F32),
            pltpu.VMEM((mats, rows, 6 * RANK), BF16),
            pltpu.VMEM((2, RANK, 128), F32),
            pltpu.VMEM((nx, 2, share, 128), F32),
            pltpu.VMEM((nz, 2, share, 128), F32),
            pltpu.VMEM((nx, 2, share, 128), F32),
            pltpu.VMEM((RANK, 128), F32),
            pltpu.VMEM((RANK, 128), F32),
            pltpu.VMEM((mats, half, 128), F32),
            pltpu.VMEM((pairs, nx, block, 128), F32),
            pltpu.VMEM((pairs, nx, block, 128), F32),
            [pltpu.VMEM((nz, n, tile, 128), F32) for n in sizes],
            [pltpu.VMEM((nz, n, tile, 128), F32) for n in sizes],
            [pltpu.VMEM((nx, nz, n, tile, 128), F32) for n in sizes],
            pltpu.VMEM((nc, 8, 128), F32),
            dma((3 * mats,)),
            dma,
            dma((ny + 1,)), dma((ny + 1,)),
            dma((ny,)), dma((ny,)),
            dma((ny,)), dma((ny,)),
            dma((ny,)), dma((ny,)),
            dma((1,)), dma((1,)),
            dma((nx,)), dma((nx,)),
            dma((nz,)), dma((nz,)),
            dma((nx,)), dma((nx,)),
            dma((pairs, nx)), dma((pairs, nx)),
            dma((2, nz)), dma((2, nz)),
            dma((2, nz)), dma((2, nz)),
            dma((2, nx, nz)), dma((2, nx, nz)),
            dma((nc,)), dma((nc,)),
            dma((nc,)), dma((nc,)),
            pltpu.SemaphoreType.REGULAR,
            pltpu.SemaphoreType.REGULAR,
        ],
        compiler_params=pltpu.CompilerParams(
            collective_id=0, has_side_effects=True, vmem_limit_bytes=40 * 1024 * 1024
        ),
        name="exchange",
    )(*[pltpu.with_memory_space_constraint(v, pltpu.HBM) for v in (weight, grad, momentum, rt)])

    gain = math.sqrt(depth / ff)
    new_weight, new_momentum, new_right = pl.pallas_call(
        functools.partial(update_kernel, gain),
        out_shape=(
            jax.ShapeDtypeStruct(weight.shape, F32),
            jax.ShapeDtypeStruct(weight.shape, F32),
            jax.ShapeDtypeStruct((mats, RANK, cols), F32),
        ),
        in_specs=[vmem] * 5,
        out_specs=(hbm,) * 3,
        scratch_shapes=[
            pltpu.VMEM((mats, rows, cols), F32),
            pltpu.VMEM((mats, RANK, cols), F32),
            dma((mats,)),
            dma((mats,)),
            dma((mats,)),
        ],
        compiler_params=pltpu.CompilerParams(vmem_limit_bytes=12 * 1024 * 1024),
        name="update",
    )(w, mom, q, prod, scale)
    return new_weight, new_momentum, jnp.transpose(new_right, (2, 0, 1))


def solution(mesh):
    nr, nc = mesh.shape["row"], mesh.shape["col"]
    nz = min(nr, 8)
    nx = nr // nz

    def run(weight, grad, momentum, right):
        return body(nx, nz, nc // 2, weight.shape[1] * nr, weight, grad, momentum, right)

    placed = P(None, "row", "col")
    return jax.shard_map(
        run,
        mesh=mesh,
        in_specs=(placed, placed, placed, P("col", None, None)),
        out_specs=(placed, placed, P("col", None, None)),
        check_vma=False,
    )
```

```python
import functools
import math

import jax
import jax.numpy as jnp
from jax import lax
from jax.experimental import pallas as pl
from jax.experimental.pallas import tpu as pltpu
from jax.sharding import PartitionSpec as P

MESH = pl.DeviceIdType.MESH
F32 = jnp.float32
BF16 = jnp.bfloat16

EPSILON = 1e-06
DECAY = 0.95
RANK = 64


def two_sum(a, b):
    s = a + b
    back = s - a
    return s, (a - (s - back)) + (b - back)


def split(a):
    t = a * 4097.0
    high = t - (t - a)
    return high, a - high


def two_prod(a, b):
    p = a * b
    ah, al = split(a)
    bh, bl = split(b)
    return p, ((ah * bh - p) + ah * bl + al * bh) + al * bl


def add_pair(ah, al, bh, bl):
    s, t = two_sum(ah, bh)
    t = t + (al + bl)
    h = s + t
    return h, t - (h - s)


def nt(a, b, precision=None):
    return lax.dot_general(a, b, (((1,), (1,)), ((), ())), precision=precision, preferred_element_type=F32)


def nn(a, b, precision=None):
    return lax.dot_general(a, b, (((1,), (0,)), ((), ())), precision=precision, preferred_element_type=F32)


def tn(a, b, precision=None):
    return lax.dot_general(a, b, (((0,), (0,)), ((), ())), precision=precision, preferred_element_type=F32)


def cut(a):
    a1 = a.astype(BF16)
    rest = a - a1.astype(F32)
    a2 = rest.astype(BF16)
    return a1, a2, (rest - a2.astype(F32)).astype(BF16)


def cut_product(dot, a, b):
    a1, a2, a3 = cut(a)
    b1, b2, b3 = cut(b)
    p = dot(jnp.concatenate([a1, a2, a3], axis=0), b1)
    q = dot(jnp.concatenate([a1, a2], axis=0), b2)
    r = dot(a1, b3)
    return p[0:RANK] + ((p[RANK : 2 * RANK] + q[0:RANK]) + (p[2 * RANK :] + q[RANK:] + r))


def six_left(a):
    a1, a2, a3 = cut(a)
    return jnp.concatenate([a1, a2, a1, a3, a2, a1], axis=1)


def six_right(a, axis):
    a1, a2, a3 = cut(a)
    return jnp.concatenate([a1, a1, a2, a1, a2, a3], axis=axis)


def round_int(v):
    magic = 1.5 * 2.0**23
    return (v + magic) - magic


def exact_gram(x):
    top = jnp.maximum(jnp.max(jnp.abs(x), axis=1, keepdims=True), 1e-18)
    top = jnp.broadcast_to(top, (RANK, 128))
    power = jnp.floor(jnp.log(top) * (1.0 / math.log(2.0))) + 1.0
    unit = jnp.exp2(power - 7.0).astype(BF16).astype(F32)
    inverse = jnp.exp2(7.0 - power).astype(BF16).astype(F32)
    y = x * inverse[:, 0:1]
    slices = []
    for i in range(4):
        q = round_int(y)
        slices.append(q.astype(BF16))
        y = (y - q) * 256.0
    q = jnp.concatenate(slices, axis=0)
    e = nt(q, q)
    low = [e[RANK * a : RANK * (a + 1), 0:128] for a in range(4)]
    high = [e[RANK * a : RANK * (a + 1), 128:256] for a in range(4)]
    levels = [low[0], low[1], low[2] + high[0], low[3] + high[1], high[2], high[3]]
    s, t = levels[0], jnp.zeros_like(levels[0])
    for i in range(1, 6):
        s, err = two_sum(s, levels[i] * (2.0 ** (-8 * i)))
        t = t + err
    s2 = pltpu.roll(s, 64, 1) * (1.0 / 256.0)
    t2 = pltpu.roll(t, 64, 1) * (1.0 / 256.0)
    gh, gl = add_pair(s, t, s2, t2)
    rows = lax.broadcasted_iota(jnp.int32, (RANK, 128), 0)
    lanes = lax.broadcasted_iota(jnp.int32, (RANK, 128), 1)
    across = jnp.sum(jnp.where(rows == lanes, unit, 0.0), axis=0, keepdims=True)
    return gh * unit * across, gl * unit * across


def mul_pair(ah, al, bh, bl):
    p, e = two_prod(ah, bh)
    return p, e + (ah * bl + al * bh)


def sub_pairs(h, l, m1, r1, m2, r2):
    p, q = mul_pair(*m1, *r1)
    s, e = two_sum(h, -p)
    p2, q2 = mul_pair(*m2, *r2)
    s, e2 = two_sum(s, -p2)
    e = (e + e2) + (l - (q + q2))
    h = s + e
    return h, e - (h - s)


def cross(a, b, c, d):
    p1, e1 = mul_pair(*a, *b)
    p2, e2 = mul_pair(*c, *d)
    return add_pair(p1, e1, -p2, -e2)


def factor_block(mh, ml, first):
    tiles = (RANK - first) // 8
    rows = lax.broadcasted_iota(jnp.int32, (8, 128), 0)
    lanes = lax.broadcasted_iota(jnp.int32, (8, 128), 1)
    half = jnp.where(lanes >= 64, 64, 0)
    column = lanes - half
    m = [(mh[first + 8 * t : first + 8 * t + 8, :], ml[first + 8 * t : first + 8 * t + 8, :]) for t in range(tiles)]

    def row(v, i):
        return tuple(jnp.broadcast_to(part[i : i + 1], (8, 128)) for part in v)

    def masked(mask, v):
        return tuple(jnp.where(mask, part, 0.0) for part in v)

    own = [tuple(jnp.take_along_axis(part, half + (first + j), axis=1) for part in m[0]) for j in range(8)]
    steps = []
    for i in range(0, 8, 2):
        k = first + i
        c1, c2 = own[i], own[i + 1]
        a, b, c = row(c1, i), row(c2, i), row(c2, i + 1)
        dh, dl = cross(a, c, b, b)
        inv = 1.0 / dh
        p, e = two_prod(dh, inv)
        inv = (inv, inv * (((1.0 - p) - e) - dl * inv))
        later = rows > i + 1
        n1 = masked(later, mul_pair(*cross(c1, c, c2, b), *inv))
        n2 = masked(later, mul_pair(*cross(c2, a, c1, b), *inv))
        for j in range(i + 2, 8):
            own[j] = sub_pairs(*own[j], n1, row(own[j], i), n2, row(own[j], i + 1))
        r1, r2 = row(m[0], i), row(m[0], i + 1)
        w1 = mul_pair(*cross(r1, c, r2, b), *inv)
        w2 = mul_pair(*cross(r2, a, r1, b), *inv)
        here1, here2 = column == k, column == k + 1
        here = here1 | here2
        r1 = (jnp.where(here1, 1.0, jnp.where(here2, 0.0, r1[0])), jnp.where(here, 0.0, r1[1]))
        r2 = (jnp.where(here2, 1.0, jnp.where(here1, 0.0, r2[0])), jnp.where(here, 0.0, r2[1]))
        m[0] = sub_pairs(*masked(jnp.logical_not(here & later), m[0]), n1, r1, n2, r2)
        steps.append((here, w1, w2, r1, r2))
    for t in range(1, tiles):
        index = half + (rows + (first + 8 * t))

        def spread(v):
            return tuple(jnp.take_along_axis(part, index, axis=1) for part in v)

        for here, w1, w2, r1, r2 in steps:
            m[t] = sub_pairs(*masked(jnp.logical_not(here), m[t]), spread(w1), r1, spread(w2), r2)
    for t in range(tiles):
        mh[first + 8 * t : first + 8 * t + 8, :] = m[t][0]
        ml[first + 8 * t : first + 8 * t + 8, :] = m[t][1]


def factor_pair(mh, ml, begin, end):
    for first in range(begin, end, 8):
        factor_block(mh, ml, first)


def inverse_of(mh, ml):
    m = mh[...]
    rows = lax.broadcasted_iota(jnp.int32, (RANK, 128), 0)
    lanes = lax.broadcasted_iota(jnp.int32, (RANK, 128), 1)
    left = lanes < 64
    column = jnp.where(left, lanes, lanes - 64)
    odd = (rows & 1) == 1

    def pick(v, mask):
        v = jnp.where(mask, v, 0.0)
        a = jnp.sum(jnp.where(left, v, 0.0), axis=1, keepdims=True)
        b = jnp.sum(jnp.where(left, 0.0, v), axis=1, keepdims=True)
        return jnp.where(left, a, b)

    same, next_to = column == rows, column == (rows ^ 1)
    ch, cl = pick(m, same), pick(ml[...], same)
    bh, bl = pick(m, next_to), pick(ml[...], next_to)
    ah, al = pltpu.roll(ch, 1, 0), pltpu.roll(cl, 1, 0)
    inv = 1.0 / ah
    p, e = two_prod(ah, inv)
    rh, rl = mul_pair(bh, bl, inv, inv * (((1.0 - p) - e) - al * inv))
    p, e = mul_pair(rh, rl, bh, bl)
    ph, _ = add_pair(ch, cl, -p, -e)
    root = 1.0 / jnp.sqrt(jnp.where(odd, ph, ch))
    ratio = jnp.where(odd, rh, 0.0)
    unit = jnp.where(column < rows - (rows & 1), m, jnp.where(column == rows, 1.0, 0.0))
    return (unit - ratio * pltpu.roll(unit, 1, 0)) * root


def exchange_kernel(nx, nz, ny, weight, grad, mom, right, w_out, m_out, q_out, prod_out, scale_out, s_v, g_v, r_v, part,
                    mate, ysend, yrecv, pt, pw, gp, gx, gz, ga, mh, ml, linv, tp, xrecv, zsend, zrecv, tfull, sq, load_sem,
                    w_sem, mate_send, mate_recv, y_send, y_recv, ag_send, ag_recv, fw_send, fw_recv, h_send, h_recv,
                    gx_send, gx_recv, gz_send, gz_recv, ga_send, ga_recv, tx_send, tx_recv, tz_send, tz_recv, az_send,
                    az_recv, ax_send, ax_recv, l_send, l_recv, sq_send, sq_recv, near_sem, far_sem):
    nr, nc = nx * nz, ny * 2
    mats = nc + 1
    last = mats - 1
    ff = 256 * nc
    row, col = lax.axis_index("row"), lax.axis_index("col")
    x, z = row // nz, row % nz
    y, k = col // 2, col % 2
    mate_id = (row, y * 2 + (1 - k))
    half = RANK // 2

    pending = []

    def finish():
        for c in pending:
            c.wait_send()

    def send(src, dst, sems, index, target):
        c = pltpu.make_async_remote_copy(src_ref=src, dst_ref=dst, send_sem=sems[0].at[index], recv_sem=sems[1].at[index],
                                         device_id=target, device_id_type=MESH)
        c.start()
        pending.append(c)
        return c

    def x_peer(i):
        return lax.rem(x + i, nx)

    def z_peer(i):
        return lax.rem(z + i, nz)

    def y_peer(i):
        return lax.rem(y + i, ny)

    far_first = sorted(range(1, nz), key=lambda i: -min(i, nz - i))

    barrier = pltpu.get_barrier_semaphore()
    along_z = [(x * nz + z_peer(i), col) for i in (1, nz - 1)]
    along_x = [(x_peer(i) * nz + z, col) for i in (1, nx - 1)]
    two_off = [(x * nz + z_peer(i), col) for i in (2, nz - 2)]
    peers = along_z + along_x + [(row, lax.rem(col + i, nc)) for i in range(1, nc)]
    for peer in peers:
        pl.semaphore_signal(barrier, inc=1, device_id=peer, device_id_type=MESH)
    load_right = pltpu.make_async_copy(right, r_v, load_sem.at[2 * mats])
    load_right.start()

    def loads(m):
        return (pltpu.make_async_copy(mom.at[m], s_v.at[m], load_sem.at[m]),
                pltpu.make_async_copy(grad.at[m], g_v.at[m], load_sem.at[mats + m]))

    turns = list(range(1, ny)) + [0]
    for m in [2 * y_peer(i) + (1 - k) for i in turns] + [last] + [2 * y_peer(i) + k for i in turns]:
        for c in loads(m):
            c.start()

    load_right.wait()

    def power(m):
        for c in loads(m):
            c.wait()
        s = s_v[m] + g_v[m].astype(F32)
        s_v[m] = s
        part[m] = cut_product(nt, r_v[m], s)

    to_mate = {}
    mate_sems = (mate_send, mate_recv)
    for n, i in enumerate(turns):
        m = 2 * y_peer(i) + (1 - k)
        power(m)
    power(last)
    pl.semaphore_wait(barrier, len(peers))
    for i in turns:
        to_mate[i] = send(part.at[2 * y_peer(i) + (1 - k)], mate.at[i], mate_sems, i, mate_id)
    other_rows = pl.ds(pl.multiple_of((1 - k) * half, half), half)
    my_rows = pl.ds(pl.multiple_of(k * half, half), half)
    to_mate[ny] = send(part.at[last, other_rows], mate.at[ny, pl.ds(0, half)], mate_sems, ny, mate_id)
    for peer in along_z + along_x:
        pl.semaphore_signal(near_sem, inc=1, device_id=peer, device_id_type=MESH)
    load_weight = pltpu.make_async_copy(weight, w_out, w_sem)
    load_weight.start()

    own = 2 * y + k
    to_y = []
    for n, i in enumerate(turns):
        yd = y_peer(i)
        power(2 * yd + k)
        if n == 0:
            to_mate[ny].wait_recv()
            shared = part[last, my_rows, :] + mate[ny, 0:half, :]
        to_mate[i].wait_recv()
        if i == 0:
            yrecv[y, 0:RANK, :] = part[own] + mate[0]
            yrecv[y, RANK:, :] = shared
        else:
            ysend[i, 0:RANK, :] = part[2 * yd + k] + mate[i]
            ysend[i, RANK:, :] = shared
            to_y.append(send(ysend.at[i], yrecv.at[y], (y_send, y_recv), i, (row, 2 * yd + k)))
    pl.semaphore_wait(near_sem, len(along_z + along_x))
    for peer in two_off:
        pl.semaphore_signal(far_sem, inc=1, device_id=peer, device_id_type=MESH)
    for c in to_y:
        c.wait_recv()
    total = yrecv[0]
    for i in range(1, ny):
        total = total + yrecv[i]
    pt[last, my_rows, :] = total[RANK:]
    swap = send(pt.at[last, my_rows], pt.at[last, my_rows], (h_send, h_recv), 0, mate_id)
    pt[own] = total[0:RANK]
    gather = [send(pt.at[own], pt.at[own], (ag_send, ag_recv), i, (row, 2 * y_peer(i) + k)) for i in range(1, ny)]
    forward = {0: send(pt.at[own], pt.at[own], (fw_send, fw_recv), 0, mate_id)}

    lanes = lax.broadcasted_iota(jnp.int32, (RANK, 128), 1)
    ah, al = exact_gram(total[0:RANK])
    swap.wait_recv()
    bh, bl = exact_gram(pt[last])
    gp[0] = jnp.where(lanes < 64, ah, pltpu.roll(bh, 64, 1))
    gp[1] = jnp.where(lanes < 64, al, pltpu.roll(bl, 64, 1))
    share = RANK // nx

    def rows_of(d):
        return pl.ds(pl.multiple_of(d * share, share), share)

    to_x = [send(gp.at[:, rows_of(x_peer(i))], gx.at[x], (gx_send, gx_recv), i, (x_peer(i) * nz + z, col))
            for i in range(1, nx)]
    gx[x] = gp[:, rows_of(x), :]

    pl.semaphore_wait(far_sem, len(two_off))
    pairs = tp.shape[0]
    depth = tp.shape[2]
    t_x = {}

    def times(m, q, e):
        t = cut_product(nn, pt[m], s_v[m])
        at, to = (e, 0) if depth == RANK else (0, e * RANK)
        for h in range(2):
            tp[q, h * nx // 2 + at, pl.ds(to, RANK), :] = t[:, h * 128 : (h + 1) * 128]

    def block_out(turn, q):
        for i in range(1, nx):
            t_x[turn, i] = send(tp.at[q, x_peer(i)], xrecv.at[turn, i], (tx_send, tx_recv), (turn, i),
                                (x_peer(i) * nz + z, col))

    def times_pair(d):
        q = y_peer(d)
        times(2 * q + k, q, k)
        forward[d].wait_recv()
        times(2 * q + (1 - k), q, 1 - k)
        block_out(d, q)

    arrivals = sorted(range(1, ny), key=lambda d: min(d, ny - d))

    def pass_power(d):
        gather[ny - d - 1].wait_recv()
        m = 2 * y_peer(d) + k
        forward[d] = send(pt.at[m], pt.at[m], (fw_send, fw_recv), d, mate_id)

    at, to = RANK // depth, RANK % depth
    for h in range(2):
        tp[pairs - 1, h * nx // 2 + at, to : to + RANK, :] = jnp.zeros((RANK, 128), F32)
    times(last, pairs - 1, 0)
    block_out(ny, pairs - 1)
    times_pair(0)
    for d in arrivals:
        pass_power(d)
    times_pair(arrivals[0])

    def sum_pairs(ref, n):
        h, l = ref[0, 0], ref[0, 1]
        for i in range(1, n):
            h, l = add_pair(h, l, ref[i, 0], ref[i, 1])
        return h, l

    for c in to_x:
        c.wait_recv()
    h, l = sum_pairs(gx, nx)
    gz[z, 0] = h
    gz[z, 1] = l
    to_z = [send(gz.at[z], gz.at[z], (gz_send, gz_recv), i, (x * nz + z_peer(i), col)) for i in far_first]
    for d in arrivals[1:]:
        times_pair(d)
    turn_order = [ny, 0] + arrivals
    cut_at = (len(turn_order) + 1) // 2
    groups = [turn_order[:cut_at], turn_order[cut_at:]]

    def pair_of(d):
        return pairs - 1 if d == ny else y_peer(d)

    def sum_over_x(g):
        for n, d in enumerate(groups[g]):
            acc = tp[pair_of(d), x]
            for i in range(1, nx):
                t_x[d, i].wait_recv()
                acc = acc + xrecv[d, i]
            zsend[g][:, n] = acc.reshape(nz, *zsend[g].shape[2:])
        zrecv[g][0] = zsend[g][z]
        return [send(zsend[g].at[z_peer(j)], zrecv[g].at[j], (tz_send, tz_recv), (g, j), (x * nz + z_peer(j), col))
                for j in far_first]

    t_z = [sum_over_x(0)]
    t_z.append(sum_over_x(1))

    for c in to_z:
        c.wait_recv()
    h, l = sum_pairs(gz, nz)
    ga[x, 0] = h
    ga[x, 1] = l
    to_a = [send(ga.at[x], ga.at[x], (ga_send, ga_recv), i, (x_peer(i) * nz + z, col)) for i in range(1, nx)]

    for m in range(mats):
        pw[m] = six_right(jnp.transpose(pt[m]), 1)
    a_z, a_x = {}, ([], [])

    def pass_on(g, j):
        if j:
            a_z[g, j].wait_recv()
        p = tfull[g].at[x, z_peer(nz - j)] if j else tfull[g].at[x, z]
        for i in range(1, nx):
            a_x[g].append(send(p, p, (ax_send, ax_recv), (g, i, j), (x_peer(i) * nz + z, col)))

    for g in range(2):
        for c in t_z[g]:
            c.wait_recv()
        acc = zrecv[g][0]
        for j in range(1, nz):
            acc = acc + zrecv[g][j]
        tfull[g][x, z] = acc
        for j in far_first:
            a_z[g, j] = send(tfull[g].at[x, z], tfull[g].at[x, z], (az_send, az_recv), (g, j), (x * nz + z_peer(j), col))
        pass_on(g, 0)

    for c in to_a:
        c.wait_recv()
    for i in range(nx):
        mh[i * share : (i + 1) * share, :] = ga[i, 0]
        ml[i * share : (i + 1) * share, :] = ga[i, 1]
    near_first = far_first[::-1]
    near = near_first[:4]
    rest = near_first[4:]
    factor_pair(mh, ml, 0, 32)
    for j in near:
        pass_on(0, j)
    factor_pair(mh, ml, 32, 48)
    for j in rest:
        pass_on(0, j)
    factor_pair(mh, ml, 48, RANK)
    inverse = inverse_of(mh, ml)
    low = pltpu.roll(inverse[half:], 64, 1)
    first_lanes = lax.broadcasted_iota(jnp.int32, (half, 128), 1) < 64
    linv[own] = jnp.where(first_lanes, inverse[0:half], low)
    linv[last] = jnp.where(first_lanes, pltpu.roll(inverse[0:half], 64, 1), inverse[half:])
    spread = [send(linv.at[own], linv.at[own], (l_send, l_recv), i, (row, lax.rem(col + i, nc))) for i in range(1, nc)]
    for j in near_first:
        pass_on(1, j)
    for c in spread:
        c.wait_recv()
    inverses = {}
    for d in turn_order:
        for e in range(1 if d == ny else 2):
            packed = linv[2 * pair_of(d) + e]
            inverses[d, e] = six_left(jnp.concatenate([packed[:, 0:RANK], packed[:, RANK:]], axis=0))
    squares = jnp.zeros((16, 128), F32)
    places = lax.broadcasted_iota(jnp.int32, (16, 256), 0)
    for g in range(2):
        for c in a_x[g]:
            c.wait_recv()
        for n, d in enumerate(groups[g]):
            sqs = []
            for e in range(2):
                if (d, e) not in inverses:
                    sqs.append(jnp.zeros((RANK, 256), F32))
                    continue
                at, to = e * RANK // depth, e * RANK % depth
                t = jnp.concatenate([tfull[g][h * nx // 2 + at, :, n].reshape(depth, 128)[to : to + RANK]
                                     for h in range(2)], axis=1)
                p = nn(inverses[d, e], six_right(t, 0))
                prod_out[2 * pair_of(d) + e] = p
                sqs.append(p * p)
            ones = jnp.where(places == pair_of(d), 1.0, 0.0).astype(BF16)
            both = jnp.concatenate(sqs, axis=0)
            high = both.astype(BF16)
            squares = squares + nt(ones, high) + nt(ones, (both - high.astype(F32)).astype(BF16))
    sq[col] = squares[0:8]
    to_all = [send(sq.at[col], sq.at[col], (sq_send, sq_recv), i, (row, lax.rem(col + i, nc))) for i in range(1, nc)]
    left = lax.broadcasted_iota(jnp.int32, (pw.shape[1], 3 * RANK), 1) < 2 * RANK
    for d, e in inverses:
        m = 2 * pair_of(d) + e
        q = nt(pw[m], jnp.concatenate([inverses[d, e]] * 3, axis=0))
        q1 = q.astype(BF16)
        pieces = jnp.where(left, q1.astype(F32), q - q1.astype(F32)).astype(BF16)
        q_out[m] = pieces
        m_out[m] = s_v[m] - nn(pieces, stacked_pieces(prod_out[m] * (1.0 - DECAY)))
    for c in to_all:
        c.wait_recv()
    squares = sq[0]
    for i in range(1, nc):
        squares = squares + sq[i]
    scale_out[...] = jnp.transpose(1.0 / jnp.sqrt(squares * (1.0 / ff) + EPSILON))
    load_weight.wait()
    finish()


def stacked_pieces(p):
    p1 = p.astype(BF16)
    p2 = (p - p1.astype(F32)).astype(BF16)
    return jnp.concatenate([p1, p2, p1], axis=0)


def update_kernel(gain, w, mom, q, prod, scale, new_weight, new_mom, new_right, w_v, r_v, w_sem, m_sem, r_sem):
    mats = w.shape[0]
    move = pltpu.make_async_copy(mom, new_mom, m_sem)
    move.start()
    table = scale[...]
    moves = [move]
    for m in range(mats):
        column = table[(m % 2) * RANK : (m % 2 + 1) * RANK, m // 2 : m // 2 + 1]
        normed = prod[m] * column
        r_v[m] = normed
        c = pltpu.make_async_copy(r_v.at[m], new_right.at[m], r_sem.at[m])
        c.start()
        moves.append(c)
        w_v[m] = w[m] - nn(q[m], stacked_pieces(normed * gain))
        c = pltpu.make_async_copy(w_v.at[m], new_weight.at[m], w_sem.at[m])
        c.start()
        moves.append(c)
    for c in moves:
        c.wait()


def body(nx, nz, ny, depth, weight, grad, momentum, right):
    nr, nc = nx * nz, ny * 2
    mats, rows, cols = weight.shape
    ff = cols * nc
    rt = jnp.transpose(right, (1, 2, 0))
    pairs = (mats + 1) // 2
    sizes = ((pairs + 1) // 2, pairs // 2)
    block = 256 // nx
    tile = block // nz
    share = RANK // nx
    vmem = pl.BlockSpec(memory_space=pltpu.VMEM)
    hbm = pl.BlockSpec(memory_space=pltpu.HBM)
    dma = pltpu.SemaphoreType.DMA
    half = RANK // 2
    w, mom, q, prod, scale = pl.pallas_call(
        functools.partial(exchange_kernel, nx, nz, ny),
        out_shape=(
            jax.ShapeDtypeStruct((mats, rows, cols), F32),
            jax.ShapeDtypeStruct((mats, rows, cols), F32),
            jax.ShapeDtypeStruct((mats, rows, 3 * RANK), BF16),
            jax.ShapeDtypeStruct((mats, RANK, cols), F32),
            jax.ShapeDtypeStruct((128, 8), F32),
        ),
        in_specs=[hbm] * 4,
        out_specs=(vmem,) * 5,
        scratch_shapes=[
            pltpu.VMEM((mats, rows, cols), F32),
            pltpu.VMEM((mats, rows, cols), BF16),
            pltpu.VMEM((mats, RANK, cols), F32),
            pltpu.VMEM((mats, RANK, rows), F32),
            pltpu.VMEM((ny + 1, RANK, rows), F32),
            pltpu.VMEM((ny, RANK + half, rows), F32),
            pltpu.VMEM((ny, RANK + half, rows), F32),
            pltpu.VMEM((mats, RANK, rows), F32),
            pltpu.VMEM((mats, rows, 6 * RANK), BF16),
            pltpu.VMEM((2, RANK, 128), F32),
            pltpu.VMEM((nx, 2, share, 128), F32),
            pltpu.VMEM((nz, 2, share, 128), F32),
            pltpu.VMEM((nx, 2, share, 128), F32),
            pltpu.VMEM((RANK, 128), F32),
            pltpu.VMEM((RANK, 128), F32),
            pltpu.VMEM((mats, half, 128), F32),
            pltpu.VMEM((pairs, nx, block, 128), F32),
            pltpu.VMEM((pairs, nx, block, 128), F32),
            [pltpu.VMEM((nz, n, tile, 128), F32) for n in sizes],
            [pltpu.VMEM((nz, n, tile, 128), F32) for n in sizes],
            [pltpu.VMEM((nx, nz, n, tile, 128), F32) for n in sizes],
            pltpu.VMEM((nc, 8, 128), F32),
            dma((2 * mats + 1,)),
            dma,
            dma((ny + 1,)), dma((ny + 1,)),
            dma((ny,)), dma((ny,)),
            dma((ny,)), dma((ny,)),
            dma((ny,)), dma((ny,)),
            dma((1,)), dma((1,)),
            dma((nx,)), dma((nx,)),
            dma((nz,)), dma((nz,)),
            dma((nx,)), dma((nx,)),
            dma((pairs, nx)), dma((pairs, nx)),
            dma((2, nz)), dma((2, nz)),
            dma((2, nz)), dma((2, nz)),
            dma((2, nx, nz)), dma((2, nx, nz)),
            dma((nc,)), dma((nc,)),
            dma((nc,)), dma((nc,)),
            pltpu.SemaphoreType.REGULAR,
            pltpu.SemaphoreType.REGULAR,
        ],
        compiler_params=pltpu.CompilerParams(
            collective_id=0, has_side_effects=True, vmem_limit_bytes=40 * 1024 * 1024
        ),
        name="exchange",
    )(*[pltpu.with_memory_space_constraint(v, pltpu.HBM) for v in (weight, grad, momentum, rt)])

    gain = math.sqrt(depth / ff)
    new_weight, new_momentum, new_right = pl.pallas_call(
        functools.partial(update_kernel, gain),
        out_shape=(
            jax.ShapeDtypeStruct(weight.shape, F32),
            jax.ShapeDtypeStruct(weight.shape, F32),
            jax.ShapeDtypeStruct((mats, RANK, cols), F32),
        ),
        in_specs=[vmem] * 5,
        out_specs=(hbm,) * 3,
        scratch_shapes=[
            pltpu.VMEM((mats, rows, cols), F32),
            pltpu.VMEM((mats, RANK, cols), F32),
            dma((mats,)),
            dma,
            dma((mats,)),
        ],
        compiler_params=pltpu.CompilerParams(vmem_limit_bytes=12 * 1024 * 1024),
        name="update",
    )(w, mom, q, prod, scale)
    return new_weight, new_momentum, jnp.transpose(new_right, (2, 0, 1))


def solution(mesh):
    nr, nc = mesh.shape["row"], mesh.shape["col"]
    nz = min(nr, 8)
    nx = nr // nz

    def run(weight, grad, momentum, right):
        return body(nx, nz, nc // 2, weight.shape[1] * nr, weight, grad, momentum, right)

    placed = P(None, "row", "col")
    return jax.shard_map(
        run,
        mesh=mesh,
        in_specs=(placed, placed, placed, P("col", None, None)),
        out_specs=(placed, placed, P("col", None, None)),
        check_vma=False,
    )
```

```python
import functools
import math

import jax
import jax.numpy as jnp
from jax import lax
from jax.experimental import pallas as pl
from jax.experimental.pallas import tpu as pltpu
from jax.sharding import PartitionSpec as P

MESH = pl.DeviceIdType.MESH
F32 = jnp.float32
BF16 = jnp.bfloat16

EPSILON = 1e-06
DECAY = 0.95
RANK = 64


def two_sum(a, b):
    s = a + b
    back = s - a
    return s, (a - (s - back)) + (b - back)


def split(a):
    t = a * 4097.0
    high = t - (t - a)
    return high, a - high


def two_prod(a, b):
    p = a * b
    ah, al = split(a)
    bh, bl = split(b)
    return p, ((ah * bh - p) + ah * bl + al * bh) + al * bl


def add_pair(ah, al, bh, bl):
    s, t = two_sum(ah, bh)
    t = t + (al + bl)
    h = s + t
    return h, t - (h - s)


def nt(a, b, precision=None):
    return lax.dot_general(a, b, (((1,), (1,)), ((), ())), precision=precision, preferred_element_type=F32)


def nn(a, b, precision=None):
    return lax.dot_general(a, b, (((1,), (0,)), ((), ())), precision=precision, preferred_element_type=F32)


def tn(a, b, precision=None):
    return lax.dot_general(a, b, (((0,), (0,)), ((), ())), precision=precision, preferred_element_type=F32)


def cut(a):
    a1 = a.astype(BF16)
    rest = a - a1.astype(F32)
    a2 = rest.astype(BF16)
    return a1, a2, (rest - a2.astype(F32)).astype(BF16)


def cut_product(dot, a, b):
    a1, a2, a3 = cut(a)
    b1, b2, b3 = cut(b)
    p = dot(jnp.concatenate([a1, a2, a3], axis=0), b1)
    q = dot(jnp.concatenate([a1, a2], axis=0), b2)
    r = dot(a1, b3)
    return p[0:RANK] + ((p[RANK : 2 * RANK] + q[0:RANK]) + (p[2 * RANK :] + q[RANK:] + r))


def six_left(a):
    a1, a2, a3 = cut(a)
    return jnp.concatenate([a1, a2, a1, a3, a2, a1], axis=1)


def six_right(a, axis):
    a1, a2, a3 = cut(a)
    return jnp.concatenate([a1, a1, a2, a1, a2, a3], axis=axis)


def round_int(v):
    magic = 1.5 * 2.0**23
    return (v + magic) - magic


def exact_gram(x):
    top = jnp.maximum(jnp.max(jnp.abs(x), axis=1, keepdims=True), 1e-18)
    top = jnp.broadcast_to(top, (RANK, 128))
    power = jnp.floor(jnp.log(top) * (1.0 / math.log(2.0))) + 1.0
    unit = jnp.exp2(power - 7.0).astype(BF16).astype(F32)
    inverse = jnp.exp2(7.0 - power).astype(BF16).astype(F32)
    y = x * inverse[:, 0:1]
    slices = []
    for i in range(4):
        q = round_int(y)
        slices.append(q.astype(BF16))
        y = (y - q) * 256.0
    q = jnp.concatenate(slices, axis=0)
    e = nt(q, q)
    low = [e[RANK * a : RANK * (a + 1), 0:128] for a in range(4)]
    high = [e[RANK * a : RANK * (a + 1), 128:256] for a in range(4)]
    levels = [low[0], low[1], low[2] + high[0], low[3] + high[1], high[2], high[3]]
    s, t = levels[0], jnp.zeros_like(levels[0])
    for i in range(1, 6):
        s, err = two_sum(s, levels[i] * (2.0 ** (-8 * i)))
        t = t + err
    s2 = pltpu.roll(s, 64, 1) * (1.0 / 256.0)
    t2 = pltpu.roll(t, 64, 1) * (1.0 / 256.0)
    gh, gl = add_pair(s, t, s2, t2)
    rows = lax.broadcasted_iota(jnp.int32, (RANK, 128), 0)
    lanes = lax.broadcasted_iota(jnp.int32, (RANK, 128), 1)
    across = jnp.sum(jnp.where(rows == lanes, unit, 0.0), axis=0, keepdims=True)
    return gh * unit * across, gl * unit * across


def mul_pair(ah, al, bh, bl):
    p, e = two_prod(ah, bh)
    return p, e + (ah * bl + al * bh)


def sub_pairs(h, l, m1, r1, m2, r2):
    p, q = mul_pair(*m1, *r1)
    s, e = two_sum(h, -p)
    p2, q2 = mul_pair(*m2, *r2)
    s, e2 = two_sum(s, -p2)
    e = (e + e2) + (l - (q + q2))
    h = s + e
    return h, e - (h - s)


def cross(a, b, c, d):
    p1, e1 = mul_pair(*a, *b)
    p2, e2 = mul_pair(*c, *d)
    return add_pair(p1, e1, -p2, -e2)


def factor_block(mh, ml, first):
    tiles = (RANK - first) // 8
    rows = lax.broadcasted_iota(jnp.int32, (8, 128), 0)
    lanes = lax.broadcasted_iota(jnp.int32, (8, 128), 1)
    half = jnp.where(lanes >= 64, 64, 0)
    column = lanes - half
    m = [(mh[first + 8 * t : first + 8 * t + 8, :], ml[first + 8 * t : first + 8 * t + 8, :]) for t in range(tiles)]

    def row(v, i):
        return tuple(jnp.broadcast_to(part[i : i + 1], (8, 128)) for part in v)

    def masked(mask, v):
        return tuple(jnp.where(mask, part, 0.0) for part in v)

    own = [tuple(jnp.take_along_axis(part, half + (first + j), axis=1) for part in m[0]) for j in range(8)]
    steps = []
    for i in range(0, 8, 2):
        k = first + i
        c1, c2 = own[i], own[i + 1]
        a, b, c = row(c1, i), row(c2, i), row(c2, i + 1)
        dh, dl = cross(a, c, b, b)
        inv = 1.0 / dh
        p, e = two_prod(dh, inv)
        inv = (inv, inv * (((1.0 - p) - e) - dl * inv))
        later = rows > i + 1
        n1 = masked(later, mul_pair(*cross(c1, c, c2, b), *inv))
        n2 = masked(later, mul_pair(*cross(c2, a, c1, b), *inv))
        for j in range(i + 2, 8):
            own[j] = sub_pairs(*own[j], n1, row(own[j], i), n2, row(own[j], i + 1))
        r1, r2 = row(m[0], i), row(m[0], i + 1)
        w1 = mul_pair(*cross(r1, c, r2, b), *inv)
        w2 = mul_pair(*cross(r2, a, r1, b), *inv)
        here1, here2 = column == k, column == k + 1
        here = here1 | here2
        r1 = (jnp.where(here1, 1.0, jnp.where(here2, 0.0, r1[0])), jnp.where(here, 0.0, r1[1]))
        r2 = (jnp.where(here2, 1.0, jnp.where(here1, 0.0, r2[0])), jnp.where(here, 0.0, r2[1]))
        m[0] = sub_pairs(*masked(jnp.logical_not(here & later), m[0]), n1, r1, n2, r2)
        steps.append((here, w1, w2, r1, r2))
    for t in range(1, tiles):
        index = half + (rows + (first + 8 * t))

        def spread(v):
            return tuple(jnp.take_along_axis(part, index, axis=1) for part in v)

        for here, w1, w2, r1, r2 in steps:
            m[t] = sub_pairs(*masked(jnp.logical_not(here), m[t]), spread(w1), r1, spread(w2), r2)
    for t in range(tiles):
        mh[first + 8 * t : first + 8 * t + 8, :] = m[t][0]
        ml[first + 8 * t : first + 8 * t + 8, :] = m[t][1]


def factor_pair(mh, ml, begin, end):
    for first in range(begin, end, 8):
        factor_block(mh, ml, first)


def inverse_of(mh, ml):
    m = mh[...]
    rows = lax.broadcasted_iota(jnp.int32, (RANK, 128), 0)
    lanes = lax.broadcasted_iota(jnp.int32, (RANK, 128), 1)
    left = lanes < 64
    column = jnp.where(left, lanes, lanes - 64)
    odd = (rows & 1) == 1

    def pick(v, mask):
        v = jnp.where(mask, v, 0.0)
        a = jnp.sum(jnp.where(left, v, 0.0), axis=1, keepdims=True)
        b = jnp.sum(jnp.where(left, 0.0, v), axis=1, keepdims=True)
        return jnp.where(left, a, b)

    same, next_to = column == rows, column == (rows ^ 1)
    ch, cl = pick(m, same), pick(ml[...], same)
    bh, bl = pick(m, next_to), pick(ml[...], next_to)
    ah, al = pltpu.roll(ch, 1, 0), pltpu.roll(cl, 1, 0)
    inv = 1.0 / ah
    p, e = two_prod(ah, inv)
    rh, rl = mul_pair(bh, bl, inv, inv * (((1.0 - p) - e) - al * inv))
    p, e = mul_pair(rh, rl, bh, bl)
    ph, _ = add_pair(ch, cl, -p, -e)
    root = 1.0 / jnp.sqrt(jnp.where(odd, ph, ch))
    ratio = jnp.where(odd, rh, 0.0)
    unit = jnp.where(column < rows - (rows & 1), m, jnp.where(column == rows, 1.0, 0.0))
    return (unit - ratio * pltpu.roll(unit, 1, 0)) * root


def exchange_kernel(nx, nz, ny, weight, grad, mom, right, w_out, m_out, q_out, prod_out, scale_out, s_v, g_v, r_v, part,
                    mate, ysend, yrecv, pt, pw, gp, gx, gz, ga, mh, ml, linv, tp, xrecv, zsend, zrecv, tfull, sq, load_sem,
                    w_sem, mate_send, mate_recv, y_send, y_recv, ag_send, ag_recv, fw_send, fw_recv, h_send, h_recv,
                    gx_send, gx_recv, gz_send, gz_recv, ga_send, ga_recv, tx_send, tx_recv, tz_send, tz_recv, az_send,
                    az_recv, ax_send, ax_recv, l_send, l_recv, sq_send, sq_recv, near_sem, far_sem):
    nr, nc = nx * nz, ny * 2
    mats = nc + 1
    last = mats - 1
    ff = 256 * nc
    row, col = lax.axis_index("row"), lax.axis_index("col")
    x, z = row // nz, row % nz
    y, k = col // 2, col % 2
    mate_id = (row, y * 2 + (1 - k))
    half = RANK // 2

    pending = []

    def finish():
        for c in pending:
            c.wait_send()

    def send(src, dst, sems, index, target):
        c = pltpu.make_async_remote_copy(src_ref=src, dst_ref=dst, send_sem=sems[0].at[index], recv_sem=sems[1].at[index],
                                         device_id=target, device_id_type=MESH)
        c.start()
        pending.append(c)
        return c

    def x_peer(i):
        return lax.rem(x + i, nx)

    def z_peer(i):
        return lax.rem(z + i, nz)

    def y_peer(i):
        return lax.rem(y + i, ny)

    far_first = sorted(range(1, nz), key=lambda i: -min(i, nz - i))

    barrier = pltpu.get_barrier_semaphore()
    along_z = [(x * nz + z_peer(i), col) for i in (1, nz - 1)]
    along_x = [(x_peer(i) * nz + z, col) for i in (1, nx - 1)]
    two_off = [(x * nz + z_peer(i), col) for i in (2, nz - 2)]
    peers = along_z + along_x + [(row, lax.rem(col + i, nc)) for i in range(1, nc)]
    for peer in peers:
        pl.semaphore_signal(barrier, inc=1, device_id=peer, device_id_type=MESH)
    load_right = pltpu.make_async_copy(right, r_v, load_sem.at[2 * mats])
    load_right.start()

    def loads(m):
        return (pltpu.make_async_copy(mom.at[m], s_v.at[m], load_sem.at[m]),
                pltpu.make_async_copy(grad.at[m], g_v.at[m], load_sem.at[mats + m]))

    turns = list(range(1, ny)) + [0]
    for m in [2 * y_peer(i) + (1 - k) for i in turns] + [last] + [2 * y_peer(i) + k for i in turns]:
        for c in loads(m):
            c.start()

    load_right.wait()

    def power(m):
        for c in loads(m):
            c.wait()
        s = s_v[m] + g_v[m].astype(F32)
        s_v[m] = s
        part[m] = cut_product(nt, r_v[m], s)

    to_mate = {}
    mate_sems = (mate_send, mate_recv)
    for n, i in enumerate(turns):
        m = 2 * y_peer(i) + (1 - k)
        power(m)
    power(last)
    pl.semaphore_wait(barrier, len(peers))
    for i in turns:
        to_mate[i] = send(part.at[2 * y_peer(i) + (1 - k)], mate.at[i], mate_sems, i, mate_id)
    other_rows = pl.ds(pl.multiple_of((1 - k) * half, half), half)
    my_rows = pl.ds(pl.multiple_of(k * half, half), half)
    to_mate[ny] = send(part.at[last, other_rows], mate.at[ny, pl.ds(0, half)], mate_sems, ny, mate_id)
    for peer in along_z + along_x:
        pl.semaphore_signal(near_sem, inc=1, device_id=peer, device_id_type=MESH)
    load_weight = pltpu.make_async_copy(weight, w_out, w_sem)
    load_weight.start()

    own = 2 * y + k
    to_y = []
    for n, i in enumerate(turns):
        yd = y_peer(i)
        power(2 * yd + k)
        if n == 0:
            to_mate[ny].wait_recv()
            shared = part[last, my_rows, :] + mate[ny, 0:half, :]
        to_mate[i].wait_recv()
        if i == 0:
            yrecv[y, 0:RANK, :] = part[own] + mate[0]
            yrecv[y, RANK:, :] = shared
        else:
            ysend[i, 0:RANK, :] = part[2 * yd + k] + mate[i]
            ysend[i, RANK:, :] = shared
            to_y.append(send(ysend.at[i], yrecv.at[y], (y_send, y_recv), i, (row, 2 * yd + k)))
    pl.semaphore_wait(near_sem, len(along_z + along_x))
    for peer in two_off:
        pl.semaphore_signal(far_sem, inc=1, device_id=peer, device_id_type=MESH)
    for c in to_y:
        c.wait_recv()
    total = yrecv[0]
    for i in range(1, ny):
        total = total + yrecv[i]
    pt[last, my_rows, :] = total[RANK:]
    swap = send(pt.at[last, my_rows], pt.at[last, my_rows], (h_send, h_recv), 0, mate_id)
    pt[own] = total[0:RANK]
    gather = [send(pt.at[own], pt.at[own], (ag_send, ag_recv), i, (row, 2 * y_peer(i) + k)) for i in range(1, ny)]
    forward = {0: send(pt.at[own], pt.at[own], (fw_send, fw_recv), 0, mate_id)}

    lanes = lax.broadcasted_iota(jnp.int32, (RANK, 128), 1)
    ah, al = exact_gram(total[0:RANK])
    swap.wait_recv()
    bh, bl = exact_gram(pt[last])
    gp[0] = jnp.where(lanes < 64, ah, pltpu.roll(bh, 64, 1))
    gp[1] = jnp.where(lanes < 64, al, pltpu.roll(bl, 64, 1))
    share = RANK // nx

    def rows_of(d):
        return pl.ds(pl.multiple_of(d * share, share), share)

    to_x = [send(gp.at[:, rows_of(x_peer(i))], gx.at[x], (gx_send, gx_recv), i, (x_peer(i) * nz + z, col))
            for i in range(1, nx)]
    gx[x] = gp[:, rows_of(x), :]

    pl.semaphore_wait(far_sem, len(two_off))
    pairs = tp.shape[0]
    depth = tp.shape[2]
    t_x = {}

    def times(m, q, e):
        t = cut_product(nn, pt[m], s_v[m])
        at, to = (e, 0) if depth == RANK else (0, e * RANK)
        for h in range(2):
            tp[q, h * nx // 2 + at, pl.ds(to, RANK), :] = t[:, h * 128 : (h + 1) * 128]

    def block_out(turn, q):
        for i in range(1, nx):
            t_x[turn, i] = send(tp.at[q, x_peer(i)], xrecv.at[turn, i], (tx_send, tx_recv), (turn, i),
                                (x_peer(i) * nz + z, col))

    def times_pair(d):
        q = y_peer(d)
        times(2 * q + k, q, k)
        forward[d].wait_recv()
        times(2 * q + (1 - k), q, 1 - k)
        block_out(d, q)

    arrivals = sorted(range(1, ny), key=lambda d: min(d, ny - d))

    def pass_power(d):
        gather[ny - d - 1].wait_recv()
        m = 2 * y_peer(d) + k
        forward[d] = send(pt.at[m], pt.at[m], (fw_send, fw_recv), d, mate_id)

    at, to = RANK // depth, RANK % depth
    for h in range(2):
        tp[pairs - 1, h * nx // 2 + at, to : to + RANK, :] = jnp.zeros((RANK, 128), F32)
    times(last, pairs - 1, 0)
    block_out(ny, pairs - 1)
    times_pair(0)
    for d in arrivals:
        pass_power(d)
    times_pair(arrivals[0])

    def sum_pairs(ref, n):
        h, l = ref[0, 0], ref[0, 1]
        for i in range(1, n):
            h, l = add_pair(h, l, ref[i, 0], ref[i, 1])
        return h, l

    for c in to_x:
        c.wait_recv()
    h, l = sum_pairs(gx, nx)
    gz[z, 0] = h
    gz[z, 1] = l
    to_z = [send(gz.at[z], gz.at[z], (gz_send, gz_recv), i, (x * nz + z_peer(i), col)) for i in far_first]
    for d in arrivals[1:]:
        times_pair(d)
    turn_order = [ny, 0] + arrivals
    cut_at = (len(turn_order) + 1) // 2
    groups = [turn_order[:cut_at], turn_order[cut_at:]]

    def pair_of(d):
        return pairs - 1 if d == ny else y_peer(d)

    def sum_over_x(g):
        for n, d in enumerate(groups[g]):
            acc = tp[pair_of(d), x]
            for i in range(1, nx):
                t_x[d, i].wait_recv()
                acc = acc + xrecv[d, i]
            zsend[g][:, n] = acc.reshape(nz, *zsend[g].shape[2:])
        zrecv[g][0] = zsend[g][z]
        return [send(zsend[g].at[z_peer(j)], zrecv[g].at[j], (tz_send, tz_recv), (g, j), (x * nz + z_peer(j), col))
                for j in far_first]

    t_z = [sum_over_x(0)]
    for m in range(mats):
        pw[m] = six_right(jnp.transpose(pt[m]), 1)
    t_z.append(sum_over_x(1))

    for c in to_z:
        c.wait_recv()
    h, l = sum_pairs(gz, nz)
    ga[x, 0] = h
    ga[x, 1] = l
    to_a = [send(ga.at[x], ga.at[x], (ga_send, ga_recv), i, (x_peer(i) * nz + z, col)) for i in range(1, nx)]

    a_z, a_x = {}, ([], [])

    def pass_on(g, j):
        if j:
            a_z[g, j].wait_recv()
        p = tfull[g].at[x, z_peer(nz - j)] if j else tfull[g].at[x, z]
        for i in range(1, nx):
            a_x[g].append(send(p, p, (ax_send, ax_recv), (g, i, j), (x_peer(i) * nz + z, col)))

    for g in range(2):
        for c in t_z[g]:
            c.wait_recv()
        acc = zrecv[g][0]
        for j in range(1, nz):
            acc = acc + zrecv[g][j]
        tfull[g][x, z] = acc
        for j in far_first:
            a_z[g, j] = send(tfull[g].at[x, z], tfull[g].at[x, z], (az_send, az_recv), (g, j), (x * nz + z_peer(j), col))
        pass_on(g, 0)

    for c in to_a:
        c.wait_recv()
    for i in range(nx):
        mh[i * share : (i + 1) * share, :] = ga[i, 0]
        ml[i * share : (i + 1) * share, :] = ga[i, 1]
    near_first = far_first[::-1]
    near = near_first[:4]
    rest = near_first[4:]
    factor_pair(mh, ml, 0, 32)
    for j in near:
        pass_on(0, j)
    factor_pair(mh, ml, 32, 48)
    for j in rest:
        pass_on(0, j)
    factor_pair(mh, ml, 48, RANK)
    inverse = inverse_of(mh, ml)
    low = pltpu.roll(inverse[half:], 64, 1)
    first_lanes = lax.broadcasted_iota(jnp.int32, (half, 128), 1) < 64
    linv[own] = jnp.where(first_lanes, inverse[0:half], low)
    linv[last] = jnp.where(first_lanes, pltpu.roll(inverse[0:half], 64, 1), inverse[half:])
    spread = [send(linv.at[own], linv.at[own], (l_send, l_recv), i, (row, lax.rem(col + i, nc))) for i in range(1, nc)]
    for j in near_first:
        pass_on(1, j)
    for c in spread:
        c.wait_recv()
    inverses = {}
    for d in turn_order:
        for e in range(1 if d == ny else 2):
            packed = linv[2 * pair_of(d) + e]
            inverses[d, e] = six_left(jnp.concatenate([packed[:, 0:RANK], packed[:, RANK:]], axis=0))
    squares = jnp.zeros((16, 128), F32)
    places = lax.broadcasted_iota(jnp.int32, (16, 256), 0)
    for g in range(2):
        for c in a_x[g]:
            c.wait_recv()
        for n, d in enumerate(groups[g]):
            sqs = []
            for e in range(2):
                if (d, e) not in inverses:
                    sqs.append(jnp.zeros((RANK, 256), F32))
                    continue
                at, to = e * RANK // depth, e * RANK % depth
                t = jnp.concatenate([tfull[g][h * nx // 2 + at, :, n].reshape(depth, 128)[to : to + RANK]
                                     for h in range(2)], axis=1)
                p = nn(inverses[d, e], six_right(t, 0))
                prod_out[2 * pair_of(d) + e] = p
                sqs.append(p * p)
            ones = jnp.where(places == pair_of(d), 1.0, 0.0).astype(BF16)
            both = jnp.concatenate(sqs, axis=0)
            high = both.astype(BF16)
            squares = squares + nt(ones, high) + nt(ones, (both - high.astype(F32)).astype(BF16))
    sq[col] = squares[0:8]
    to_all = [send(sq.at[col], sq.at[col], (sq_send, sq_recv), i, (row, lax.rem(col + i, nc))) for i in range(1, nc)]
    left = lax.broadcasted_iota(jnp.int32, (pw.shape[1], 3 * RANK), 1) < 2 * RANK
    for d, e in inverses:
        m = 2 * pair_of(d) + e
        q = nt(pw[m], jnp.concatenate([inverses[d, e]] * 3, axis=0))
        q1 = q.astype(BF16)
        pieces = jnp.where(left, q1.astype(F32), q - q1.astype(F32)).astype(BF16)
        q_out[m] = pieces
        m_out[m] = s_v[m] - nn(pieces, stacked_pieces(prod_out[m] * (1.0 - DECAY)))
    for c in to_all:
        c.wait_recv()
    squares = sq[0]
    for i in range(1, nc):
        squares = squares + sq[i]
    scale_out[...] = jnp.transpose(1.0 / jnp.sqrt(squares * (1.0 / ff) + EPSILON))
    load_weight.wait()
    finish()


def stacked_pieces(p):
    p1 = p.astype(BF16)
    p2 = (p - p1.astype(F32)).astype(BF16)
    return jnp.concatenate([p1, p2, p1], axis=0)


def update_kernel(gain, w, mom, q, prod, scale, new_weight, new_mom, new_right, w_v, r_v, w_sem, m_sem, r_sem):
    mats = w.shape[0]
    move = pltpu.make_async_copy(mom, new_mom, m_sem)
    move.start()
    table = scale[...]
    moves = [move]
    for m in range(mats):
        column = table[(m % 2) * RANK : (m % 2 + 1) * RANK, m // 2 : m // 2 + 1]
        normed = prod[m] * column
        r_v[m] = normed
        c = pltpu.make_async_copy(r_v.at[m], new_right.at[m], r_sem.at[m])
        c.start()
        moves.append(c)
        w_v[m] = w[m] - nn(q[m], stacked_pieces(normed * gain))
        c = pltpu.make_async_copy(w_v.at[m], new_weight.at[m], w_sem.at[m])
        c.start()
        moves.append(c)
    for c in moves:
        c.wait()


def body(nx, nz, ny, depth, weight, grad, momentum, right):
    nr, nc = nx * nz, ny * 2
    mats, rows, cols = weight.shape
    ff = cols * nc
    rt = jnp.transpose(right, (1, 2, 0))
    pairs = (mats + 1) // 2
    sizes = ((pairs + 1) // 2, pairs // 2)
    block = 256 // nx
    tile = block // nz
    share = RANK // nx
    vmem = pl.BlockSpec(memory_space=pltpu.VMEM)
    hbm = pl.BlockSpec(memory_space=pltpu.HBM)
    dma = pltpu.SemaphoreType.DMA
    half = RANK // 2
    w, mom, q, prod, scale = pl.pallas_call(
        functools.partial(exchange_kernel, nx, nz, ny),
        out_shape=(
            jax.ShapeDtypeStruct((mats, rows, cols), F32),
            jax.ShapeDtypeStruct((mats, rows, cols), F32),
            jax.ShapeDtypeStruct((mats, rows, 3 * RANK), BF16),
            jax.ShapeDtypeStruct((mats, RANK, cols), F32),
            jax.ShapeDtypeStruct((128, 8), F32),
        ),
        in_specs=[hbm] * 4,
        out_specs=(vmem,) * 5,
        scratch_shapes=[
            pltpu.VMEM((mats, rows, cols), F32),
            pltpu.VMEM((mats, rows, cols), BF16),
            pltpu.VMEM((mats, RANK, cols), F32),
            pltpu.VMEM((mats, RANK, rows), F32),
            pltpu.VMEM((ny + 1, RANK, rows), F32),
            pltpu.VMEM((ny, RANK + half, rows), F32),
            pltpu.VMEM((ny, RANK + half, rows), F32),
            pltpu.VMEM((mats, RANK, rows), F32),
            pltpu.VMEM((mats, rows, 6 * RANK), BF16),
            pltpu.VMEM((2, RANK, 128), F32),
            pltpu.VMEM((nx, 2, share, 128), F32),
            pltpu.VMEM((nz, 2, share, 128), F32),
            pltpu.VMEM((nx, 2, share, 128), F32),
            pltpu.VMEM((RANK, 128), F32),
            pltpu.VMEM((RANK, 128), F32),
            pltpu.VMEM((mats, half, 128), F32),
            pltpu.VMEM((pairs, nx, block, 128), F32),
            pltpu.VMEM((pairs, nx, block, 128), F32),
            [pltpu.VMEM((nz, n, tile, 128), F32) for n in sizes],
            [pltpu.VMEM((nz, n, tile, 128), F32) for n in sizes],
            [pltpu.VMEM((nx, nz, n, tile, 128), F32) for n in sizes],
            pltpu.VMEM((nc, 8, 128), F32),
            dma((2 * mats + 1,)),
            dma,
            dma((ny + 1,)), dma((ny + 1,)),
            dma((ny,)), dma((ny,)),
            dma((ny,)), dma((ny,)),
            dma((ny,)), dma((ny,)),
            dma((1,)), dma((1,)),
            dma((nx,)), dma((nx,)),
            dma((nz,)), dma((nz,)),
            dma((nx,)), dma((nx,)),
            dma((pairs, nx)), dma((pairs, nx)),
            dma((2, nz)), dma((2, nz)),
            dma((2, nz)), dma((2, nz)),
            dma((2, nx, nz)), dma((2, nx, nz)),
            dma((nc,)), dma((nc,)),
            dma((nc,)), dma((nc,)),
            pltpu.SemaphoreType.REGULAR,
            pltpu.SemaphoreType.REGULAR,
        ],
        compiler_params=pltpu.CompilerParams(
            collective_id=0, has_side_effects=True, vmem_limit_bytes=40 * 1024 * 1024
        ),
        name="exchange",
    )(*[pltpu.with_memory_space_constraint(v, pltpu.HBM) for v in (weight, grad, momentum, rt)])

    gain = math.sqrt(depth / ff)
    new_weight, new_momentum, new_right = pl.pallas_call(
        functools.partial(update_kernel, gain),
        out_shape=(
            jax.ShapeDtypeStruct(weight.shape, F32),
            jax.ShapeDtypeStruct(weight.shape, F32),
            jax.ShapeDtypeStruct((mats, RANK, cols), F32),
        ),
        in_specs=[vmem] * 5,
        out_specs=(hbm,) * 3,
        scratch_shapes=[
            pltpu.VMEM((mats, rows, cols), F32),
            pltpu.VMEM((mats, RANK, cols), F32),
            dma((mats,)),
            dma,
            dma((mats,)),
        ],
        compiler_params=pltpu.CompilerParams(vmem_limit_bytes=12 * 1024 * 1024),
        name="update",
    )(w, mom, q, prod, scale)
    return new_weight, new_momentum, jnp.transpose(new_right, (2, 0, 1))


def solution(mesh):
    nr, nc = mesh.shape["row"], mesh.shape["col"]
    nz = min(nr, 8)
    nx = nr // nz

    def run(weight, grad, momentum, right):
        return body(nx, nz, nc // 2, weight.shape[1] * nr, weight, grad, momentum, right)

    placed = P(None, "row", "col")
    return jax.shard_map(
        run,
        mesh=mesh,
        in_specs=(placed, placed, placed, P("col", None, None)),
        out_specs=(placed, placed, P("col", None, None)),
        check_vma=False,
    )
```
